32 devices in a mesh: seq: 8 (over y, x, core), tp: 4 (over z).
Axes of the slice: x: 2, y: 2, z: 4, core: 2. Of those that a mesh axis runs over, the one named last changes fastest.
Arguments:
- byte_ids: int32 [1024, 8], P('seq'), may hold values from 0 to 255
- global_out: bfloat16 [1024, 8192], P('seq', 'tp'), may hold values from -6 to 6
- global_in_grad: bfloat16 [1024, 8192], P('seq', 'tp'), may hold values from -6 to 6
- out_grad: bfloat16 [8192, 1024], P(('seq', 'tp')), may hold values from -6 to 6
- proj_weight: bfloat16 [1024, 1024], replicated, may hold values from -0.1875 to 0.1875
- emb_local: bfloat16 [256, 1024], replicated, may hold values from -6 to 6
- norm_gain: float32 [1024], replicated, may hold values from 0.1 to 1.9
- up_weight: bfloat16 [1024, 2048], replicated, may hold values from -0.1875 to 0.1875
- down_weight: bfloat16 [2048, 1024], replicated, may hold values from -0.125 to 0.125
Outputs:
- glob_out_grad: bfloat16 [1024, 8192], P('seq', 'tp')
- emb_global_grad: float32 [256, 1024], replicated
- emb_local_grad: float32 [256, 1024], replicated
- gain_grad: float32 [1024], replicated
- proj_grad: float32 [1024, 1024], P(None, ('seq', 'tp'))
- up_grad: float32 [1024, 2048], P(None, ('seq', 'tp'))
- down_grad: float32 [2048, 1024], P(('seq', 'tp'))
The draws below stay inside these ranges and needn't reach their ends.
All inputs are finite; a program needn't handle non-finite values.
Results may differ from the reference program's by a relative error of at most 0.015.
Values may be sent and summed in bfloat16 or wider, within the bound.
No kernel may reach another device: no remote copies, remote signals or barrier semaphores. Data moves between devices by JAX's collectives and lax.ppermute only.
A program may use at most 128 MiB of HBM per device.

```python
import jax
import jax.numpy as jnp
from jax import lax

PATCH = 8
SLOT = 1024
DL = 1024
FF = 2048
VOCAB = 256
GW = 8192
PATCHES = 1024
BYTES = 8192


def with_ends(values, stream_key, smallest, largest):
    shape = values.shape
    index_at = [jax.random.randint(jax.random.fold_in(stream_key, axis), (), 0, shape[axis]) for axis in range(len(shape))]
    values = values.at[tuple(index_at)].set(smallest)
    longest = shape.index(max(shape))
    index_at[longest] = (index_at[longest] + 1) % shape[longest]
    return values.at[tuple(index_at)].set(largest)


def level_of(key, dims, split, low, top_value):
    def one(dim, shards_of):
        draws = jax.random.uniform(jax.random.fold_in(jax.random.fold_in(key, 6), dim), (shards_of,), jnp.float32, low / len(split), top_value / len(split))
        return jnp.repeat(jnp.exp(draws), dims[dim] // shards_of).reshape((-1,) + (1,) * (len(dims) - dim - 1))

    factor_of = one(*split[0])
    for cut in split[1:]:
        factor_of = factor_of * one(*cut)
    return factor_of


def scatter_about(own_key, extent, deviation, limit, split=(), kind=jnp.bfloat16):
    loudness = level_of(own_key, extent, split, -0.22, 0.18) if split else 1.0
    result = jax.random.normal(own_key, extent, jnp.float32) * deviation * loudness
    return jnp.minimum(jnp.maximum(result, -limit), limit).astype(kind)


def setup_inputs(seed: int = 0) -> dict:
    splits = jax.random.split(jax.random.key(seed), 10)
    byte_ids = with_ends(jax.random.randint(splits[0], (PATCHES, PATCH), 0, 256), jax.random.fold_in(splits[0], 1), 0, 255).astype(jnp.int32)
    global_out = scatter_about(splits[1], (PATCHES, GW), 1.0, 6.0, ((0, 8), (1, 4)))
    global_in_grad = scatter_about(splits[2], (PATCHES, GW), 1.0, 6.0, ((0, 8), (1, 4)))
    out_grad = scatter_about(splits[3], (BYTES, DL), 1.0, 6.0, ((0, 32),))
    proj_weight = scatter_about(splits[4], (SLOT, DL), SLOT ** -0.5, 0.1875)
    emb_local = scatter_about(splits[5], (VOCAB, DL), 1.0, 6.0)
    norm_gain = jnp.clip(1.0 + 0.18 * jax.random.normal(splits[6], (DL,), jnp.float32), 0.1, 1.9)
    up_weight = scatter_about(splits[7], (DL, FF), DL ** -0.5, 0.1875)
    down_weight = scatter_about(splits[8], (FF, DL), FF ** -0.5, 0.125)
    return {"byte_ids": byte_ids, "global_out": global_out, "global_in_grad": global_in_grad, "out_grad": out_grad, "proj_weight": proj_weight, "emb_local": emb_local, "norm_gain": norm_gain, "up_weight": up_weight, "down_weight": down_weight}


def inner(left, right):
    return lax.dot_general(left, right, (((0,), (0,)), ((), ())), preferred_element_type=jnp.float32)

def outer(left, right):
    return lax.dot_general(left, right, (((1,), (1,)), ((), ())), preferred_element_type=jnp.float32)

def reference(byte_ids, global_out, global_in_grad, out_grad, proj_weight, emb_local, norm_gain, up_weight, down_weight):
    slot_in = global_out.reshape(BYTES, SLOT)
    first = jnp.full((PATCHES, 1), -1, jnp.int32)
    prev_id = jnp.concatenate([first, byte_ids[:, :-1]], axis=1).reshape(BYTES)
    prev_hot = jax.nn.one_hot(prev_id, VOCAB, dtype=jnp.bfloat16)
    u_rows = jnp.dot(slot_in, proj_weight, preferred_element_type=jnp.float32) + jnp.dot(prev_hot, emb_local, preferred_element_type=jnp.float32)
    scale = lax.rsqrt(lax.optimization_barrier(jnp.mean(u_rows * u_rows, axis=1, keepdims=True)) + 1e-05)
    normed = u_rows * scale
    r_rows = (normed * norm_gain).astype(jnp.bfloat16)
    a_rows = jnp.dot(r_rows, up_weight, preferred_element_type=jnp.float32)
    sig = jax.nn.sigmoid(a_rows)
    h_rows = (a_rows * sig).astype(jnp.bfloat16)
    dh_rows = outer(out_grad, down_weight)
    da_rows = (dh_rows * sig * (1.0 + a_rows * (1.0 - sig))).astype(jnp.bfloat16)
    down_grad = inner(h_rows, out_grad)
    up_grad = inner(r_rows, da_rows)
    dr_rows = outer(da_rows, up_weight)
    gain_grad = lax.optimization_barrier(jnp.sum(dr_rows * normed, axis=0))
    dn_rows = dr_rows * norm_gain
    du_rows = (out_grad.astype(jnp.float32) + scale * (dn_rows - normed * lax.optimization_barrier(jnp.mean(dn_rows * normed, axis=1, keepdims=True)))).astype(jnp.bfloat16)
    proj_grad = inner(slot_in, du_rows)
    emb_local_grad = inner(prev_hot, du_rows)
    glob_out_grad = outer(du_rows, proj_weight).astype(jnp.bfloat16).reshape(PATCHES, GW)
    own_hot = jax.nn.one_hot(byte_ids.reshape(BYTES), VOCAB, dtype=jnp.bfloat16)
    emb_global_grad = inner(own_hot, global_in_grad.reshape(BYTES, SLOT))
    return (glob_out_grad, emb_global_grad, emb_local_grad, gain_grad, proj_grad, up_grad, down_grad)
```

```python
import jax
import jax.numpy as jnp
from jax import lax
from jax.sharding import PartitionSpec as P

BF = jnp.bfloat16
F32 = jnp.float32


def inner(left, right):
    return lax.dot_general(
        left, right, (((0,), (0,)), ((), ())), preferred_element_type=F32
    )


def outer(left, right):
    return lax.dot_general(
        left, right, (((1,), (1,)), ((), ())), preferred_element_type=F32
    )


def swap(value, axis, mask):
    count = lax.axis_size(axis)
    return lax.ppermute(value, axis, [(i, i ^ mask) for i in range(count)])


def pick(value, index, axis):
    return lax.dynamic_index_in_dim(value, index, axis, keepdims=False)


def on_device(
    byte_ids,
    global_out,
    global_in_grad,
    out_grad,
    proj_weight,
    emb_local,
    norm_gain,
    up_weight,
    down_weight,
):
    seq_count = lax.axis_size("seq")
    tp_count = lax.axis_size("tp")
    seq_place = lax.axis_index("seq")
    tp_place = lax.axis_index("tp")
    bits = seq_count.bit_length() - 1
    patches, patch = byte_ids.shape
    slot, width = proj_weight.shape
    vocab = emb_local.shape[0]
    own = patch // tp_count
    part = patches // tp_count
    rows = own * patches

    def bit_of(bit):
        return (seq_place >> bit) & 1

    grad_by_slot = jnp.swapaxes(out_grad.reshape(part, patch, width), 0, 1).reshape(
        tp_count, own, part, width
    )
    out_rows = jnp.zeros((own, tp_count, part, width), BF)
    for mask in range(tp_count):
        block = pick(grad_by_slot, tp_place ^ mask, 0)
        if mask:
            block = swap(block, "tp", mask)
        out_rows = lax.dynamic_update_slice(
            out_rows, block[:, None], (0, tp_place ^ mask, 0, 0)
        )
    out_rows = out_rows.reshape(rows, width)

    def by_slot(value):
        return jnp.concatenate(
            [value[:, j * slot : (j + 1) * slot] for j in range(own)], axis=0
        )

    ids = byte_ids.T
    before = jnp.concatenate([jnp.full((1, patches), -1, jnp.int32), ids[:-1]], axis=0)
    own_ids = lax.dynamic_slice_in_dim(ids, tp_place * own, own, 0).reshape(rows)
    prev_id = lax.dynamic_slice_in_dim(before, tp_place * own, own, 0).reshape(rows)
    own_hot = jax.nn.one_hot(own_ids, vocab, dtype=BF)
    prev_hot = jax.nn.one_hot(prev_id, vocab, dtype=BF)

    def scatter(value, order):
        left = list(range(bits - 1, -1, -1))
        for bit in order:
            axis = left.index(bit)
            here = bit_of(bit)
            arrived = swap(pick(value, 1 - here, axis).astype(BF), "seq", 1 << bit)
            value = pick(value, here, axis).astype(F32) + arrived.astype(F32)
            left.remove(bit)
        return value

    def tree(parts):
        while len(parts) > 1:
            parts = [parts[i] + parts[i + 1] for i in range(0, len(parts), 2)]
        return parts[0]

    def table_sum(table, order, extra=None):
        height = vocab // seq_count
        block = table.reshape([2] * bits + [height, width])
        if extra is not None:
            extra = extra.reshape([2] * bits + [1, width // seq_count])
            pad = [(0, 0)] * bits + [(0, 15), (0, width - width // seq_count)]
            block = jnp.concatenate([block, jnp.pad(extra, pad)], axis=bits)
        sent = scatter(block, order).astype(BF)
        parts = [swap(sent, "tp", mask) if mask else sent for mask in range(tp_count)]
        whole = tree([value.astype(F32) for value in parts]).astype(BF)
        have = []
        for bit in reversed(order):
            arrived = swap(whole, "seq", 1 << bit)
            have.append(bit)
            axis = sorted(have, reverse=True).index(bit)
            both = jnp.stack([whole, arrived], axis=axis)
            turned = jnp.stack([arrived, whole], axis=axis)
            whole = jnp.where(bit_of(bit) == 0, both, turned)
        whole = whole.reshape(seq_count, -1, width).astype(F32)
        summed = whole[:, :height].reshape(vocab, width)
        if extra is None:
            return summed
        return summed, whole[:, height, : width // seq_count].reshape(width)

    up_order = list(range(bits))
    down_order = [0] + list(range(bits - 1, 0, -1))
    emb_global_part = inner(own_hot, by_slot(global_in_grad))
    emb_global_grad = table_sum(emb_global_part, up_order)

    slot_in = by_slot(global_out)
    u_rows = jnp.dot(slot_in, proj_weight, preferred_element_type=F32) + jnp.dot(
        prev_hot, emb_local, preferred_element_type=F32
    )
    scale = lax.rsqrt(jnp.mean(u_rows * u_rows, axis=1, keepdims=True) + 1e-05)
    normed = u_rows * scale
    r_rows = (normed * norm_gain).astype(BF)
    a_rows = jnp.dot(r_rows, up_weight, preferred_element_type=F32)
    sig = jax.nn.sigmoid(a_rows)
    h_rows = (a_rows * sig).astype(BF)

    def weight_sum(left, right):
        share = left.shape[1] // (seq_count * tp_count)
        cut = left.reshape(rows, seq_count // 2, 2, tp_count * share)

        def product(side):
            chosen = pick(cut, side, 2).reshape(rows, -1)
            return inner(chosen, right)

        core = bit_of(0)
        arrived = swap(product(1 - core).astype(BF), "seq", 1)
        half = product(core) + arrived.astype(F32)
        half = half.reshape([2] * (bits - 1) + [tp_count, share, right.shape[1]])
        columns = right.shape[1] // 2
        sums = []
        for order, first in ((up_order[1:], 0), (down_order[1:], columns)):
            value = half[..., first : first + columns]
            left_bits = list(range(bits - 1, 0, -1))
            for bit in order:
                axis = left_bits.index(bit)
                here = bit_of(bit)
                arrived = swap(pick(value, 1 - here, axis).astype(BF), "seq", 1 << bit)
                value = pick(value, here, axis) + arrived.astype(F32)
                left_bits.remove(bit)
            total = pick(value, tp_place, 0)
            for mask in range(1, tp_count):
                block = pick(value, tp_place ^ mask, 0).astype(BF)
                total = total + swap(block, "tp", mask).astype(F32)
            sums.append(total)
        return jnp.concatenate(sums, axis=1)

    down_grad = weight_sum(h_rows, out_rows)
    dh_rows = outer(out_rows, down_weight)
    da_rows = (dh_rows * sig * (1.0 + a_rows * (1.0 - sig))).astype(BF)
    up_grad = weight_sum(da_rows, r_rows).T
    dr_rows = outer(da_rows, up_weight)
    gain_part = jnp.sum(dr_rows * normed, axis=0)
    dn_rows = dr_rows * norm_gain
    du_rows = (
        out_rows.astype(F32)
        + scale * (dn_rows - normed * jnp.mean(dn_rows * normed, axis=1, keepdims=True))
    ).astype(BF)
    proj_grad = weight_sum(du_rows, slot_in).T
    emb_local_part = inner(prev_hot, du_rows)
    emb_local_grad, gain_grad = table_sum(emb_local_part, down_order, gain_part)
    back = outer(du_rows, proj_weight).astype(BF)
    glob_out_grad = jnp.concatenate(
        [back[j * patches : (j + 1) * patches] for j in range(own)], axis=1
    )
    return (
        glob_out_grad,
        emb_global_grad,
        emb_local_grad,
        gain_grad,
        proj_grad,
        up_grad,
        down_grad,
    )


def solution(mesh):
    placed = (
        P("seq", None),
        P("seq", "tp"),
        P("seq", "tp"),
        P(("seq", "tp"), None),
        P(),
        P(),
        P(),
        P(),
        P(),
    )
    return jax.shard_map(
        on_device,
        mesh=mesh,
        in_specs=placed,
        out_specs=(
            P("seq", "tp"),
            P(),
            P(),
            P(),
            P(None, ("seq", "tp")),
            P(None, ("seq", "tp")),
            P(("seq", "tp"), None),
        ),
        check_vma=False,
    )
```

```python
import jax
import jax.numpy as jnp
from jax import lax
from jax.sharding import PartitionSpec as P

BF = jnp.bfloat16
F32 = jnp.float32


def inner(left, right):
    return lax.dot_general(
        left, right, (((0,), (0,)), ((), ())), preferred_element_type=F32
    )


def outer(left, right):
    return lax.dot_general(
        left, right, (((1,), (1,)), ((), ())), preferred_element_type=F32
    )


def times(left, right):
    return jnp.dot(left, right, preferred_element_type=F32)


def swap(value, axis, masks):
    count = lax.axis_size(axis)
    pairs = [(i, i ^ masks[i % len(masks)]) for i in range(count)]
    return lax.ppermute(value, axis, pairs)


def block_at(value, index, size, axis):
    return lax.dynamic_slice_in_dim(value, index * size, size, axis)


def tree(parts):
    while len(parts) > 1:
        parts = [parts[i] + parts[i + 1] for i in range(0, len(parts), 2)]
    return parts[0]


def on_device(
    byte_ids,
    global_out,
    global_in_grad,
    out_grad,
    proj_weight,
    emb_local,
    norm_gain,
    up_weight,
    down_weight,
):
    seq_count = lax.axis_size("seq")
    tp_count = lax.axis_size("tp")
    seq_place = lax.axis_index("seq")
    tp_place = lax.axis_index("tp")
    core = seq_place & 1
    chip = seq_place >> 1
    stages = seq_count.bit_length() - 2
    walks = (list(range(1, stages + 1)), list(range(stages, 0, -1)))
    patches, patch = byte_ids.shape
    slot, width = proj_weight.shape
    hidden = up_weight.shape[1]
    vocab = emb_local.shape[0]
    own = patch // tp_count
    part = patches // tp_count
    rows = own * patches

    def share_mask(number, walk):
        mask = 0
        for k in range(stages):
            if (number >> (stages - 1 - k)) & 1:
                mask |= 1 << (walk[k] - 1)
        return mask

    shares = [
        2 * (chip ^ jnp.where(core == 0, share_mask(n, walks[0]), share_mask(n, walks[1]))) + core
        for n in range(1 << stages)
    ]

    def stage_swap(value, k):
        return swap(value, "seq", (1 << walks[0][k], 1 << walks[1][k]))

    def core_swap(value):
        return swap(value, "seq", (1,))

    grad_by_slot = jnp.swapaxes(out_grad.reshape(part, patch, width), 0, 1).reshape(
        tp_count * own * part, width
    )
    out_own = jnp.zeros((own, tp_count, part, width), BF)
    for mask in range(tp_count):
        block = block_at(grad_by_slot, tp_place ^ mask, own * part, 0)
        if mask:
            block = swap(block, "tp", (mask,))
        out_own = lax.dynamic_update_slice(
            out_own, block.reshape(own, 1, part, width), (0, tp_place ^ mask, 0, 0)
        )
    out_own = out_own.reshape(rows, width)
    out_rows = jnp.concatenate([out_own, core_swap(out_own)], axis=0)

    def by_slot(value):
        other = core_swap(value)
        return jnp.concatenate(
            [part[:, j * slot : (j + 1) * slot] for part in (value, other) for j in range(own)],
            axis=0,
        )

    ids = byte_ids.T
    ids = jnp.concatenate([ids, core_swap(ids)], axis=1)
    before = jnp.concatenate([jnp.full((1, 2 * patches), -1, jnp.int32), ids[:-1]], axis=0)

    def of_rows(value):
        mine = lax.dynamic_slice_in_dim(value, tp_place * own, own, 0)
        return jnp.swapaxes(mine.reshape(own, 2, patches), 0, 1).reshape(2 * rows)

    own_ids = of_rows(ids)
    prev_ids = of_rows(before)
    prev_hot = (prev_ids[:, None] == jnp.arange(vocab)[None, :]).astype(BF)

    height = vocab // seq_count
    here = jnp.concatenate([share * height + jnp.arange(height) for share in shares])
    own_hot = (here[:, None] == own_ids[None, :]).astype(BF)
    prev_hot_here = (here[:, None] == prev_ids[None, :]).astype(BF)
    emb_global_part = times(own_hot, by_slot(global_in_grad))

    chunk = hidden // seq_count
    up_here = jnp.concatenate([block_at(up_weight, s, chunk, 1) for s in shares], axis=1)
    down_here = jnp.concatenate([block_at(down_weight, s, chunk, 0) for s in shares], axis=0)

    slot_in = by_slot(global_out)
    u_rows = times(slot_in, proj_weight) + times(prev_hot, emb_local)
    scale = lax.rsqrt(jnp.mean(u_rows * u_rows, axis=1, keepdims=True) + 1e-05)
    normed = u_rows * scale
    r_rows = (normed * norm_gain).astype(BF)
    a_rows = times(r_rows, up_here)
    sig = jax.nn.sigmoid(a_rows)
    h_rows = (a_rows * sig).astype(BF)

    def halving(keep, sent):
        for k in range(stages):
            value = keep + stage_swap(sent, k).astype(F32)
            size = value.shape[0] // 2
            if k + 1 < stages:
                keep, sent = value[:size], value[size:].astype(BF)
        return value

    def weight_sum(left, right):
        size = left.shape[1] // 2
        sent = inner(left[:, size:], right).astype(BF)
        keep = inner(left[:, :size], right)
        value = halving(keep, sent)
        size = value.shape[0] // tp_count
        parts = []
        for mask in range(tp_count):
            block = block_at(value, tp_place ^ mask, size, 0)
            if mask:
                block = swap(block.astype(BF), "tp", (mask,)).astype(F32)
            parts.append(block)
        return tree(parts)

    down_grad = weight_sum(h_rows, out_rows)
    dh_rows = outer(out_rows, down_here)
    da_rows = (dh_rows * sig * (1.0 + a_rows * (1.0 - sig))).astype(BF)
    up_grad = weight_sum(da_rows, r_rows).T
    dr_part = outer(da_rows, up_here)
    dr_sent = jnp.concatenate([dr_part[rows:], dr_part[:rows]], axis=0).astype(BF)
    dr_rows = dr_part + core_swap(dr_sent).astype(F32)
    gain_part = jnp.sum(dr_rows * normed, axis=0)
    dn_rows = dr_rows * norm_gain
    du_rows = (
        out_rows.astype(F32)
        + scale * (dn_rows - normed * jnp.mean(dn_rows * normed, axis=1, keepdims=True))
    ).astype(BF)

    emb_local_part = times(prev_hot_here, du_rows)
    strip = width // seq_count
    pieces = []
    for n, share in enumerate(shares):
        pieces.append(emb_global_part[n * height : (n + 1) * height])
        pieces.append(emb_local_part[n * height : (n + 1) * height])
        line = block_at(gain_part, share, strip, 0)[None]
        pieces.append(jnp.pad(line, ((0, 15), (0, width - strip))))
    tables = jnp.concatenate(pieces, axis=0)
    size = tables.shape[0] // 2
    value = halving(tables[:size], tables[size:].astype(BF)).astype(BF)
    parts = [swap(value, "tp", (mask,)) if mask else value for mask in range(tp_count)]
    value = tree([p.astype(F32) for p in parts]).astype(BF)
    for k in range(stages - 1, -1, -1):
        value = jnp.concatenate([value, stage_swap(value, k)], axis=0)
    both = jnp.stack([value, core_swap(value)]).reshape(2 << stages, -1, width)
    numbers = []
    for side in range(2):
        turn = core ^ side
        for n in range(1 << stages):
            mask = jnp.where(turn == 0, share_mask(n, walks[0]), share_mask(n, walks[1]))
            numbers.append(2 * (chip ^ mask) + turn)
    numbers = jnp.stack(numbers)
    where_from = (numbers[:, None] * height + jnp.arange(height)[None, :]).reshape(-1)
    sort = (jnp.arange(vocab)[:, None] == where_from[None, :]).astype(BF)
    emb_global_grad = times(sort, both[:, :height].reshape(vocab, width))
    emb_local_grad = times(sort, both[:, height : 2 * height].reshape(vocab, width))
    gain_sort = (jnp.arange(seq_count)[:, None] == numbers[None, :]).astype(BF)
    gain_grad = times(gain_sort, both[:, 2 * height, :strip]).reshape(width)

    columns = width // seq_count
    du_here = jnp.concatenate([block_at(du_rows, s, columns, 1) for s in shares], axis=1)
    proj_grad = weight_sum(du_here, slot_in).T
    back = outer(du_rows[:rows], proj_weight).astype(BF)
    glob_out_grad = jnp.concatenate(
        [back[j * patches : (j + 1) * patches] for j in range(own)], axis=1
    )
    return (
        glob_out_grad,
        emb_global_grad,
        emb_local_grad,
        gain_grad,
        proj_grad,
        up_grad,
        down_grad,
    )


def solution(mesh):
    placed = (
        P("seq", None),
        P("seq", "tp"),
        P("seq", "tp"),
        P(("seq", "tp"), None),
        P(),
        P(),
        P(),
        P(),
        P(),
    )
    return jax.shard_map(
        on_device,
        mesh=mesh,
        in_specs=placed,
        out_specs=(
            P("seq", "tp"),
            P(),
            P(),
            P(),
            P(None, ("seq", "tp")),
            P(None, ("seq", "tp")),
            P(("seq", "tp"), None),
        ),
        check_vma=False,
    )
```

```python
import functools

import jax
import jax.numpy as jnp
from jax import lax
from jax.experimental import pallas as pl
from jax.experimental.pallas import tpu as pltpu
from jax.sharding import PartitionSpec as P

BF = jnp.bfloat16
F32 = jnp.float32
ROOM = 32 * 1024 * 1024


def inner(left, right):
    return lax.dot_general(
        left, right, (((0,), (0,)), ((), ())), preferred_element_type=F32
    )


def outer(left, right):
    return lax.dot_general(
        left, right, (((1,), (1,)), ((), ())), preferred_element_type=F32
    )


def times(left, right):
    return jnp.dot(left, right, preferred_element_type=F32)


def swap(value, axis, masks):
    count = lax.axis_size(axis)
    pairs = [(i, i ^ masks[i % len(masks)]) for i in range(count)]
    return lax.ppermute(value, axis, pairs)


def block_at(value, index, size, axis):
    return lax.dynamic_slice_in_dim(value, index * size, size, axis)


def like(rows, columns, kind):
    return jax.ShapeDtypeStruct((rows, columns), kind)


def run(body, outs, ins, after=(), numbers=None, scratch=(), flops=0):
    scalars = [] if numbers is None else [numbers]
    count, late = len(scalars) + len(ins), len(after)

    def kernel(*refs):
        body(*refs[:count], *refs[count + late :])

    moved = sum(a.size * a.dtype.itemsize for a in ins)
    return pl.pallas_call(
        kernel,
        out_shape=tuple(outs),
        in_specs=[pl.BlockSpec(memory_space=pltpu.SMEM)] * len(scalars)
        + [pl.BlockSpec(memory_space=pltpu.VMEM)] * len(ins)
        + [pl.BlockSpec(memory_space=pl.ANY)] * late,
        out_specs=tuple(pl.BlockSpec(memory_space=pltpu.VMEM) for _ in outs),
        scratch_shapes=list(scratch),
        compiler_params=pltpu.CompilerParams(vmem_limit_bytes=ROOM),
        cost_estimate=pl.CostEstimate(flops=flops, bytes_accessed=moved, transcendentals=0),
    )(*scalars, *ins, *after)


def sort_body(patch, part, own, numbers, grad, *blocks):
    size = own * part
    row = lax.broadcasted_iota(jnp.int32, (size, grad.shape[0]), 0)
    source = lax.broadcasted_iota(jnp.int32, (size, grad.shape[0]), 1)
    for m, block in enumerate(blocks):
        wanted = (row % part) * patch + numbers[m] * own + row // part
        block[...] = times((source == wanted).astype(BF), grad[...]).astype(BF)


def join_body(part, own, count, numbers, *refs):
    blocks, whole = refs[:-1], refs[-1]
    for m, block in enumerate(blocks):
        for j in range(own):
            start = pl.multiple_of((j * count + numbers[m]) * part, part)
            whole[pl.ds(start, part), :] = block[j * part : (j + 1) * part, :]


def product_body(shares, width, unit, places, moving, halves, numbers, *refs):
    left, rights = refs[0], refs[1 : 1 + halves]
    total = refs[-1]
    outs = refs[1 + halves : -1]
    kept, sent = outs[0], outs[1]
    count = len(places) // shares
    half = len(places) // 2
    if len(outs) == 3:
        first = 0
        for right in rights:
            outs[2][first : first + right.shape[0], :] = right[...]
            first += right.shape[0]
    for n in range(shares):
        if moving:
            start = pl.multiple_of(numbers[count + n] * width, width)
        else:
            start = n * width
        first = 0
        value = None
        for right in rights:
            rows = right.shape[0]
            term = inner(left[first : first + rows, pl.ds(start, width)], right[...])
            value = term if value is None else value + term
            first += rows
        total[...] = value
        for m in range(count):
            place = places[n * count + m]
            target = kept if place < half else sent
            row = (place % half) * unit
            block = total[pl.ds(pl.multiple_of(numbers[m] * unit, unit), unit), :]
            target[row : row + unit, :] = block.astype(target.dtype)


def add_body(kept, arrived, keep, send):
    half = keep.shape[0]
    keep[...] = (kept[:half, :].astype(F32) + arrived[:half, :].astype(F32)).astype(keep.dtype)
    send[...] = (kept[half:, :].astype(F32) + arrived[half:, :].astype(F32)).astype(send.dtype)


def sum_body(kept, arrived, whole):
    whole[...] = (kept[...].astype(F32) + arrived[...].astype(F32)).astype(whole.dtype)


def turned_body(kept, arrived, whole):
    whole[...] = (kept[...].astype(F32) + arrived[...].astype(F32)).T


def stack_body(first, second, both):
    rows = first.shape[0]
    both[:rows, :] = first[...]
    both[rows:, :] = second[...]


def on_device(
    byte_ids,
    global_out,
    global_in_grad,
    out_grad,
    proj_weight,
    emb_local,
    norm_gain,
    up_weight,
    down_weight,
):
    seq_count = lax.axis_size("seq")
    tp_count = lax.axis_size("tp")
    seq_place = lax.axis_index("seq")
    tp_place = lax.axis_index("tp")
    core = seq_place & 1
    chip = seq_place >> 1
    stages = seq_count.bit_length() - 2
    levels = tp_count.bit_length() - 1
    share_count = 1 << stages
    walks = (list(range(1, stages + 1)), list(range(stages, 0, -1)))
    patches, patch = byte_ids.shape
    slot, width = proj_weight.shape
    hidden = up_weight.shape[1]
    vocab = emb_local.shape[0]
    own = patch // tp_count
    part = patches // tp_count
    rows = own * patches

    def share_mask(number, walk):
        mask = 0
        for k in range(stages):
            if (number >> (stages - 1 - k)) & 1:
                mask |= 1 << (walk[k] - 1)
        return mask

    def shares_of(which):
        return [
            2 * (chip ^ jnp.where(which == 0, share_mask(n, walks[0]), share_mask(n, walks[1])))
            + which
            for n in range(share_count)
        ]

    shares = shares_of(core)
    others = shares_of(1 - core)
    near = [tp_place ^ m for m in range(tp_count)]
    numbers = jnp.stack(near + shares).astype(jnp.int32)

    def core_swap(value):
        return swap(value, "seq", (1,))

    def go(value, step):
        kind, k = step
        if kind == "seq":
            return swap(value, "seq", (1 << walks[0][k], 1 << walks[1][k]))
        return swap(value, "tp", (1 << k,))

    blocks = run(
        functools.partial(sort_body, patch, part, own),
        [like(own * part, width, BF)] * tp_count,
        [out_grad],
        numbers=numbers,
    )
    blocks = [swap(b, "tp", (m,)) if m else b for m, b in enumerate(blocks)]

    def by_slot(value):
        return [value[:, j * slot : (j + 1) * slot] for j in range(own)]

    slot_in = jnp.concatenate(by_slot(global_out) + by_slot(core_swap(global_out)), axis=0)
    ids = byte_ids.T
    ids = jnp.concatenate([ids, core_swap(ids)], axis=1)
    before = jnp.concatenate([jnp.full((1, 2 * patches), -1, jnp.int32), ids[:-1]], axis=0)

    def of_rows(value):
        mine = lax.dynamic_slice_in_dim(value, tp_place * own, own, 0)
        return jnp.swapaxes(mine.reshape(own, 2, patches), 0, 1).reshape(2 * rows)

    own_ids = of_rows(ids)[:rows]
    prev_ids = of_rows(before)
    prev_hot = (prev_ids[:, None] == jnp.arange(vocab)[None, :]).astype(BF)

    chunk = hidden // seq_count
    up_here = jnp.concatenate([block_at(up_weight, s, chunk, 1) for s in shares], axis=1)
    down_here = jnp.concatenate([block_at(down_weight, s, chunk, 0) for s in shares], axis=0)

    u_rows = times(slot_in, proj_weight) + times(prev_hot, emb_local)
    scale = lax.rsqrt(jnp.mean(u_rows * u_rows, axis=1, keepdims=True) + 1e-05)
    normed = u_rows * scale
    r_rows = (normed * norm_gain).astype(BF)
    a_rows = times(r_rows, up_here)
    sig = jax.nn.sigmoid(a_rows)
    h_rows = (a_rows * sig).astype(BF)

    height = vocab // seq_count

    def vocab_of(numbers):
        return jnp.concatenate([n * height + jnp.arange(height) for n in numbers])

    here, there = vocab_of(shares), vocab_of(others)
    gin = jnp.concatenate(by_slot(global_in_grad), axis=0)
    glob_sent = times((there[:, None] == own_ids[None, :]).astype(BF), gin).astype(BF)
    glob_kept = times((here[:, None] == own_ids[None, :]).astype(BF), gin)

    seq_steps = [("seq", k) for k in range(stages)]
    tp_steps = [("tp", k) for k in range(levels)]

    def add(kept, arrived, after):
        half = kept.shape[0] // 2
        kind = arrived.dtype
        outs = [like(half, kept.shape[1], kind)] * 2
        return run(add_body, outs, [kept, arrived], after)

    class Chain:
        def __init__(self, kept, sent, steps, turned):
            self.kept, self.steps, self.turned, self.at = kept, steps, turned, 0
            self.arrived = go(sent, steps[0])

        def next(self, after):
            self.at += 1
            if self.at < len(self.steps):
                self.kept, sent = add(self.kept, self.arrived, after)
                self.arrived = go(sent, self.steps[self.at])
                return self.kept
            if self.turned:
                shape = like(self.kept.shape[1], self.kept.shape[0], F32)
                (self.kept,) = run(turned_body, [shape], [self.kept, self.arrived], after)
            else:
                shape = like(self.kept.shape[0], self.kept.shape[1], F32)
                (self.kept,) = run(sum_body, [shape], [self.kept, self.arrived], after)
            return self.kept

    class Table:
        def __init__(self, kept, arrived):
            self.kept, self.arrived, self.at = kept, arrived, 0
            self.plan = (
                [("half", s) for s in seq_steps[1:]]
                + [("whole", s) for s in tp_steps]
                + [("join", s) for s in reversed(seq_steps)]
                + [("join", None)]
            )
            self.last = "half"

        def next(self, after):
            kind, step = self.plan[self.at] if self.at < len(self.plan) else ("end", None)
            rows, columns = self.kept.shape
            if self.last == "half" and kind == "half":
                self.kept, sent = add(self.kept, self.arrived, after)
            elif self.last == "join":
                shape = like(2 * rows, columns, BF)
                (self.kept,) = run(stack_body, [shape], [self.kept, self.arrived], after)
                sent = self.kept
            else:
                shape = like(rows, columns, BF)
                (self.kept,) = run(sum_body, [shape], [self.kept, self.arrived], after)
                sent = self.kept
            if kind != "end":
                self.arrived = core_swap(sent) if step is None else go(sent, step)
                self.last = kind
                self.at += 1
            return self.kept

    def product(left, rights, steps, moving, copied, after):
        share = left.shape[1] // share_count
        if moving:
            share = left.shape[1] // seq_count
            if share % 128:
                left = jnp.concatenate([block_at(left, s, share, 1) for s in shares], axis=1)
                moving = False
        unit = share // tp_count
        kind = BF if unit % 16 == 0 else F32
        places = []
        for n in range(share_count):
            for m in range(tp_count):
                place = 0
                for axis, k in steps:
                    digit = (n >> (stages - 1 - k)) & 1 if axis == "seq" else (m >> k) & 1
                    place = 2 * place + digit
                places.append(place)
        columns = rights[0].shape[1]
        height = share * share_count // 2
        outs = [like(height, columns, kind)] * 2
        if copied:
            outs.append(like(left.shape[0], columns, BF))
        body = functools.partial(
            product_body, share_count, share, unit, places, moving, len(rights)
        )
        return run(
            body,
            outs,
            [left, *rights],
            after,
            numbers=numbers,
            scratch=[pltpu.VMEM((share, columns), F32)],
            flops=4 * height * columns * left.shape[0],
        )

    glob_arrived = core_swap(glob_sent)
    half = glob_kept.shape[0] // 2
    glob_kept, glob_sent = add(glob_kept, glob_arrived, [h_rows])
    glob = Table(glob_kept, go(glob_sent, seq_steps[0]))
    (out_own,) = run(
        functools.partial(join_body, part, own, tp_count),
        [like(rows, width, BF)],
        blocks,
        [glob_kept, h_rows],
        numbers=numbers,
    )
    out_other = core_swap(out_own)
    last = glob.next([out_own])

    order = seq_steps + tp_steps
    kept, sent, out_rows = product(h_rows, [out_own, out_other], order, False, True, [last])
    down = Chain(kept, sent, order, False)
    dh_rows = outer(out_rows, down_here)
    da_rows = (dh_rows * sig * (1.0 + a_rows * (1.0 - sig))).astype(BF)
    dr_part = outer(da_rows, up_here)
    dr_sent = jnp.concatenate([dr_part[rows:], dr_part[:rows]], axis=0).astype(BF)
    dr_arrived = core_swap(dr_sent)
    last = glob.next([dr_sent])
    (dr_arrived,) = run(
        lambda a, b: b.__setitem__(Ellipsis, a[...]),
        [like(2 * rows, width, BF)],
        [dr_arrived],
        [last],
    )
    dr_rows = dr_part + dr_arrived.astype(F32)
    gain_part = jnp.sum(dr_rows * normed, axis=0)
    dn_rows = dr_rows * norm_gain
    du_rows = (
        out_rows.astype(F32)
        + scale * (dn_rows - normed * jnp.mean(dn_rows * normed, axis=1, keepdims=True))
    ).astype(BF)

    strip = width // seq_count
    emb_part = times((here[:, None] == prev_ids[None, :]).astype(BF), du_rows)
    lines = jnp.stack([block_at(gain_part, s, strip, 0) for s in shares])[:, None]
    lines = jnp.pad(lines, ((0, 0), (0, height - 1), (0, 0))).reshape(-1, strip)
    tables = jnp.concatenate([emb_part, lines], axis=1).astype(BF)
    half = tables.shape[0] // 2
    local_kept, local_sent = tables[:half], tables[half:]
    local = Table(local_kept, go(local_sent, seq_steps[0]))

    order = tp_steps[:1] + seq_steps + tp_steps[1:]
    kept, sent = product(du_rows, [slot_in], order, True, False, [local_sent])
    proj = Chain(kept, sent, order, True)
    order = seq_steps + tp_steps
    kept, sent = product(da_rows, [r_rows], order, False, False, [kept])
    up = Chain(kept, sent, order, True)
    back = outer(du_rows[:rows], proj_weight).astype(BF)
    glob_out_grad = jnp.concatenate(
        [back[j * patches : (j + 1) * patches] for j in range(own)], axis=1
    )

    last = kept
    seen = {down: 0, proj: 0, up: 0, local: 0, glob: 2}
    ends = {
        down: len(order),
        proj: len(order),
        up: len(order),
        local: len(local.plan) + 1,
        glob: len(glob.plan) + 1,
    }
    queue = [
        local, down, local, glob, proj, local, glob, down, local, up, proj, local,
        glob, down, proj, local, up, glob, local, down, proj, up, glob, up,
    ]
    for chain in queue + [local, proj, down, glob, up] * 16:
        if seen[chain] < ends[chain]:
            last = chain.next([last])
            seen[chain] += 1

    all_numbers = jnp.stack(shares + others)
    sort = jnp.arange(vocab)[:, None] == (
        all_numbers[:, None] * height + jnp.arange(height)[None, :]
    ).reshape(1, -1)
    sort = sort.astype(BF)
    emb_global_grad = times(sort, glob.kept)
    emb_local_grad = times(sort, local.kept[:, :width])
    gain_sort = (jnp.arange(seq_count)[:, None] == all_numbers[None, :]).astype(BF)
    gain_lines = local.kept[:, width:].reshape(seq_count, height, strip)[:, 0]
    gain_grad = times(gain_sort, gain_lines).reshape(width)
    return (
        glob_out_grad,
        emb_global_grad,
        emb_local_grad,
        gain_grad,
        proj.kept,
        up.kept,
        down.kept,
    )


def solution(mesh):
    placed = (
        P("seq", None),
        P("seq", "tp"),
        P("seq", "tp"),
        P(("seq", "tp"), None),
        P(),
        P(),
        P(),
        P(),
        P(),
    )
    return jax.shard_map(
        on_device,
        mesh=mesh,
        in_specs=placed,
        out_specs=(
            P("seq", "tp"),
            P(),
            P(),
            P(),
            P(None, ("seq", "tp")),
            P(None, ("seq", "tp")),
            P(("seq", "tp"), None),
        ),
        check_vma=False,
    )
```

```python
import functools

import jax
import jax.numpy as jnp
from jax import lax
from jax.experimental import pallas as pl
from jax.experimental.pallas import tpu as pltpu
from jax.sharding import PartitionSpec as P

BF = jnp.bfloat16
F32 = jnp.float32
ROOM = 48 * 1024 * 1024
VMEM = pltpu.VMEM


def inner(left, right):
    return lax.dot_general(
        left, right, (((0,), (0,)), ((), ())), preferred_element_type=F32
    )


def outer(left, right):
    return lax.dot_general(
        left, right, (((1,), (1,)), ((), ())), preferred_element_type=F32
    )


def times(left, right):
    return jnp.dot(left, right, preferred_element_type=F32)


def swap(value, axis, masks):
    count = lax.axis_size(axis)
    pairs = [(i, i ^ masks[i % len(masks)]) for i in range(count)]
    return lax.ppermute(value, axis, pairs)


def like(rows, columns, kind):
    return jax.ShapeDtypeStruct((rows, columns), kind)


def whole(array):
    return pl.BlockSpec(array.shape, lambda n, s: (0,) * len(array.shape))


def run(body, outs, ins, after, numbers, grid=1, in_specs=None, out_specs=None, scratch=()):
    count, late = 1 + len(ins), len(after)

    def kernel(*refs):
        body(*refs[:count], *refs[count + late :])

    in_specs = in_specs or [None] * len(ins)
    out_specs = out_specs or [None] * len(outs)
    return pl.pallas_call(
        kernel,
        out_shape=tuple(outs),
        grid_spec=pltpu.PrefetchScalarGridSpec(
            num_scalar_prefetch=1,
            grid=(grid,),
            in_specs=[s or whole(a) for s, a in zip(in_specs, ins)]
            + [pl.BlockSpec(memory_space=pl.ANY)] * late,
            out_specs=tuple(s or whole(a) for s, a in zip(out_specs, outs)),
            scratch_shapes=list(scratch),
        ),
        compiler_params=pltpu.CompilerParams(vmem_limit_bytes=ROOM),
        cost_estimate=pl.CostEstimate(flops=0, bytes_accessed=0, transcendentals=0),
    )(numbers, *ins, *after)


def sort_body(patch, part, own, numbers, grad, *blocks):
    size = own * part
    row = lax.broadcasted_iota(jnp.int32, (size, grad.shape[0]), 0)
    source = lax.broadcasted_iota(jnp.int32, (size, grad.shape[0]), 1)
    for m, block in enumerate(blocks):
        wanted = (row % part) * patch + numbers[m] * own + row // part
        block[...] = times((source == wanted).astype(BF), grad[...]).astype(BF)


def join_body(part, own, count, numbers, *refs):
    blocks, joined = refs[:-1], refs[-1]
    for m, block in enumerate(blocks):
        for j in range(own):
            start = pl.multiple_of((j * count + numbers[m]) * part, part)
            joined[pl.ds(start, part), :] = block[j * part : (j + 1) * part, :]


def id_of(ids, place):
    lane = lax.broadcasted_iota(jnp.int32, ids.shape, 1)
    return jnp.sum(jnp.where(lane == place, ids[...] + 1, 0), axis=1, keepdims=True) - 1


def vocab_line(numbers, first, count, height):
    lane = lax.broadcasted_iota(jnp.int32, (1, count * height), 1)
    line = lane % height
    for n in range(count):
        line = line + jnp.where(lane // height == n, numbers[first + n] * height, 0)
    return line


def hot(ids, line):
    return jnp.where(ids == line, 1.0, 0.0).astype(BF)


def forward_body(
    own, tp_count, share_count, height,
    numbers, ids_own, ids_other, out_own, out_other, in_grad, proj, emb, gain, up,
    slots, normed, scale, r_rows, h_part, slope, table_kept, table_sent,
):
    n = pl.program_id(0)
    patches = ids_own.shape[0]
    slot = proj.shape[0]
    vocab = emb.shape[0]

    @pl.when(n == 0)
    def _():
        hots = []
        line = lax.broadcasted_iota(jnp.int32, (1, vocab), 1)
        for side, (ids, out) in enumerate(((ids_own, out_own), (ids_other, out_other))):
            for j in range(own):
                first = (side * own + j) * patches
                slots[first : first + patches, :] = out[:, j * slot : (j + 1) * slot]
                hots.append(hot(id_of(ids, numbers[0] * own + j - 1), line))
        u_rows = times(slots[...], proj[...])
        u_rows = u_rows + times(jnp.concatenate(hots, axis=0), emb[...])
        factor = lax.rsqrt(jnp.mean(u_rows * u_rows, axis=1, keepdims=True) + 1e-05)
        value = u_rows * factor
        scale[...] = factor
        normed[...] = value.astype(BF)
        r_rows[...] = (value * gain[...]).astype(BF)

    a_rows = times(r_rows[...], up[...])
    sig = jax.nn.sigmoid(a_rows)
    h_part[...] = (a_rows * sig).astype(BF)
    slope[...] = (sig * (1.0 + a_rows * (1.0 - sig))).astype(BF)

    @pl.when(n == share_count - 1)
    def _():
        for first, target in ((tp_count, table_kept), (tp_count + share_count, table_sent)):
            line = vocab_line(numbers, first, share_count, height)
            total = None
            for j in range(own):
                picked = hot(id_of(ids_own, numbers[0] * own + j), line)
                term = inner(picked, in_grad[:, j * slot : (j + 1) * slot])
                total = term if total is None else total + term
            target[...] = total.astype(target.dtype)


def back_body(share_count, numbers, out_rows, slope, down, up, da, dr_part, dr_sent):
    n = pl.program_id(0)
    value = (outer(out_rows[...], down[...]) * slope[...].astype(F32)).astype(BF)
    da[...] = value
    term = outer(value, up[...])

    @pl.when(n == 0)
    def _():
        dr_part[...] = term

    @pl.when(n > 0)
    def _():
        dr_part[...] += term

    @pl.when(n == share_count - 1)
    def _():
        dr_sent[...] = dr_part[...].astype(BF)


def product_body(lefts, rights, unit, rows, seq_first, numbers, *refs):
    left, right = refs[:lefts], refs[lefts : lefts + rights]
    kept, sent, total = refs[lefts + rights :]
    n = pl.program_id(0)

    def piece(parts, i):
        if len(parts) > 1:
            return parts[i][...]
        return parts[0][i * rows : (i + 1) * rows, :]

    value = inner(piece(left, 0), piece(right, 0))
    value = value + inner(piece(left, 1), piece(right, 1))
    total[...] = value
    count = total.shape[0] // unit

    def put(target, places):
        for i, m in enumerate(places):
            start = pl.multiple_of(numbers[m] * unit, unit)
            block = total[pl.ds(start, unit), :]
            target[i * unit : (i + 1) * unit, :] = block.astype(target.dtype)

    if seq_first:
        reverse = sorted(range(count), key=lambda m: bin(m + count)[:2:-1])

        @pl.when(n < pl.num_programs(0) // 2)
        def _():
            put(kept, reverse)

        @pl.when(n >= pl.num_programs(0) // 2)
        def _():
            put(sent, reverse)

    else:
        ordered = sorted(range(count), key=lambda m: bin(m + count)[:2:-1])
        put(kept, ordered[: count // 2])
        put(sent, ordered[count // 2 :])


def norm_body(
    own, tp_count, share_count, height,
    numbers, part_own, part_other, more_own, more_other, normed, scale, gain, out_own,
    out_other, ids_own, ids_other, table_kept, table_more,
    du, kept, sent,
):
    patches = ids_own.shape[0]
    rows = part_own.shape[0]
    line = vocab_line(numbers, tp_count, share_count, height)
    gains = None
    table = None
    sides = (
        (part_own, more_own, out_own, ids_own),
        (part_other, more_other, out_other, ids_other),
    )
    for side, (part, more, out, ids) in enumerate(sides):
        at = slice(side * rows, (side + 1) * rows)
        dr = part[...] + more[...].astype(F32)
        unit = normed[at, :].astype(F32)
        term = jnp.sum(dr * unit, axis=0, keepdims=True)
        gains = term if gains is None else gains + term
        dn = dr * gain[...]
        mean = jnp.mean(dn * unit, axis=1, keepdims=True)
        value = (out[...].astype(F32) + scale[at, :] * (dn - unit * mean)).astype(BF)
        du[at, :] = value
        for j in range(own):
            picked = hot(id_of(ids, numbers[0] * own + j - 1), line)
            term = inner(picked, value[j * patches : (j + 1) * patches, :])
            table = term if table is None else table + term
    width = normed.shape[1]
    strip = width // (2 * share_count)
    lane = lax.broadcasted_iota(jnp.int32, (16, width), 1)
    row = lax.broadcasted_iota(jnp.int32, (16, width), 0)
    other = table_kept[...] + table_more[...].astype(F32)
    size = 2 * height + 16
    for n in range(share_count):
        target = kept if n < share_count // 2 else sent
        first = (n % (share_count // 2)) * size
        at = slice(n * height, (n + 1) * height)
        target[first : first + height, :] = other[at, :].astype(BF)
        target[first + height : first + 2 * height, :] = table[at, :].astype(BF)
        mine = (lane // strip == numbers[tp_count + n]) & (row == 0)
        target[first + 2 * height : first + size, :] = jnp.where(mine, gains, 0.0).astype(BF)


def spread_body(own, numbers, du, proj, out):
    patches = out.shape[0]
    slot = proj.shape[0]
    for j in range(own):
        value = outer(du[j * patches : (j + 1) * patches, :], proj[...])
        out[:, j * slot : (j + 1) * slot] = value.astype(BF)


def add_body(numbers, kept, arrived, keep, send):
    half = keep.shape[0]
    keep[...] = (kept[:half, :].astype(F32) + arrived[:half, :].astype(F32)).astype(keep.dtype)
    send[...] = (kept[half:, :].astype(F32) + arrived[half:, :].astype(F32)).astype(send.dtype)


def sum_body(numbers, kept, arrived, summed):
    summed[...] = (kept[...].astype(F32) + arrived[...].astype(F32)).astype(summed.dtype)


def turned_body(numbers, kept, arrived, summed):
    summed[...] = (kept[...].astype(F32) + arrived[...].astype(F32)).T


def stack_body(numbers, first, second, both):
    rows = first.shape[0]
    both[:rows, :] = first[...]
    both[rows:, :] = second[...]


def tables_body(numbers, first, second, place, glob, local, gain):
    half = first.shape[0]
    vocab = glob.shape[0]
    row = lax.broadcasted_iota(jnp.int32, (vocab, half), 0)
    for which, target in enumerate((glob, local)):
        total = None
        for side, value in enumerate((first, second)):
            line = place[which : which + 1, side * half : (side + 1) * half]
            term = times(hot(row, line), value[...])
            total = term if total is None else total + term
        target[...] = total
    mark = place[2:10, :].astype(F32).astype(BF)
    gains = times(mark[:, :half], first[...]) + times(mark[:, half:], second[...])
    gain[...] = gains[:1, :]


def on_device(
    byte_ids,
    global_out,
    global_in_grad,
    out_grad,
    proj_weight,
    emb_local,
    norm_gain,
    up_weight,
    down_weight,
):
    seq_count = lax.axis_size("seq")
    tp_count = lax.axis_size("tp")
    seq_place = lax.axis_index("seq")
    tp_place = lax.axis_index("tp")
    core = seq_place & 1
    chip = seq_place >> 1
    stages = seq_count.bit_length() - 2
    levels = tp_count.bit_length() - 1
    share_count = 1 << stages
    walks = (list(range(1, stages + 1)), list(range(stages, 0, -1)))
    patches, patch = byte_ids.shape
    slot, width = proj_weight.shape
    hidden = up_weight.shape[1]
    vocab = emb_local.shape[0]
    own = patch // tp_count
    part = patches // tp_count
    rows = own * patches
    height = vocab // seq_count
    chunk = hidden // seq_count

    def share_mask(number, walk):
        mask = 0
        for k in range(stages):
            if (number >> (stages - 1 - k)) & 1:
                mask |= 1 << (walk[k] - 1)
        return mask

    def shares_of(which):
        return [
            2 * (chip ^ jnp.where(which == 0, share_mask(n, walks[0]), share_mask(n, walks[1])))
            + which
            for n in range(share_count)
        ]

    shares = shares_of(core)
    others = shares_of(1 - core)
    near = [tp_place ^ m for m in range(tp_count)]
    numbers = jnp.stack(near + shares + others).astype(jnp.int32)
    call = functools.partial(run, numbers=numbers)

    def core_swap(value):
        return swap(value, "seq", (1,))

    def go(value, step):
        kind, k = step
        if kind == "seq":
            return swap(value, "seq", (1 << walks[0][k], 1 << walks[1][k]))
        return swap(value, "tp", (1 << k,))

    ids_other = core_swap(byte_ids)
    out_other = core_swap(global_out)
    blocks = call(
        functools.partial(sort_body, patch, part, own),
        [like(own * part, width, BF)] * tp_count,
        [out_grad],
        [],
    )
    blocks = [swap(b, "tp", (m,)) if m else b for m, b in enumerate(blocks)]

    by_share = pl.BlockSpec((2 * rows, chunk), lambda n, s: (0, n))
    up_spec = pl.BlockSpec((slot, chunk), lambda n, s: (0, s[tp_count + n]))
    down_spec = pl.BlockSpec((chunk, width), lambda n, s: (s[tp_count + n], 0))
    gain_line = norm_gain.reshape(1, width)
    slots, normed, scale, r_rows, h_rows, slope, glob_kept, glob_sent = call(
        functools.partial(forward_body, own, tp_count, share_count, height),
        [
            like(2 * rows, slot, BF),
            like(2 * rows, width, BF),
            like(2 * rows, 1, F32),
            like(2 * rows, width, BF),
            like(2 * rows, share_count * chunk, BF),
            like(2 * rows, share_count * chunk, BF),
            like(vocab // 2, width, F32),
            like(vocab // 2, width, BF),
        ],
        [
            byte_ids, ids_other, global_out, out_other, global_in_grad,
            proj_weight, emb_local, gain_line, up_weight,
        ],
        [blocks[0]],
        grid=share_count,
        in_specs=[None] * 8 + [up_spec],
        out_specs=[None] * 4 + [by_share, by_share, None, None],
    )
    glob_more = core_swap(glob_sent)

    (grad_own,) = call(
        functools.partial(join_body, part, own, tp_count),
        [like(rows, width, BF)],
        blocks,
        [r_rows],
    )
    grad_other = core_swap(grad_own)

    def back(grad, side, after):
        return call(
            functools.partial(back_body, share_count),
            [
                like(rows, share_count * chunk, BF),
                like(rows, width, F32),
                like(rows, width, BF),
            ],
            [grad, slope, down_weight, up_weight],
            after,
            grid=share_count,
            in_specs=[
                None,
                pl.BlockSpec((rows, chunk), lambda n, s: (side, n)),
                down_spec,
                up_spec,
            ],
            out_specs=[pl.BlockSpec((rows, chunk), lambda n, s: (0, n)), None, None],
        )

    def product(lefts, rights, share, seq_first, moving, after):
        unit = share // tp_count
        kind = BF if unit % 16 == 0 else F32
        columns = rights[0].shape[1]
        if moving and share % 128:
            lefts = [
                jnp.concatenate(
                    [lax.dynamic_slice_in_dim(x, s * share, share, 1) for s in shares], axis=1
                )
                for x in lefts
            ]
            moving = False

        def left_spec(array):
            if share % 128:
                return None
            if moving:
                return pl.BlockSpec((array.shape[0], share), lambda n, s: (0, s[tp_count + n]))
            return pl.BlockSpec((array.shape[0], share), lambda n, s: (0, n))

        grid = share_count
        if share % 128:
            return slow_product(lefts, rights, share, seq_first, after)
        half = share_count // 2
        if seq_first:
            out_specs = [
                pl.BlockSpec((share, columns), lambda n, s: (jnp.minimum(n, half - 1), 0)),
                pl.BlockSpec((share, columns), lambda n, s: (jnp.maximum(n - half, 0), 0)),
            ]
        else:
            out_specs = [pl.BlockSpec((share // 2, columns), lambda n, s: (n, 0))] * 2
        return call(
            functools.partial(
                product_body, len(lefts), len(rights), unit, rows, seq_first
            ),
            [like(share * share_count // 2, columns, kind)] * 2,
            [*lefts, *rights],
            after,
            grid=grid,
            in_specs=[left_spec(x) for x in lefts] + [None] * len(rights),
            out_specs=out_specs,
            scratch=[VMEM((share, columns), F32)],
        )

    def slow_product(lefts, rights, share, seq_first, after):
        left = jnp.concatenate(lefts, axis=0)
        right = jnp.concatenate(rights, axis=0)
        unit = share // tp_count
        value = inner(left, right).reshape(share_count, tp_count, unit, -1)
        value = jnp.stack(
            [lax.dynamic_index_in_dim(value, m, 1, keepdims=False) for m in near], axis=1
        )
        order = sorted(range(tp_count), key=lambda m: bin(m + tp_count)[:2:-1])
        value = jnp.stack([value[:, m] for m in order], axis=1)
        if not seq_first:
            value = value.reshape(share_count, 2, tp_count // 2, unit, -1).swapaxes(0, 1)
        value = value.reshape(2, share * share_count // 2, -1)
        value = value.astype(BF if unit % 16 == 0 else F32)
        return value[0], value[1]

    seq_steps = [("seq", k) for k in range(stages)]
    tp_steps = [("tp", k) for k in range(levels)]
    orders = {True: seq_steps + tp_steps, False: tp_steps[:1] + seq_steps + tp_steps[1:]}

    class Chain:
        def __init__(self, halves, seq_first, turned):
            self.kept, sent = halves
            self.steps, self.turned, self.at = orders[seq_first], turned, 0
            self.arrived = go(sent, self.steps[0])
            self.left = len(self.steps)

        def next(self, after):
            self.at += 1
            self.left -= 1
            rows, columns = self.kept.shape
            ins = [self.kept, self.arrived]
            if self.left:
                outs = [like(rows // 2, columns, self.kept.dtype)] * 2
                self.kept, sent = call(add_body, outs, ins, after)
                self.arrived = go(sent, self.steps[self.at])
            elif self.turned:
                (self.kept,) = call(turned_body, [like(columns, rows, F32)], ins, after)
            else:
                (self.kept,) = call(sum_body, [like(rows, columns, F32)], ins, after)
            return self.kept

    class Table:
        def __init__(self, kept, sent):
            self.kept, self.at = kept, 0
            self.plan = (
                [("half", s) for s in seq_steps]
                + [("sum", s) for s in tp_steps]
                + [("join", s) for s in reversed(seq_steps)]
                + [("join", None)]
            )
            self.left = len(self.plan) - 1
            self.arrived = go(sent, self.plan[0][1])

        def next(self, after):
            last, (kind, step) = self.plan[self.at][0], self.plan[self.at + 1]
            rows, columns = self.kept.shape
            ins = [self.kept, self.arrived]
            if last == "half" and kind == "half":
                self.kept, sent = call(add_body, [like(rows // 2, columns, BF)] * 2, ins, after)
            elif last == "join":
                (self.kept,) = call(stack_body, [like(2 * rows, columns, BF)], ins, after)
                sent = self.kept
            else:
                (self.kept,) = call(sum_body, [like(rows, columns, BF)], ins, after)
                sent = self.kept
            self.at += 1
            self.left -= 1
            self.arrived = core_swap(sent) if step is None else go(sent, step)
            return self.kept

    da_own, dr_own, dr_own_sent = back(grad_own, 0, [glob_kept])
    dr_other_more = core_swap(dr_own_sent)
    down = Chain(
        product([h_rows], [grad_own, grad_other], chunk, True, False, [da_own]), True, False
    )
    da_other, dr_other, dr_other_sent = back(grad_other, 1, [down.kept])
    dr_own_more = core_swap(dr_other_sent)
    up = Chain(
        product([da_own, da_other], [r_rows], chunk, False, False, [dr_other]), False, True
    )
    size = 2 * height + 16
    du_rows, kept, sent = call(
        functools.partial(norm_body, own, tp_count, share_count, height),
        [like(2 * rows, width, BF)] + [like(share_count // 2 * size, width, BF)] * 2,
        [
            dr_own, dr_other, dr_own_more, dr_other_more, normed, scale, gain_line, grad_own,
            grad_other, byte_ids, ids_other, glob_kept, glob_more,
        ],
        [up.kept],
    )
    table = Table(kept, sent)
    proj = Chain(
        product([du_rows], [slots], width // seq_count, True, True, [kept]), True, True
    )
    (glob_out_grad,) = call(
        functools.partial(spread_body, own),
        [like(patches, own * slot, BF)],
        [du_rows, proj_weight],
        [proj.kept],
        in_specs=[pl.BlockSpec((rows, width), lambda n, s: (0, 0)), None],
    )

    last = glob_out_grad
    queue = [
        down, table, proj, down, table, proj, up, table, down, proj, table, up, down,
        table, proj, up, table, up, table,
    ]
    for chain in queue + [table, proj, down, up] * 16:
        if chain.left:
            last = chain.next([last])

    all_numbers = jnp.stack(shares + others)
    inside = jnp.arange(size)[None, :]
    own_row = all_numbers[:, None] * height + inside
    place = jnp.stack(
        [
            jnp.where(inside < height, own_row, -1).reshape(-1),
            jnp.where(
                (inside >= height) & (inside < 2 * height), own_row - height, -1
            ).reshape(-1),
        ]
        + [jnp.broadcast_to(inside == 2 * height, own_row.shape).reshape(-1).astype(jnp.int32)] * 8
    ).astype(jnp.int32)
    emb_global_grad, emb_local_grad, gain_grad = call(
        tables_body,
        [like(vocab, width, F32), like(vocab, width, F32), like(1, width, F32)],
        [table.kept, table.arrived, place],
        [last],
    )
    return (
        glob_out_grad,
        emb_global_grad,
        emb_local_grad,
        gain_grad.reshape(width),
        proj.kept,
        up.kept,
        down.kept,
    )


def solution(mesh):
    placed = (
        P("seq", None),
        P("seq", "tp"),
        P("seq", "tp"),
        P(("seq", "tp"), None),
        P(),
        P(),
        P(),
        P(),
        P(),
    )
    return jax.shard_map(
        on_device,
        mesh=mesh,
        in_specs=placed,
        out_specs=(
            P("seq", "tp"),
            P(),
            P(),
            P(),
            P(None, ("seq", "tp")),
            P(None, ("seq", "tp")),
            P(("seq", "tp"), None),
        ),
        check_vma=False,
    )
```

```python
import functools

import jax
import jax.numpy as jnp
from jax import lax
from jax.experimental import pallas as pl
from jax.experimental.pallas import tpu as pltpu
from jax.sharding import PartitionSpec as P

BF = jnp.bfloat16
F32 = jnp.float32
ROOM = 48 * 1024 * 1024
SMALL = 16 * 1024 * 1024
VMEM = pltpu.VMEM


def inner(left, right):
    return lax.dot_general(
        left, right, (((0,), (0,)), ((), ())), preferred_element_type=F32
    )


def outer(left, right):
    return lax.dot_general(
        left, right, (((1,), (1,)), ((), ())), preferred_element_type=F32
    )


def times(left, right):
    return jnp.dot(left, right, preferred_element_type=F32)


def swap(value, axis, masks):
    count = lax.axis_size(axis)
    pairs = [(i, i ^ masks[i % len(masks)]) for i in range(count)]
    return lax.ppermute(value, axis, pairs)


def like(rows, columns, kind):
    return jax.ShapeDtypeStruct((rows, columns), kind)


def whole(array):
    return pl.BlockSpec(array.shape, lambda n, s: (0,) * len(array.shape))


def run(
    body, outs, ins, after, numbers, in_specs=None, out_specs=None, scratch=(), room=ROOM, alias=None
):
    count, late = 1 + len(ins), len(after)

    def kernel(*refs):
        body(*refs[:count], *refs[count + late :])

    in_specs = in_specs or [None] * len(ins)
    out_specs = out_specs or [None] * len(outs)
    return pl.pallas_call(
        kernel,
        out_shape=tuple(outs),
        grid_spec=pltpu.PrefetchScalarGridSpec(
            num_scalar_prefetch=1,
            grid=(1,),
            in_specs=[s or whole(a) for s, a in zip(in_specs, ins)]
            + [pl.BlockSpec(memory_space=pl.ANY)] * late,
            out_specs=tuple(s or whole(a) for s, a in zip(out_specs, outs)),
            scratch_shapes=list(scratch),
        ),
        input_output_aliases=alias or {},
        compiler_params=pltpu.CompilerParams(vmem_limit_bytes=room),
        cost_estimate=pl.CostEstimate(flops=0, bytes_accessed=0, transcendentals=0),
    )(numbers, *ins, *after)


def sort_body(patch, part, own, numbers, grad, *blocks):
    size = own * part
    row = lax.broadcasted_iota(jnp.int32, (size, grad.shape[0]), 0)
    source = lax.broadcasted_iota(jnp.int32, (size, grad.shape[0]), 1)
    for m, block in enumerate(blocks):
        wanted = (row % part) * patch + numbers[m] * own + row // part
        block[...] = times((source == wanted).astype(BF), grad[...]).astype(BF)


def join_body(part, own, count, numbers, *refs):
    blocks, joined = refs[:-1], refs[-1]
    for m, block in enumerate(blocks):
        for j in range(own):
            start = pl.multiple_of((j * count + numbers[m]) * part, part)
            joined[pl.ds(start, part), :] = block[j * part : (j + 1) * part, :]


def id_of(ids, place):
    lane = lax.broadcasted_iota(jnp.int32, ids.shape, 1)
    return jnp.sum(jnp.where(lane == place, ids[...] + 1, 0), axis=1, keepdims=True) - 1


def vocab_line(numbers, first, count, height):
    lane = lax.broadcasted_iota(jnp.int32, (1, count * height), 1)
    line = lane % height
    for n in range(count):
        line = line + jnp.where(lane // height == n, numbers[first + n] * height, 0)
    return line


def hot(ids, line):
    return jnp.where(ids == line, 1.0, 0.0).astype(BF)


def hots_body(own, tp_count, share_count, height, numbers, ids_own, ids_other, prev, here, mine):
    patches = ids_own.shape[0]
    plain = lax.broadcasted_iota(jnp.int32, (1, prev.shape[1]), 1)
    line = vocab_line(numbers, tp_count, share_count, height)
    both = vocab_line(numbers, tp_count, 2 * share_count, height)
    for side, ids in enumerate((ids_own, ids_other)):
        for j in range(own):
            at = slice((side * own + j) * patches, (side * own + j + 1) * patches)
            before = id_of(ids, numbers[0] * own + j - 1)
            prev[at, :] = hot(before, plain)
            here[at, :] = hot(before, line)
            if side == 0:
                mine[at, :] = hot(id_of(ids, numbers[0] * own + j), both)


def pick_body(tp_count, share_count, numbers, up, down, up_here, down_here, ups, downs, ready):
    chunk = downs.shape[1]
    unit = chunk // tp_count
    half = chunk // 2
    copies = []
    for n in range(share_count):
        at = pl.ds(pl.multiple_of(numbers[tp_count + n] * chunk, chunk), chunk)
        copies.append(
            (
                pltpu.make_async_copy(up.at[:, at], ups.at[n], ready.at[0, n]),
                pltpu.make_async_copy(down.at[at, :], downs.at[n], ready.at[1, n]),
            )
        )
        copies[-1][0].start()
        copies[-1][1].start()
    order = sorted(range(tp_count), key=lambda m: bin(m + tp_count)[:2:-1])
    row = lax.broadcasted_iota(jnp.int32, (chunk, chunk), 0)
    column = lax.broadcasted_iota(jnp.int32, (chunk, chunk), 1)
    source = column % unit
    for i, m in enumerate(order):
        source = source + jnp.where(column // unit == i, numbers[m] * unit, 0)
    turn = (row == source).astype(BF)
    for n in range(share_count):
        copies[n][0].wait()
        copies[n][1].wait()
        sorted_up = times(ups[n], turn).astype(BF)
        for z in range(2):
            first = (z * share_count + n) * half
            up_here[:, first : first + half] = sorted_up[:, z * half : (z + 1) * half]
            for i in range(tp_count // 2):
                m = order[z * (tp_count // 2) + i]
                start = pl.multiple_of(numbers[m] * unit, unit)
                down_here[first + i * unit : first + (i + 1) * unit, :] = downs[
                    n, pl.ds(start, unit), :
                ]


def tables_in_body(
    share_count, first_share, height, numbers, glob, glob_more, local, gains, kept, sent
):
    width = glob.shape[1]
    strip = width // (2 * share_count)
    lane = lax.broadcasted_iota(jnp.int32, (16, width), 1)
    row = lax.broadcasted_iota(jnp.int32, (16, width), 0)
    both = glob[...].astype(F32) + glob_more[...].astype(F32)
    size = 2 * height + 16
    for n in range(share_count):
        target = kept if n < share_count // 2 else sent
        first = (n % (share_count // 2)) * size
        at = slice(n * height, (n + 1) * height)
        target[first : first + height, :] = both[at, :].astype(BF)
        target[first + height : first + 2 * height, :] = local[at, :].astype(BF)
        mine = (lane // strip == numbers[first_share + n]) & (row == 0)
        target[first + 2 * height : first + size, :] = jnp.where(mine, gains[...], 0.0).astype(BF)


def gate_body(numbers, value, same):
    pass


def sorted_add_body(tp_count, share, numbers, kept, arrived, keep, send):
    half = keep.shape[0]
    unit = share // tp_count
    order = sorted(range(tp_count), key=lambda m: bin(m + tp_count)[:2:-1])
    for n in range(kept.shape[0] // share):
        for i, m in enumerate(order):
            at = pl.ds(n * share + pl.multiple_of(numbers[m] * unit, unit), unit)
            value = kept[at, :].astype(F32) + arrived[at, :].astype(F32)
            place = n * share + i * unit
            target = keep if place < half else send
            row = place % half
            target[row : row + unit, :] = value.astype(target.dtype)


def add_body(numbers, kept, arrived, keep, send):
    half = keep.shape[0]
    keep[...] = (kept[:half, :].astype(F32) + arrived[:half, :].astype(F32)).astype(keep.dtype)
    send[...] = (kept[half:, :].astype(F32) + arrived[half:, :].astype(F32)).astype(send.dtype)


def sum_body(numbers, kept, arrived, summed):
    summed[...] = (kept[...].astype(F32) + arrived[...].astype(F32)).astype(summed.dtype)


def turned_body(numbers, kept, arrived, summed):
    summed[...] = (kept[...].astype(F32) + arrived[...].astype(F32)).T


def stack_body(numbers, first, second, both):
    rows = first.shape[0]
    both[:rows, :] = first[...]
    both[rows:, :] = second[...]


def tables_body(numbers, first, second, place, glob, local, gain):
    half = first.shape[0]
    vocab = glob.shape[0]
    row = lax.broadcasted_iota(jnp.int32, (vocab, half), 0)
    for which, target in enumerate((glob, local)):
        total = None
        for side, value in enumerate((first, second)):
            line = place[which : which + 1, side * half : (side + 1) * half]
            term = times(hot(row, line), value[...])
            total = term if total is None else total + term
        target[...] = total
    mark = place[2:10, :].astype(F32).astype(BF)
    gains = times(mark[:, :half], first[...]) + times(mark[:, half:], second[...])
    gain[...] = gains[:1, :]


def on_device(
    byte_ids,
    global_out,
    global_in_grad,
    out_grad,
    proj_weight,
    emb_local,
    norm_gain,
    up_weight,
    down_weight,
):
    seq_count = lax.axis_size("seq")
    tp_count = lax.axis_size("tp")
    seq_place = lax.axis_index("seq")
    tp_place = lax.axis_index("tp")
    core = seq_place & 1
    chip = seq_place >> 1
    stages = seq_count.bit_length() - 2
    levels = tp_count.bit_length() - 1
    share_count = 1 << stages
    walks = (list(range(1, stages + 1)), list(range(stages, 0, -1)))
    patches, patch = byte_ids.shape
    slot, width = proj_weight.shape
    hidden = up_weight.shape[1]
    vocab = emb_local.shape[0]
    own = patch // tp_count
    part = patches // tp_count
    rows = own * patches
    height = vocab // seq_count
    chunk = hidden // seq_count

    def share_mask(number, walk):
        mask = 0
        for k in range(stages):
            if (number >> (stages - 1 - k)) & 1:
                mask |= 1 << (walk[k] - 1)
        return mask

    def shares_of(which):
        return [
            2 * (chip ^ jnp.where(which == 0, share_mask(n, walks[0]), share_mask(n, walks[1])))
            + which
            for n in range(share_count)
        ]

    shares = shares_of(core)
    others = shares_of(1 - core)
    near = [tp_place ^ m for m in range(tp_count)]
    numbers = jnp.stack(near + shares + others).astype(jnp.int32)
    call = functools.partial(run, numbers=numbers)

    def core_swap(value):
        return swap(value, "seq", (1,))

    def go(value, step):
        kind, k = step
        if kind == "seq":
            return swap(value, "seq", (1 << walks[0][k], 1 << walks[1][k]))
        return swap(value, "tp", (1 << k,))

    def gate(value, after):
        there = pl.BlockSpec(memory_space=pl.ANY)
        (value,) = call(
            gate_body,
            [like(*value.shape, value.dtype)],
            [value],
            after,
            in_specs=[there],
            out_specs=[there],
            room=SMALL,
            alias={1: 0},
        )
        return value

    ids_other = core_swap(byte_ids)
    out_other = core_swap(global_out)
    blocks = call(
        functools.partial(sort_body, patch, part, own),
        [like(own * part, width, BF)] * tp_count,
        [out_grad],
        [],
        room=SMALL,
    )
    blocks = [swap(b, "tp", (m,)) if m else b for m, b in enumerate(blocks)]
    there = pl.BlockSpec(memory_space=pl.ANY)
    half = hidden // 4
    up_here, down_here = call(
        functools.partial(pick_body, tp_count, share_count),
        [like(width, hidden // 2, BF), like(hidden // 2, width, BF)],
        [up_weight, down_weight],
        [blocks[0]],
        in_specs=[there, there],
        scratch=[
            VMEM((share_count, width, chunk), BF),
            VMEM((share_count, chunk, width), BF),
            pltpu.SemaphoreType.DMA((2, share_count)),
        ],
        room=SMALL,
    )
    prev_hot, prev_here, own_hot = call(
        functools.partial(hots_body, own, tp_count, share_count, height),
        [like(2 * rows, vocab, BF), like(2 * rows, vocab // 2, BF), like(rows, vocab, BF)],
        [byte_ids, ids_other],
        [up_here],
        room=SMALL,
    )

    def by_slot(value):
        return [value[:, j * slot : (j + 1) * slot] for j in range(own)]

    slot_in = jnp.concatenate(by_slot(global_out) + by_slot(out_other), axis=0)
    u_rows = times(slot_in, proj_weight) + times(prev_hot, emb_local)
    scale = lax.rsqrt(jnp.mean(u_rows * u_rows, axis=1, keepdims=True) + 1e-05)
    normed = u_rows * scale
    r_rows = (normed * norm_gain).astype(BF)
    a_rows = times(r_rows, up_here)
    sig = jax.nn.sigmoid(a_rows)
    h_rows = (a_rows * sig).astype(BF)
    part_of = half // 2
    h_rows = jnp.concatenate(
        [
            h_rows[:, (2 * z + k) * part_of : (2 * z + k + 1) * part_of]
            for k in range(2)
            for z in range(2)
        ],
        axis=1,
    )

    gin = jnp.concatenate(by_slot(global_in_grad), axis=0)
    glob_sent = inner(own_hot[:, vocab // 2 :], gin).astype(BF)
    glob_kept = inner(own_hot[:, : vocab // 2], gin).astype(BF)
    glob_more = core_swap(glob_sent)

    (grad_own,) = call(
        functools.partial(join_body, part, own, tp_count),
        [like(rows, width, BF)],
        blocks,
        [h_rows, glob_kept],
        room=SMALL,
    )
    out_rows = jnp.concatenate([grad_own, core_swap(grad_own)], axis=0)

    seq_steps = [("seq", k) for k in range(stages)]
    tp_steps = [("tp", k) for k in range(levels)]

    class Chain:
        def __init__(self, kept, sent, steps, turned, share=0):
            self.kept, self.steps, self.turned, self.at = kept, steps, turned, 0
            self.share = share
            self.arrived = go(sent, self.steps[0])
            self.left = len(self.steps)

        def next(self, after):
            self.at += 1
            self.left -= 1
            rows, columns = self.kept.shape
            ins = [self.kept, self.arrived]
            if self.left:
                outs = [like(rows // 2, columns, self.kept.dtype)] * 2
                body = add_body
                if self.share and self.steps[self.at][0] == "tp" and self.steps[self.at][1] == 0:
                    body = functools.partial(sorted_add_body, tp_count, self.share)
                self.kept, sent = call(body, outs, ins, after)
                self.arrived = go(sent, self.steps[self.at])
            elif self.turned:
                (self.kept,) = call(turned_body, [like(columns, rows, F32)], ins, after)
            else:
                (self.kept,) = call(sum_body, [like(rows, columns, F32)], ins, after)
            return self.kept

    class Table:
        def __init__(self, kept, sent):
            self.kept, self.at = kept, 0
            self.plan = (
                [("half", s) for s in seq_steps]
                + [("sum", s) for s in tp_steps]
                + [("join", s) for s in reversed(seq_steps)]
                + [("join", None)]
            )
            self.left = len(self.plan) - 1
            self.arrived = go(sent, self.plan[0][1])

        def next(self, after):
            last, (kind, step) = self.plan[self.at][0], self.plan[self.at + 1]
            rows, columns = self.kept.shape
            ins = [self.kept, self.arrived]
            if last == "half" and kind == "half":
                self.kept, sent = call(add_body, [like(rows // 2, columns, BF)] * 2, ins, after)
            elif last == "join":
                (self.kept,) = call(stack_body, [like(2 * rows, columns, BF)], ins, after)
                sent = self.kept
            else:
                (self.kept,) = call(sum_body, [like(rows, columns, BF)], ins, after)
                sent = self.kept
            self.at += 1
            self.left -= 1
            self.arrived = core_swap(sent) if step is None else go(sent, step)
            return self.kept

    kind = BF if chunk // tp_count % 16 == 0 else F32
    sent = inner(h_rows[:, half:], out_rows).astype(kind)
    out_rows = gate(out_rows, [sent])
    kept = inner(h_rows[:, :half], out_rows).astype(kind)
    steps = seq_steps[:1] + tp_steps[:1] + seq_steps[1:] + tp_steps[1:]
    down = Chain(kept, sent, steps, False)

    dh_rows = outer(out_rows, down_here)
    da_rows = (dh_rows * sig * (1.0 + a_rows * (1.0 - sig))).astype(BF)
    dr_part = outer(da_rows, up_here)
    dr_sent = jnp.concatenate([dr_part[rows:], dr_part[:rows]], axis=0).astype(BF)
    dr_rows = dr_part + core_swap(dr_sent).astype(F32)
    sent = inner(da_rows[:, half:], r_rows).astype(kind)
    kept = inner(da_rows[:, :half], r_rows).astype(kind)
    steps = tp_steps[:1] + seq_steps + tp_steps[1:]
    up = Chain(kept, sent, steps, True)

    gain_part = jnp.sum(dr_rows * normed, axis=0, keepdims=True)
    dn_rows = dr_rows * norm_gain
    du_rows = (
        out_rows.astype(F32)
        + scale * (dn_rows - normed * jnp.mean(dn_rows * normed, axis=1, keepdims=True))
    ).astype(BF)
    size = 2 * height + 16
    kept, sent = call(
        functools.partial(tables_in_body, share_count, tp_count, height),
        [like(share_count // 2 * size, width, BF)] * 2,
        [glob_kept, glob_more, inner(prev_here, du_rows), gain_part],
        [up.kept],
        room=SMALL,
    )
    table = Table(kept, sent)
    share = width // seq_count
    kind = BF if share // tp_count % 16 == 0 else F32
    du_here = jnp.concatenate(
        [lax.dynamic_slice_in_dim(du_rows, s * share, share, 1) for s in shares], axis=1
    )
    cut = du_here.shape[1] // 2
    sent = inner(du_here[:, cut:], slot_in).astype(kind)
    kept = inner(du_here[:, :cut], slot_in).astype(kind)
    proj = Chain(kept, sent, seq_steps + tp_steps, True, share)
    back = outer(du_rows[:rows], proj_weight).astype(BF)
    glob_out_grad = jnp.concatenate(
        [back[j * patches : (j + 1) * patches] for j in range(own)], axis=1
    )

    last = [up.kept, proj.kept, table.kept, down.kept]
    queue = [
        down, table, proj, down, table, proj, up, table, down, proj, table, up, down,
        table, proj, up, table, up, table,
    ]
    for chain in queue + [table, proj, down, up] * 16:
        if chain.left:
            last = [chain.next(last)]

    all_numbers = jnp.stack(shares + others)
    inside = jnp.arange(size)[None, :]
    own_row = all_numbers[:, None] * height + inside
    place = jnp.stack(
        [
            jnp.where(inside < height, own_row, -1).reshape(-1),
            jnp.where(
                (inside >= height) & (inside < 2 * height), own_row - height, -1
            ).reshape(-1),
        ]
        + [jnp.broadcast_to(inside == 2 * height, own_row.shape).reshape(-1).astype(jnp.int32)] * 8
    ).astype(jnp.int32)
    emb_global_grad, emb_local_grad, gain_grad = call(
        tables_body,
        [like(vocab, width, F32), like(vocab, width, F32), like(1, width, F32)],
        [table.kept, table.arrived, place],
        last,
    )
    return (
        glob_out_grad,
        emb_global_grad,
        emb_local_grad,
        gain_grad.reshape(width),
        proj.kept,
        up.kept,
        down.kept,
    )


def solution(mesh):
    placed = (
        P("seq", None),
        P("seq", "tp"),
        P("seq", "tp"),
        P(("seq", "tp"), None),
        P(),
        P(),
        P(),
        P(),
        P(),
    )
    return jax.shard_map(
        on_device,
        mesh=mesh,
        in_specs=placed,
        out_specs=(
            P("seq", "tp"),
            P(),
            P(),
            P(),
            P(None, ("seq", "tp")),
            P(None, ("seq", "tp")),
            P(("seq", "tp"), None),
        ),
        check_vma=False,
    )
```

```python
import functools

import jax
import jax.numpy as jnp
from jax import lax
from jax.experimental import pallas as pl
from jax.experimental.pallas import tpu as pltpu
from jax.sharding import PartitionSpec as P

BF = jnp.bfloat16
F32 = jnp.float32
ROOM = 60 * 1024 * 1024
SMALL = 16 * 1024 * 1024
VMEM = pltpu.VMEM


def inner(left, right):
    return lax.dot_general(
        left, right, (((0,), (0,)), ((), ())), preferred_element_type=F32
    )


def outer(left, right):
    return lax.dot_general(
        left, right, (((1,), (1,)), ((), ())), preferred_element_type=F32
    )


def times(left, right):
    return jnp.dot(left, right, preferred_element_type=F32)


def swap(value, axis, masks):
    count = lax.axis_size(axis)
    pairs = [(i, i ^ masks[i % len(masks)]) for i in range(count)]
    return lax.ppermute(value, axis, pairs)


def like(rows, columns, kind):
    return jax.ShapeDtypeStruct((rows, columns), kind)


def whole(array):
    return pl.BlockSpec(array.shape, lambda n, s: (0,) * len(array.shape))


def run(
    body, outs, ins, after, numbers, in_specs=None, out_specs=None, scratch=(), room=ROOM, alias=None
):
    count, late = 1 + len(ins), len(after)

    def kernel(*refs):
        body(*refs[:count], *refs[count + late :])

    in_specs = in_specs or [None] * len(ins)
    out_specs = out_specs or [None] * len(outs)
    return pl.pallas_call(
        kernel,
        out_shape=tuple(outs),
        grid_spec=pltpu.PrefetchScalarGridSpec(
            num_scalar_prefetch=1,
            grid=(1,),
            in_specs=[s or whole(a) for s, a in zip(in_specs, ins)]
            + [pl.BlockSpec(memory_space=pl.ANY)] * late,
            out_specs=tuple(s or whole(a) for s, a in zip(out_specs, outs)),
            scratch_shapes=list(scratch),
        ),
        input_output_aliases=alias or {},
        compiler_params=pltpu.CompilerParams(vmem_limit_bytes=room),
        cost_estimate=pl.CostEstimate(flops=0, bytes_accessed=0, transcendentals=0),
    )(numbers, *ins, *after)


def sort_body(patch, part, own, numbers, grad, *blocks):
    size = own * part
    row = lax.broadcasted_iota(jnp.int32, (size, grad.shape[0]), 0)
    source = lax.broadcasted_iota(jnp.int32, (size, grad.shape[0]), 1)
    for m, block in enumerate(blocks):
        wanted = (row % part) * patch + numbers[m] * own + row // part
        block[...] = times((source == wanted).astype(BF), grad[...]).astype(BF)


def join_body(part, own, count, numbers, *refs):
    blocks, joined = refs[:-1], refs[-1]
    for m, block in enumerate(blocks):
        for j in range(own):
            start = pl.multiple_of((j * count + numbers[m]) * part, part)
            joined[pl.ds(start, part), :] = block[j * part : (j + 1) * part, :]


def sent_order(count):
    return sorted(range(count), key=lambda m: bin(m + count)[:2:-1])


def id_of(ids, place):
    lane = lax.broadcasted_iota(jnp.int32, ids.shape, 1)
    return jnp.sum(jnp.where(lane == place, ids[...] + 1, 0), axis=1, keepdims=True) - 1


def vocab_line(numbers, first, count, height):
    lane = lax.broadcasted_iota(jnp.int32, (1, count * height), 1)
    line = lane % height
    for n in range(count):
        line = line + jnp.where(lane // height == n, numbers[first + n] * height, 0)
    return line


def hot(ids, line):
    return jnp.where(ids == line, 1.0, 0.0).astype(BF)


def hots_body(own, tp_count, share_count, height, numbers, ids_own, ids_other, prev, here, mine):
    patches = ids_own.shape[0]
    plain = lax.broadcasted_iota(jnp.int32, (1, prev.shape[1]), 1)
    line = vocab_line(numbers, tp_count, share_count, height)
    both = vocab_line(numbers, tp_count, 2 * share_count, height)
    for side, ids in enumerate((ids_own, ids_other)):
        for j in range(own):
            at = slice((side * own + j) * patches, (side * own + j + 1) * patches)
            before = id_of(ids, numbers[0] * own + j - 1)
            prev[at, :] = hot(before, plain)
            here[at, :] = hot(before, line)
            if side == 0:
                mine[at, :] = hot(id_of(ids, numbers[0] * own + j), both)


def pick_body(tp_count, share_count, first, numbers, up, down, up_here, down_here, ups, downs, ready):
    chunk = downs.shape[1]
    unit = chunk // tp_count
    copies = []
    for n in range(share_count):
        at = pl.ds(pl.multiple_of(numbers[first + n] * chunk, chunk), chunk)
        copies.append(
            (
                pltpu.make_async_copy(up.at[:, at], ups.at[n], ready.at[0, n]),
                pltpu.make_async_copy(down.at[at, :], downs.at[n], ready.at[1, n]),
            )
        )
        copies[-1][0].start()
        copies[-1][1].start()
    order = sent_order(tp_count)
    row = lax.broadcasted_iota(jnp.int32, (chunk, chunk), 0)
    column = lax.broadcasted_iota(jnp.int32, (chunk, chunk), 1)
    source = column % unit
    for i, m in enumerate(order):
        source = source + jnp.where(column // unit == i, numbers[m] * unit, 0)
    turn = (row == source).astype(BF)
    for n in range(share_count):
        copies[n][0].wait()
        copies[n][1].wait()
        at = n * chunk
        up_here[:, at : at + chunk] = times(ups[n], turn).astype(BF)
        for i, m in enumerate(order):
            start = pl.multiple_of(numbers[m] * unit, unit)
            down_here[at + i * unit : at + (i + 1) * unit, :] = downs[n, pl.ds(start, unit), :]


def split_body(tp_count, share, numbers, value, kept, sent):
    unit = share // tp_count
    order = sent_order(tp_count)
    half = tp_count // 2
    for n in range(value.shape[0] // share):
        for i, m in enumerate(order):
            at = pl.ds(n * share + pl.multiple_of(numbers[m] * unit, unit), unit)
            target = kept if i < half else sent
            row = (n * half + i % half) * unit
            target[row : row + unit, :] = value[at, :].astype(target.dtype)


def tables_in_body(
    share_count, first_share, height, numbers, glob, glob_more, local, gains, kept, sent
):
    width = glob.shape[1]
    strip = width // (2 * share_count)
    lane = lax.broadcasted_iota(jnp.int32, (16, width), 1)
    row = lax.broadcasted_iota(jnp.int32, (16, width), 0)
    both = glob[...].astype(F32) + glob_more[...].astype(F32)
    size = 2 * height + 16
    for n in range(share_count):
        target = kept if n < share_count // 2 else sent
        first = (n % (share_count // 2)) * size
        at = slice(n * height, (n + 1) * height)
        target[first : first + height, :] = both[at, :].astype(BF)
        target[first + height : first + 2 * height, :] = local[at, :].astype(BF)
        mine = (lane // strip == numbers[first_share + n]) & (row == 0)
        target[first + 2 * height : first + size, :] = jnp.where(mine, gains[...], 0.0).astype(BF)


def gate_body(numbers, value, same):
    pass


def add_body(numbers, kept, arrived, keep, send):
    half = keep.shape[0]
    keep[...] = (kept[:half, :].astype(F32) + arrived[:half, :].astype(F32)).astype(keep.dtype)
    send[...] = (kept[half:, :].astype(F32) + arrived[half:, :].astype(F32)).astype(send.dtype)


def sum_body(numbers, kept, arrived, summed):
    summed[...] = (kept[...].astype(F32) + arrived[...].astype(F32)).astype(summed.dtype)


def turned_body(numbers, kept, arrived, summed):
    summed[...] = (kept[...].astype(F32) + arrived[...].astype(F32)).T


def stack_body(numbers, first, second, both):
    rows = first.shape[0]
    both[:rows, :] = first[...]
    both[rows:, :] = second[...]


def tables_body(numbers, first, second, place, glob, local, gain):
    half = first.shape[0]
    vocab = glob.shape[0]
    row = lax.broadcasted_iota(jnp.int32, (vocab, half), 0)
    for which, target in enumerate((glob, local)):
        total = None
        for side, value in enumerate((first, second)):
            line = place[which : which + 1, side * half : (side + 1) * half]
            term = times(hot(row, line), value[...])
            total = term if total is None else total + term
        target[...] = total
    mark = place[2:10, :].astype(F32).astype(BF)
    gains = times(mark[:, :half], first[...]) + times(mark[:, half:], second[...])
    gain[...] = gains[:1, :]


def on_device(
    byte_ids,
    global_out,
    global_in_grad,
    out_grad,
    proj_weight,
    emb_local,
    norm_gain,
    up_weight,
    down_weight,
):
    seq_count = lax.axis_size("seq")
    tp_count = lax.axis_size("tp")
    seq_place = lax.axis_index("seq")
    tp_place = lax.axis_index("tp")
    core = seq_place & 1
    chip = seq_place >> 1
    stages = seq_count.bit_length() - 2
    levels = tp_count.bit_length() - 1
    share_count = 1 << stages
    walks = (list(range(1, stages + 1)), list(range(stages, 0, -1)))
    patches, patch = byte_ids.shape
    slot, width = proj_weight.shape
    hidden = up_weight.shape[1]
    vocab = emb_local.shape[0]
    own = patch // tp_count
    part = patches // tp_count
    rows = own * patches
    height = vocab // seq_count
    chunk = hidden // seq_count

    def share_mask(number, walk):
        mask = 0
        for k in range(stages):
            if (number >> (stages - 1 - k)) & 1:
                mask |= 1 << (walk[k] - 1)
        return mask

    def shares_of(which):
        return [
            2 * (chip ^ jnp.where(which == 0, share_mask(n, walks[0]), share_mask(n, walks[1])))
            + which
            for n in range(share_count)
        ]

    shares = shares_of(core)
    others = shares_of(1 - core)
    near = [tp_place ^ m for m in range(tp_count)]
    upward, downward = list(range(1, stages + 1)), list(range(stages, 0, -1))
    hidden_shares = [2 * (chip ^ share_mask(n, downward)) + core for n in range(share_count)]
    numbers = jnp.stack(near + shares + others + hidden_shares).astype(jnp.int32)
    call = functools.partial(run, numbers=numbers)

    def core_swap(value):
        return swap(value, "seq", (1,))

    def go(value, step):
        kind, k = step
        if kind == "seq":
            return swap(value, "seq", (1 << walks[0][k], 1 << walks[1][k]))
        if kind == "both":
            return swap(value, "seq", (1 << k,))
        return swap(value, "tp", (1 << k,))

    def gate(value, after):
        there = pl.BlockSpec(memory_space=pl.ANY)
        (value,) = call(
            gate_body,
            [like(*value.shape, value.dtype)],
            [value],
            after,
            in_specs=[there],
            out_specs=[there],
            room=SMALL,
            alias={1: 0},
        )
        return value

    ids_other = core_swap(byte_ids)
    out_other = core_swap(global_out)
    blocks = call(
        functools.partial(sort_body, patch, part, own),
        [like(own * part, width, BF)] * tp_count,
        [out_grad],
        [],
        room=SMALL,
    )
    blocks = [swap(b, "tp", (m,)) if m else b for m, b in enumerate(blocks)]
    there = pl.BlockSpec(memory_space=pl.ANY)
    half = hidden // 4
    up_here, down_here = call(
        functools.partial(pick_body, tp_count, share_count, tp_count + 2 * share_count),
        [like(width, hidden // 2, BF), like(hidden // 2, width, BF)],
        [up_weight, down_weight],
        [blocks[0]],
        in_specs=[there, there],
        scratch=[
            VMEM((share_count, width, chunk), BF),
            VMEM((share_count, chunk, width), BF),
            pltpu.SemaphoreType.DMA((2, share_count)),
        ],
    )
    prev_hot, prev_here, own_hot = call(
        functools.partial(hots_body, own, tp_count, share_count, height),
        [like(2 * rows, vocab, BF), like(2 * rows, vocab // 2, BF), like(rows, vocab, BF)],
        [byte_ids, ids_other],
        [up_here],
        room=SMALL,
    )

    def by_slot(value):
        return [value[:, j * slot : (j + 1) * slot] for j in range(own)]

    slot_in = jnp.concatenate(by_slot(global_out) + by_slot(out_other), axis=0)
    u_rows = times(slot_in, proj_weight) + times(prev_hot, emb_local)
    scale = lax.rsqrt(jnp.mean(u_rows * u_rows, axis=1, keepdims=True) + 1e-05)
    normed = u_rows * scale
    r_rows = (normed * norm_gain).astype(BF)
    a_rows = times(r_rows, up_here)
    sig = jax.nn.sigmoid(a_rows)
    h_rows = (a_rows * sig).astype(BF)
    h_rows = lax.optimization_barrier(h_rows)
    order = sent_order(share_count)
    h_rows = jnp.concatenate([h_rows[:, n * chunk : (n + 1) * chunk] for n in order], axis=1)

    glob = [
        inner(own_hot[j * patches : (j + 1) * patches], value)
        for j, value in enumerate(by_slot(global_in_grad))
    ]
    glob = sum(glob[1:], glob[0])
    glob_sent = glob[vocab // 2 :].astype(BF)
    glob_kept = glob[: vocab // 2].astype(BF)
    glob_more = core_swap(glob_sent)

    (grad_own,) = call(
        functools.partial(join_body, part, own, tp_count),
        [like(rows, width, BF)],
        blocks,
        [h_rows, glob_kept],
        room=SMALL,
    )
    out_rows = jnp.concatenate([grad_own, core_swap(grad_own)], axis=0)

    seq_steps = [("seq", k) for k in range(stages)]
    tp_steps = [("tp", k) for k in range(levels)]

    class Chain:
        def __init__(self, kept, sent, steps, turned):
            self.kept, self.steps, self.turned, self.at = kept, steps, turned, 0
            self.arrived = go(sent, self.steps[0])
            self.left = len(self.steps)

        def next(self, after):
            self.at += 1
            self.left -= 1
            rows, columns = self.kept.shape
            ins = [self.kept, self.arrived]
            if self.left:
                outs = [like(rows // 2, columns, self.kept.dtype)] * 2
                self.kept, sent = call(add_body, outs, ins, after)
                self.arrived = go(sent, self.steps[self.at])
            elif self.turned:
                (self.kept,) = call(turned_body, [like(columns, rows, F32)], ins, after)
            else:
                (self.kept,) = call(sum_body, [like(rows, columns, F32)], ins, after)
            return self.kept

    class Table:
        def __init__(self, kept, sent):
            self.kept, self.at = kept, 0
            self.plan = (
                [("half", s) for s in seq_steps]
                + [("sum", s) for s in tp_steps]
                + [("join", s) for s in reversed(seq_steps)]
                + [("join", None)]
            )
            self.left = len(self.plan) - 1
            self.arrived = go(sent, self.plan[0][1])

        def next(self, after):
            last, (kind, step) = self.plan[self.at][0], self.plan[self.at + 1]
            rows, columns = self.kept.shape
            ins = [self.kept, self.arrived]
            if last == "half" and kind == "half":
                self.kept, sent = call(add_body, [like(rows // 2, columns, BF)] * 2, ins, after)
            elif last == "join":
                (self.kept,) = call(stack_body, [like(2 * rows, columns, BF)], ins, after)
                sent = self.kept
            else:
                (self.kept,) = call(sum_body, [like(rows, columns, BF)], ins, after)
                sent = self.kept
            self.at += 1
            self.left -= 1
            self.arrived = core_swap(sent) if step is None else go(sent, step)
            return self.kept

    dh_rows = outer(out_rows, down_here)
    da_rows = (dh_rows * sig * (1.0 + a_rows * (1.0 - sig))).astype(BF)
    dr_part = outer(da_rows, up_here)
    dr_sent = jnp.concatenate([dr_part[rows:], dr_part[:rows]], axis=0).astype(BF)
    kind = BF if chunk // tp_count % 16 == 0 else F32
    half = h_rows.shape[1] // 2
    down_kept = inner(h_rows[:, :half], out_rows).astype(kind)
    down_sent = inner(h_rows[:, half:], out_rows).astype(kind)
    up_kept = inner(da_rows[:, :half], r_rows).astype(kind)
    up_sent = inner(da_rows[:, half:], r_rows).astype(kind)
    down = Chain(down_kept, down_sent, [("both", k) for k in upward] + tp_steps, False)
    up = Chain(up_kept, up_sent, [("both", k) for k in downward] + tp_steps, True)
    dr_more = gate(core_swap(dr_sent), [down_sent, up_sent])
    dr_rows = dr_part + dr_more.astype(F32)

    gain_part = jnp.sum(dr_rows * normed, axis=0, keepdims=True)
    dn_rows = dr_rows * norm_gain
    du_rows = (
        out_rows.astype(F32)
        + scale * (dn_rows - normed * jnp.mean(dn_rows * normed, axis=1, keepdims=True))
    ).astype(BF)
    size = 2 * height + 16
    kept, sent = call(
        functools.partial(tables_in_body, share_count, tp_count, height),
        [like(share_count // 2 * size, width, BF)] * 2,
        [glob_kept, glob_more, inner(prev_here, du_rows), gain_part],
        [up.kept],
        room=SMALL,
    )
    table = Table(kept, sent)
    share = width // seq_count
    kind = BF if share // tp_count % 16 == 0 else F32
    du_here = jnp.concatenate(
        [lax.dynamic_slice_in_dim(du_rows, s * share, share, 1) for s in shares], axis=1
    )
    value = inner(du_here, slot_in)
    kept, sent = call(
        functools.partial(split_body, tp_count, share),
        [like(value.shape[0] // 2, slot, kind)] * 2,
        [value],
        [table.kept],
        room=SMALL,
    )
    proj = Chain(kept, sent, tp_steps[:1] + seq_steps + tp_steps[1:], True)
    back = outer(du_rows[:rows], proj_weight).astype(BF)
    glob_out_grad = jnp.concatenate(
        [back[j * patches : (j + 1) * patches] for j in range(own)], axis=1
    )

    last = [up.kept, proj.kept, table.kept, down.kept, glob_out_grad]
    queue = [
        table, proj, down, up, table, proj, table, down, up, proj, table, down, up, proj,
        table, down, up, table,
    ]
    for chain in queue + [table, proj, down, up] * 16:
        if chain.left:
            last = [chain.next(last)]

    all_numbers = jnp.stack(shares + others)
    inside = jnp.arange(size)[None, :]
    own_row = all_numbers[:, None] * height + inside
    place = jnp.stack(
        [
            jnp.where(inside < height, own_row, -1).reshape(-1),
            jnp.where(
                (inside >= height) & (inside < 2 * height), own_row - height, -1
            ).reshape(-1),
        ]
        + [jnp.broadcast_to(inside == 2 * height, own_row.shape).reshape(-1).astype(jnp.int32)] * 8
    ).astype(jnp.int32)
    emb_global_grad, emb_local_grad, gain_grad = call(
        tables_body,
        [like(vocab, width, F32), like(vocab, width, F32), like(1, width, F32)],
        [table.kept, table.arrived, place],
        last,
    )
    return (
        glob_out_grad,
        emb_global_grad,
        emb_local_grad,
        gain_grad.reshape(width),
        proj.kept,
        up.kept,
        down.kept,
    )


def solution(mesh):
    placed = (
        P("seq", None),
        P("seq", "tp"),
        P("seq", "tp"),
        P(("seq", "tp"), None),
        P(),
        P(),
        P(),
        P(),
        P(),
    )
    return jax.shard_map(
        on_device,
        mesh=mesh,
        in_specs=placed,
        out_specs=(
            P("seq", "tp"),
            P(),
            P(),
            P(),
            P(None, ("seq", "tp")),
            P(None, ("seq", "tp")),
            P(("seq", "tp"), None),
        ),
        check_vma=False,
    )
```

```python
import functools

import jax
import jax.numpy as jnp
from jax import lax
from jax.experimental import pallas as pl
from jax.experimental.pallas import tpu as pltpu
from jax.sharding import PartitionSpec as P

BF = jnp.bfloat16
F32 = jnp.float32
ROOM = 8 * 1024 * 1024
WIDE = 16 * 1024 * 1024
VMEM = pltpu.VMEM


def inner(left, right):
    return lax.dot_general(
        left, right, (((0,), (0,)), ((), ())), preferred_element_type=F32
    )


def outer(left, right):
    return lax.dot_general(
        left, right, (((1,), (1,)), ((), ())), preferred_element_type=F32
    )


def times(left, right):
    return jnp.dot(left, right, preferred_element_type=F32)


def swap(value, axis, masks):
    count = lax.axis_size(axis)
    pairs = [(i, i ^ masks[i % len(masks)]) for i in range(count)]
    return lax.ppermute(value, axis, pairs)


def like(rows, columns, kind):
    return jax.ShapeDtypeStruct((rows, columns), kind)


def whole(array):
    return pl.BlockSpec(array.shape, lambda n, s: (0,) * len(array.shape))


def run(
    body, outs, ins, after, numbers, in_specs=None, out_specs=None, scratch=(), room=ROOM, alias=None
):
    count, late = 1 + len(ins), len(after)

    def kernel(*refs):
        body(*refs[:count], *refs[count + late :])

    in_specs = in_specs or [None] * len(ins)
    out_specs = out_specs or [None] * len(outs)
    return pl.pallas_call(
        kernel,
        out_shape=tuple(outs),
        grid_spec=pltpu.PrefetchScalarGridSpec(
            num_scalar_prefetch=1,
            grid=(1,),
            in_specs=[s or whole(a) for s, a in zip(in_specs, ins)]
            + [pl.BlockSpec(memory_space=pl.ANY)] * late,
            out_specs=tuple(s or whole(a) for s, a in zip(out_specs, outs)),
            scratch_shapes=list(scratch),
        ),
        input_output_aliases=alias or {},
        compiler_params=pltpu.CompilerParams(vmem_limit_bytes=room),
        cost_estimate=pl.CostEstimate(flops=0, bytes_accessed=0, transcendentals=0),
    )(numbers, *ins, *after)


def sort_body(patch, part, own, numbers, grad, *blocks):
    size = own * part
    row = lax.broadcasted_iota(jnp.int32, (size, grad.shape[0]), 0)
    source = lax.broadcasted_iota(jnp.int32, (size, grad.shape[0]), 1)
    for m, block in enumerate(blocks):
        wanted = (row % part) * patch + numbers[m] * own + row // part
        block[...] = times((source == wanted).astype(BF), grad[...]).astype(BF)


def join_body(part, own, count, numbers, *refs):
    blocks, joined = refs[:-1], refs[-1]
    for m, block in enumerate(blocks):
        for j in range(own):
            start = pl.multiple_of((j * count + numbers[m]) * part, part)
            joined[pl.ds(start, part), :] = block[j * part : (j + 1) * part, :]


def sent_order(count):
    return sorted(range(count), key=lambda m: bin(m + count)[:2:-1])


def id_of(ids, place):
    lane = lax.broadcasted_iota(jnp.int32, ids.shape, 1)
    return jnp.sum(jnp.where(lane == place, ids[...] + 1, 0), axis=1, keepdims=True) - 1


def vocab_line(numbers, first, count, height):
    lane = lax.broadcasted_iota(jnp.int32, (1, count * height), 1)
    line = lane % height
    for n in range(count):
        line = line + jnp.where(lane // height == n, numbers[first + n] * height, 0)
    return line


def hot(ids, line):
    return jnp.where(ids == line, 1.0, 0.0).astype(BF)


def place_body(own, core_at, numbers, mine, other, both):
    patches, width = mine.shape[0], mine.shape[1] // own
    rows = own * patches
    for side, value in ((numbers[core_at], mine), (1 - numbers[core_at], other)):
        for j in range(own):
            start = pl.multiple_of(side * rows + j * patches, patches)
            both[pl.ds(start, patches), :] = value[:, j * width : (j + 1) * width]


def hots_body(own, tp_count, share_count, height, core_at, numbers, ids_own, ids_other, prev, here, mine):
    patches = ids_own.shape[0]
    plain = lax.broadcasted_iota(jnp.int32, (1, prev.shape[1]), 1)
    line = vocab_line(numbers, tp_count, share_count, height)
    both = vocab_line(numbers, tp_count, 2 * share_count, height)
    core = numbers[core_at]
    for side, ids in ((core, ids_own), (1 - core, ids_other)):
        for j in range(own):
            start = pl.multiple_of(side * own * patches + j * patches, patches)
            at = pl.ds(start, patches)
            before = id_of(ids, numbers[0] * own + j - 1)
            prev[at, :] = hot(before, plain)
            here[at, :] = hot(before, line)
            if ids is ids_own:
                wanted = id_of(ids, numbers[0] * own + j)
                mine[j * patches : (j + 1) * patches, :] = hot(wanted, both)


def pick_body(tp_count, share_count, first, numbers, up, down, up_here, down_here, ups, downs, ready):
    chunk = downs.shape[1]
    unit = chunk // tp_count
    copies = []
    for n in range(share_count):
        at = pl.ds(pl.multiple_of(numbers[first + n] * chunk, chunk), chunk)
        copies.append(
            (
                pltpu.make_async_copy(up.at[:, at], ups.at[n], ready.at[0, n]),
                pltpu.make_async_copy(down.at[at, :], downs.at[n], ready.at[1, n]),
            )
        )
        copies[-1][0].start()
        copies[-1][1].start()
    order = sent_order(tp_count)
    row = lax.broadcasted_iota(jnp.int32, (chunk, chunk), 0)
    column = lax.broadcasted_iota(jnp.int32, (chunk, chunk), 1)
    source = column % unit
    for i, m in enumerate(order):
        source = source + jnp.where(column // unit == i, numbers[m] * unit, 0)
    turn = (row == source).astype(BF)
    for n in range(share_count):
        copies[n][0].wait()
        copies[n][1].wait()
        at = n * chunk
        up_here[:, at : at + chunk] = times(ups[n], turn).astype(BF)
        for i, m in enumerate(order):
            start = pl.multiple_of(numbers[m] * unit, unit)
            down_here[at + i * unit : at + (i + 1) * unit, :] = downs[n, pl.ds(start, unit), :]


def split_body(tp_count, share, numbers, value, kept, sent):
    unit = share // tp_count
    order = sent_order(tp_count)
    half = tp_count // 2
    for n in range(value.shape[0] // share):
        for i, m in enumerate(order):
            at = pl.ds(n * share + pl.multiple_of(numbers[m] * unit, unit), unit)
            target = kept if i < half else sent
            row = (n * half + i % half) * unit
            target[row : row + unit, :] = value[at, :].astype(target.dtype)


def tables_in_body(
    share_count, first_share, height, numbers, glob, glob_more, local, gains, kept, sent
):
    width = glob.shape[1]
    strip = width // (2 * share_count)
    lane = lax.broadcasted_iota(jnp.int32, (16, width), 1)
    row = lax.broadcasted_iota(jnp.int32, (16, width), 0)
    both = glob[...].astype(F32) + glob_more[...].astype(F32)
    size = 2 * height + 16
    for n in range(share_count):
        target = kept if n < share_count // 2 else sent
        first = (n % (share_count // 2)) * size
        at = slice(n * height, (n + 1) * height)
        target[first : first + height, :] = both[at, :].astype(BF)
        target[first + height : first + 2 * height, :] = local[at, :].astype(BF)
        mine = (lane // strip == numbers[first_share + n]) & (row == 0)
        target[first + 2 * height : first + size, :] = jnp.where(mine, gains[...], 0.0).astype(BF)


def gate_body(numbers, value, same):
    pass


def add_body(numbers, kept, arrived, keep, send):
    half = keep.shape[0]
    keep[...] = (kept[:half, :].astype(F32) + arrived[:half, :].astype(F32)).astype(keep.dtype)
    send[...] = (kept[half:, :].astype(F32) + arrived[half:, :].astype(F32)).astype(send.dtype)


def sum_body(numbers, kept, arrived, summed):
    summed[...] = (kept[...].astype(F32) + arrived[...].astype(F32)).astype(summed.dtype)


def turned_body(numbers, kept, arrived, summed):
    summed[...] = (kept[...].astype(F32) + arrived[...].astype(F32)).T


def stack_body(numbers, first, second, both):
    rows = first.shape[0]
    both[:rows, :] = first[...]
    both[rows:, :] = second[...]


def tables_body(numbers, first, second, place, glob, local, gain):
    half = first.shape[0]
    vocab = glob.shape[0]
    row = lax.broadcasted_iota(jnp.int32, (vocab, half), 0)
    for which, target in enumerate((glob, local)):
        total = None
        for side, value in enumerate((first, second)):
            line = place[which : which + 1, side * half : (side + 1) * half]
            term = times(hot(row, line), value[...])
            total = term if total is None else total + term
        target[...] = total
    mark = place[2:10, :].astype(F32).astype(BF)
    gains = times(mark[:, :half], first[...]) + times(mark[:, half:], second[...])
    gain[...] = gains[:1, :]


def on_device(
    byte_ids,
    global_out,
    global_in_grad,
    out_grad,
    proj_weight,
    emb_local,
    norm_gain,
    up_weight,
    down_weight,
):
    seq_count = lax.axis_size("seq")
    tp_count = lax.axis_size("tp")
    seq_place = lax.axis_index("seq")
    tp_place = lax.axis_index("tp")
    core = seq_place & 1
    chip = seq_place >> 1
    stages = seq_count.bit_length() - 2
    levels = tp_count.bit_length() - 1
    share_count = 1 << stages
    walks = (list(range(1, stages + 1)), list(range(stages, 0, -1)))
    patches, patch = byte_ids.shape
    slot, width = proj_weight.shape
    hidden = up_weight.shape[1]
    vocab = emb_local.shape[0]
    own = patch // tp_count
    part = patches // tp_count
    rows = own * patches
    height = vocab // seq_count
    chunk = hidden // seq_count

    def share_mask(number, walk):
        mask = 0
        for k in range(stages):
            if (number >> (stages - 1 - k)) & 1:
                mask |= 1 << (walk[k] - 1)
        return mask

    def shares_of(which):
        return [
            2 * (chip ^ jnp.where(which == 0, share_mask(n, walks[0]), share_mask(n, walks[1])))
            + which
            for n in range(share_count)
        ]

    shares = shares_of(core)
    others = shares_of(1 - core)
    near = [tp_place ^ m for m in range(tp_count)]
    upward, downward = list(range(1, stages + 1)), list(range(stages, 0, -1))
    hidden_shares = [2 * (chip ^ share_mask(n, downward)) + core for n in range(share_count)]
    numbers = jnp.stack(near + shares + others + hidden_shares + [core]).astype(jnp.int32)
    core_at = tp_count + 3 * share_count
    call = functools.partial(run, numbers=numbers)

    def core_swap(value):
        return swap(value, "seq", (1,))

    def go(value, step):
        kind, k = step
        if kind == "seq":
            return swap(value, "seq", (1 << walks[0][k], 1 << walks[1][k]))
        if kind == "both":
            return swap(value, "seq", (1 << k,))
        return swap(value, "tp", (1 << k,))

    def gate(value, after):
        there = pl.BlockSpec(memory_space=pl.ANY)
        (value,) = call(
            gate_body,
            [like(*value.shape, value.dtype)],
            [value],
            after,
            in_specs=[there],
            out_specs=[there],
            alias={1: 0},
        )
        return value

    ids_other = core_swap(byte_ids)
    out_other = core_swap(global_out)
    blocks = call(
        functools.partial(sort_body, patch, part, own),
        [like(own * part, width, BF)] * tp_count,
        [out_grad],
        [],
    )
    blocks = [swap(b, "tp", (m,)) if m else b for m, b in enumerate(blocks)]
    there = pl.BlockSpec(memory_space=pl.ANY)
    half = hidden // 4
    up_here, down_here = call(
        functools.partial(pick_body, tp_count, share_count, tp_count + 2 * share_count),
        [like(width, hidden // 2, BF), like(hidden // 2, width, BF)],
        [up_weight, down_weight],
        [blocks[0]],
        in_specs=[there, there],
        scratch=[
            VMEM((share_count, width, chunk), BF),
            VMEM((share_count, chunk, width), BF),
            pltpu.SemaphoreType.DMA((2, share_count)),
        ],
        room=WIDE,
    )
    prev_hot, prev_here, own_hot = call(
        functools.partial(hots_body, own, tp_count, share_count, height, core_at),
        [like(2 * rows, vocab, BF), like(2 * rows, vocab // 2, BF), like(rows, vocab, BF)],
        [byte_ids, ids_other],
        [up_here],
    )

    def by_slot(value):
        return [value[:, j * slot : (j + 1) * slot] for j in range(own)]

    (slot_in,) = call(
        functools.partial(place_body, own, core_at),
        [like(2 * rows, slot, BF)],
        [global_out, out_other],
        [prev_hot],
    )
    u_rows = times(slot_in, proj_weight) + times(prev_hot, emb_local)
    scale = lax.rsqrt(jnp.mean(u_rows * u_rows, axis=1, keepdims=True) + 1e-05)
    normed = u_rows * scale
    r_rows = (normed * norm_gain).astype(BF)
    a_rows = times(r_rows, up_here)
    sig = jax.nn.sigmoid(a_rows)
    h_rows = (a_rows * sig).astype(BF)
    h_rows = lax.optimization_barrier(h_rows)
    order = sent_order(share_count)
    h_rows = jnp.concatenate([h_rows[:, n * chunk : (n + 1) * chunk] for n in order], axis=1)

    glob = [
        inner(own_hot[j * patches : (j + 1) * patches], value)
        for j, value in enumerate(by_slot(global_in_grad))
    ]
    glob = sum(glob[1:], glob[0])
    glob_sent = glob[vocab // 2 :].astype(BF)
    glob_kept = glob[: vocab // 2].astype(BF)
    glob_more = core_swap(glob_sent)

    (grad_own,) = call(
        functools.partial(join_body, part, own, tp_count),
        [like(rows, width, BF)],
        blocks,
        [h_rows, glob_kept],
    )
    (out_rows,) = call(
        functools.partial(place_body, 1, core_at),
        [like(2 * rows, width, BF)],
        [grad_own, core_swap(grad_own)],
        [],
    )

    seq_steps = [("seq", k) for k in range(stages)]
    tp_steps = [("tp", k) for k in range(levels)]

    class Chain:
        def __init__(self, kept, sent, steps, turned):
            self.kept, self.steps, self.turned, self.at = kept, steps, turned, 0
            self.arrived = go(sent, self.steps[0])
            self.left = len(self.steps)

        def next(self, after):
            self.at += 1
            self.left -= 1
            rows, columns = self.kept.shape
            ins = [self.kept, self.arrived]
            if self.left:
                outs = [like(rows // 2, columns, self.kept.dtype)] * 2
                self.kept, sent = call(add_body, outs, ins, after)
                self.arrived = go(sent, self.steps[self.at])
            elif self.turned:
                (self.kept,) = call(turned_body, [like(columns, rows, F32)], ins, after)
            else:
                (self.kept,) = call(sum_body, [like(rows, columns, F32)], ins, after)
            return self.kept

    class Table:
        def __init__(self, kept, sent):
            self.kept, self.at = kept, 0
            self.plan = (
                [("half", s) for s in seq_steps]
                + [("sum", s) for s in tp_steps]
                + [("join", s) for s in reversed(seq_steps)]
                + [("join", None)]
            )
            self.left = len(self.plan) - 1
            self.arrived = go(sent, self.plan[0][1])

        def next(self, after):
            last, (kind, step) = self.plan[self.at][0], self.plan[self.at + 1]
            rows, columns = self.kept.shape
            ins = [self.kept, self.arrived]
            if last == "half" and kind == "half":
                self.kept, sent = call(add_body, [like(rows // 2, columns, BF)] * 2, ins, after)
            elif last == "join":
                (self.kept,) = call(stack_body, [like(2 * rows, columns, BF)], ins, after)
                sent = self.kept
            else:
                (self.kept,) = call(sum_body, [like(rows, columns, BF)], ins, after)
                sent = self.kept
            self.at += 1
            self.left -= 1
            self.arrived = core_swap(sent) if step is None else go(sent, step)
            return self.kept

    dh_rows = outer(out_rows, down_here)
    da_rows = (dh_rows * sig * (1.0 + a_rows * (1.0 - sig))).astype(BF)
    dr_part = outer(da_rows, up_here)
    dr_sent = dr_part.astype(BF)
    kind = BF if chunk // tp_count % 16 == 0 else F32
    half = h_rows.shape[1] // 2
    down_kept = inner(h_rows[:, :half], out_rows).astype(kind)
    down_sent = inner(h_rows[:, half:], out_rows).astype(kind)
    up_kept = inner(da_rows[:, :half], r_rows).astype(kind)
    up_sent = inner(da_rows[:, half:], r_rows).astype(kind)
    down = Chain(down_kept, down_sent, [("both", k) for k in upward] + tp_steps, False)
    up = Chain(up_kept, up_sent, [("both", k) for k in downward] + tp_steps, True)
    dr_more = gate(core_swap(dr_sent), [down_sent, up_sent])
    dr_rows = dr_part + dr_more.astype(F32)

    gain_part = jnp.sum(dr_rows * normed, axis=0, keepdims=True)
    dn_rows = dr_rows * norm_gain
    du_rows = (
        out_rows.astype(F32)
        + scale * (dn_rows - normed * jnp.mean(dn_rows * normed, axis=1, keepdims=True))
    ).astype(BF)
    size = 2 * height + 16
    kept, sent = call(
        functools.partial(tables_in_body, share_count, tp_count, height),
        [like(share_count // 2 * size, width, BF)] * 2,
        [glob_kept, glob_more, inner(prev_here, du_rows), gain_part],
        [up.kept],
    )
    table = Table(kept, sent)
    share = width // seq_count
    kind = BF if share // tp_count % 16 == 0 else F32
    du_here = jnp.concatenate(
        [lax.dynamic_slice_in_dim(du_rows, s * share, share, 1) for s in shares], axis=1
    )
    value = inner(du_here, slot_in)
    kept, sent = call(
        functools.partial(split_body, tp_count, share),
        [like(value.shape[0] // 2, slot, kind)] * 2,
        [value],
        [table.kept],
    )
    proj = Chain(kept, sent, tp_steps[:1] + seq_steps + tp_steps[1:], True)
    du_own = lax.dynamic_slice_in_dim(du_rows, core * rows, rows, 0)
    back = outer(du_own, proj_weight).astype(BF)
    glob_out_grad = jnp.concatenate(
        [back[j * patches : (j + 1) * patches] for j in range(own)], axis=1
    )

    last = [up.kept, proj.kept, table.kept, down.kept, glob_out_grad]
    queue = [
        table, proj, down, up, table, proj, table, down, up, proj, table, down, up, proj,
        table, down, up, table,
    ]
    for chain in queue + [table, proj, down, up] * 16:
        if chain.left:
            last = [chain.next(last)]

    all_numbers = jnp.stack(shares + others)
    inside = jnp.arange(size)[None, :]
    own_row = all_numbers[:, None] * height + inside
    place = jnp.stack(
        [
            jnp.where(inside < height, own_row, -1).reshape(-1),
            jnp.where(
                (inside >= height) & (inside < 2 * height), own_row - height, -1
            ).reshape(-1),
        ]
        + [jnp.broadcast_to(inside == 2 * height, own_row.shape).reshape(-1).astype(jnp.int32)] * 8
    ).astype(jnp.int32)
    emb_global_grad, emb_local_grad, gain_grad = call(
        tables_body,
        [like(vocab, width, F32), like(vocab, width, F32), like(1, width, F32)],
        [table.kept, table.arrived, place],
        last,
    )
    return (
        glob_out_grad,
        emb_global_grad,
        emb_local_grad,
        gain_grad.reshape(width),
        proj.kept,
        up.kept,
        down.kept,
    )


def solution(mesh):
    placed = (
        P("seq", None),
        P("seq", "tp"),
        P("seq", "tp"),
        P(("seq", "tp"), None),
        P(),
        P(),
        P(),
        P(),
        P(),
    )
    return jax.shard_map(
        on_device,
        mesh=mesh,
        in_specs=placed,
        out_specs=(
            P("seq", "tp"),
            P(),
            P(),
            P(),
            P(None, ("seq", "tp")),
            P(None, ("seq", "tp")),
            P(("seq", "tp"), None),
        ),
        check_vma=False,
    )
```

```python
import functools

import jax
import jax.numpy as jnp
from jax import lax
from jax.experimental import pallas as pl
from jax.experimental.pallas import tpu as pltpu
from jax.sharding import PartitionSpec as P

BF = jnp.bfloat16
F32 = jnp.float32
ROOM = 8 * 1024 * 1024
WIDE = 16 * 1024 * 1024
VMEM = pltpu.VMEM


def inner(left, right):
    return lax.dot_general(
        left, right, (((0,), (0,)), ((), ())), preferred_element_type=F32
    )


def outer(left, right):
    return lax.dot_general(
        left, right, (((1,), (1,)), ((), ())), preferred_element_type=F32
    )


def times(left, right):
    return jnp.dot(left, right, preferred_element_type=F32)


def swap(value, axis, masks):
    count = lax.axis_size(axis)
    pairs = [(i, i ^ masks[i % len(masks)]) for i in range(count)]
    return lax.ppermute(value, axis, pairs)


def like(rows, columns, kind):
    return jax.ShapeDtypeStruct((rows, columns), kind)


def whole(array):
    return pl.BlockSpec(array.shape, lambda n, s: (0,) * len(array.shape))


def run(
    body, outs, ins, after, numbers, in_specs=None, out_specs=None, scratch=(), room=ROOM, alias=None
):
    count, late = 1 + len(ins), len(after)

    def kernel(*refs):
        body(*refs[:count], *refs[count + late :])

    in_specs = in_specs or [None] * len(ins)
    out_specs = out_specs or [None] * len(outs)
    return pl.pallas_call(
        kernel,
        out_shape=tuple(outs),
        grid_spec=pltpu.PrefetchScalarGridSpec(
            num_scalar_prefetch=1,
            grid=(1,),
            in_specs=[s or whole(a) for s, a in zip(in_specs, ins)]
            + [pl.BlockSpec(memory_space=pl.ANY)] * late,
            out_specs=tuple(s or whole(a) for s, a in zip(out_specs, outs)),
            scratch_shapes=list(scratch),
        ),
        input_output_aliases=alias or {},
        compiler_params=pltpu.CompilerParams(vmem_limit_bytes=room),
        cost_estimate=pl.CostEstimate(flops=0, bytes_accessed=0, transcendentals=0),
    )(numbers, *ins, *after)


def sort_body(patch, part, own, numbers, grad, *blocks):
    size = own * part
    row = lax.broadcasted_iota(jnp.int32, (size, grad.shape[0]), 0)
    source = lax.broadcasted_iota(jnp.int32, (size, grad.shape[0]), 1)
    for m, block in enumerate(blocks):
        wanted = (row % part) * patch + numbers[m] * own + row // part
        block[...] = times((source == wanted).astype(BF), grad[...]).astype(BF)


def join_body(part, own, count, numbers, *refs):
    blocks, joined = refs[:-1], refs[-1]
    for m, block in enumerate(blocks):
        for j in range(own):
            start = pl.multiple_of((j * count + numbers[m]) * part, part)
            joined[pl.ds(start, part), :] = block[j * part : (j + 1) * part, :]


def sent_order(count):
    return sorted(range(count), key=lambda m: bin(m + count)[:2:-1])


def id_of(ids, place):
    lane = lax.broadcasted_iota(jnp.int32, ids.shape, 1)
    return jnp.sum(jnp.where(lane == place, ids[...] + 1, 0), axis=1, keepdims=True) - 1


def vocab_line(numbers, first, count, height):
    lane = lax.broadcasted_iota(jnp.int32, (1, count * height), 1)
    line = lane % height
    for n in range(count):
        line = line + jnp.where(lane // height == n, numbers[first + n] * height, 0)
    return line


def hot(ids, line):
    return jnp.where(ids == line, 1.0, 0.0).astype(BF)


def place_body(own, core_at, numbers, mine, other, both):
    patches, width = mine.shape[0], mine.shape[1] // own
    rows = own * patches
    for side, value in ((numbers[core_at], mine), (1 - numbers[core_at], other)):
        for j in range(own):
            start = pl.multiple_of(side * rows + j * patches, patches)
            both[pl.ds(start, patches), :] = value[:, j * width : (j + 1) * width]


def hots_body(own, tp_count, share_count, height, core_at, numbers, ids_own, ids_other, prev, here, mine):
    patches = ids_own.shape[0]
    plain = lax.broadcasted_iota(jnp.int32, (1, prev.shape[1]), 1)
    line = vocab_line(numbers, tp_count, share_count, height)
    both = vocab_line(numbers, tp_count, 2 * share_count, height)
    core = numbers[core_at]
    for side, ids in ((core, ids_own), (1 - core, ids_other)):
        for j in range(own):
            start = pl.multiple_of(side * own * patches + j * patches, patches)
            at = pl.ds(start, patches)
            before = id_of(ids, numbers[0] * own + j - 1)
            prev[at, :] = hot(before, plain)
            here[at, :] = hot(before, line)
            if ids is ids_own:
                wanted = id_of(ids, numbers[0] * own + j)
                mine[j * patches : (j + 1) * patches, :] = hot(wanted, both)


def turn_matrix(tp_count, chunk, numbers):
    unit = chunk // tp_count
    row = lax.broadcasted_iota(jnp.int32, (chunk, chunk), 0)
    column = lax.broadcasted_iota(jnp.int32, (chunk, chunk), 1)
    source = column % unit
    for i, m in enumerate(sent_order(tp_count)):
        source = source + jnp.where(column // unit == i, numbers[m] * unit, 0)
    return (row == source).astype(BF)


def pick_up_body(tp_count, share_count, numbers, up, up_here, ups, ready):
    chunk = ups.shape[2]
    half = chunk // 2
    copies = []
    for n in range(share_count):
        at = pl.ds(pl.multiple_of(numbers[tp_count + n] * chunk, chunk), chunk)
        copies.append(pltpu.make_async_copy(up.at[:, at], ups.at[n], ready.at[n]))
        copies[-1].start()
    turn = turn_matrix(tp_count, chunk, numbers)
    for n in range(share_count):
        copies[n].wait()
        value = times(ups[n], turn).astype(BF)
        for z in range(2):
            first = (z * share_count + n) * half
            up_here[:, first : first + half] = value[:, z * half : (z + 1) * half]


def pick_down_body(tp_count, share_count, numbers, down, down_here, downs, ready):
    chunk = downs.shape[1]
    unit = chunk // tp_count
    half = chunk // 2
    copies = []
    for n in range(share_count):
        at = pl.ds(pl.multiple_of(numbers[tp_count + n] * chunk, chunk), chunk)
        copies.append(pltpu.make_async_copy(down.at[at, :], downs.at[n], ready.at[n]))
        copies[-1].start()
    for n in range(share_count):
        copies[n].wait()
        for i, m in enumerate(sent_order(tp_count)):
            z, place = i // (tp_count // 2), i % (tp_count // 2)
            first = (z * share_count + n) * half + place * unit
            start = pl.multiple_of(numbers[m] * unit, unit)
            down_here[first : first + unit, :] = downs[n, pl.ds(start, unit), :]


def split_body(tp_count, share, numbers, value, kept, sent):
    unit = share // tp_count
    half = kept.shape[0]
    for n in range(value.shape[0] // share):
        for i, m in enumerate(sent_order(tp_count)):
            at = pl.ds(n * share + pl.multiple_of(numbers[m] * unit, unit), unit)
            place = n * share + i * unit
            target = kept if place < half else sent
            row = place % half
            target[row : row + unit, :] = value[at, :].astype(target.dtype)


def tables_in_body(
    share_count, first_share, height, numbers, glob, glob_more, local, gains, kept, sent
):
    width = glob.shape[1]
    strip = width // (2 * share_count)
    lane = lax.broadcasted_iota(jnp.int32, (16, width), 1)
    row = lax.broadcasted_iota(jnp.int32, (16, width), 0)
    both = glob[...].astype(F32) + glob_more[...].astype(F32)
    size = 2 * height + 16
    for n in range(share_count):
        target = kept if n < share_count // 2 else sent
        first = (n % (share_count // 2)) * size
        at = slice(n * height, (n + 1) * height)
        target[first : first + height, :] = both[at, :].astype(BF)
        target[first + height : first + 2 * height, :] = local[at, :].astype(BF)
        mine = (lane // strip == numbers[first_share + n]) & (row == 0)
        target[first + 2 * height : first + size, :] = jnp.where(mine, gains[...], 0.0).astype(BF)


def gate_body(numbers, value, same):
    pass


def add_body(numbers, kept, arrived, keep, send):
    half = keep.shape[0]
    keep[...] = (kept[:half, :].astype(F32) + arrived[:half, :].astype(F32)).astype(keep.dtype)
    send[...] = (kept[half:, :].astype(F32) + arrived[half:, :].astype(F32)).astype(send.dtype)


def sum_body(numbers, kept, arrived, summed):
    summed[...] = (kept[...].astype(F32) + arrived[...].astype(F32)).astype(summed.dtype)


def turned_body(numbers, kept, arrived, summed):
    summed[...] = (kept[...].astype(F32) + arrived[...].astype(F32)).T


def stack_body(numbers, first, second, both):
    rows = first.shape[0]
    both[:rows, :] = first[...]
    both[rows:, :] = second[...]


def tables_body(numbers, first, second, place, glob, local, gain):
    half = first.shape[0]
    vocab = glob.shape[0]
    row = lax.broadcasted_iota(jnp.int32, (vocab, half), 0)
    for which, target in enumerate((glob, local)):
        total = None
        for side, value in enumerate((first, second)):
            line = place[which : which + 1, side * half : (side + 1) * half]
            term = times(hot(row, line), value[...])
            total = term if total is None else total + term
        target[...] = total
    mark = place[2:10, :].astype(F32).astype(BF)
    gains = times(mark[:, :half], first[...]) + times(mark[:, half:], second[...])
    gain[...] = gains[:1, :]


def on_device(
    byte_ids,
    global_out,
    global_in_grad,
    out_grad,
    proj_weight,
    emb_local,
    norm_gain,
    up_weight,
    down_weight,
):
    seq_count = lax.axis_size("seq")
    tp_count = lax.axis_size("tp")
    seq_place = lax.axis_index("seq")
    tp_place = lax.axis_index("tp")
    core = seq_place & 1
    chip = seq_place >> 1
    stages = seq_count.bit_length() - 2
    levels = tp_count.bit_length() - 1
    share_count = 1 << stages
    walks = (list(range(1, stages + 1)), list(range(stages, 0, -1)))
    patches, patch = byte_ids.shape
    slot, width = proj_weight.shape
    hidden = up_weight.shape[1]
    vocab = emb_local.shape[0]
    own = patch // tp_count
    part = patches // tp_count
    rows = own * patches
    height = vocab // seq_count
    chunk = hidden // seq_count

    def share_mask(number, walk):
        mask = 0
        for k in range(stages):
            if (number >> (stages - 1 - k)) & 1:
                mask |= 1 << (walk[k] - 1)
        return mask

    def shares_of(which):
        return [
            2 * (chip ^ jnp.where(which == 0, share_mask(n, walks[0]), share_mask(n, walks[1])))
            + which
            for n in range(share_count)
        ]

    shares = shares_of(core)
    others = shares_of(1 - core)
    near = [tp_place ^ m for m in range(tp_count)]
    numbers = jnp.stack(near + shares + others + [core]).astype(jnp.int32)
    core_at = tp_count + 2 * share_count
    call = functools.partial(run, numbers=numbers)

    def core_swap(value):
        return swap(value, "seq", (1,))

    def go(value, step):
        kind, k = step
        if kind == "seq":
            return swap(value, "seq", (1 << walks[0][k], 1 << walks[1][k]))
        return swap(value, "tp", (1 << k,))

    def gate(value, after):
        there = pl.BlockSpec(memory_space=pl.ANY)
        (value,) = call(
            gate_body,
            [like(*value.shape, value.dtype)],
            [value],
            after,
            in_specs=[there],
            out_specs=[there],
            alias={1: 0},
        )
        return value

    ids_other = core_swap(byte_ids)
    out_other = core_swap(global_out)
    blocks = call(
        functools.partial(sort_body, patch, part, own),
        [like(own * part, width, BF)] * tp_count,
        [out_grad],
        [],
    )
    blocks = [swap(b, "tp", (m,)) if m else b for m, b in enumerate(blocks)]
    prev_hot, prev_here, own_hot = call(
        functools.partial(hots_body, own, tp_count, share_count, height, core_at),
        [like(2 * rows, vocab, BF), like(2 * rows, vocab // 2, BF), like(rows, vocab, BF)],
        [byte_ids, ids_other],
        [blocks[0]],
    )

    def by_slot(value):
        return [value[:, j * slot : (j + 1) * slot] for j in range(own)]

    (slot_in,) = call(
        functools.partial(place_body, own, core_at),
        [like(2 * rows, slot, BF)],
        [global_out, out_other],
        [prev_hot],
    )
    u_rows = times(slot_in, proj_weight) + times(prev_hot, emb_local)
    scale = lax.rsqrt(jnp.mean(u_rows * u_rows, axis=1, keepdims=True) + 1e-05)
    normed = u_rows * scale
    r_rows = (normed * norm_gain).astype(BF)
    far = pl.BlockSpec(memory_space=pltpu.HBM)
    (up_here,) = call(
        functools.partial(pick_up_body, tp_count, share_count),
        [like(width, hidden // 2, BF)],
        [up_weight],
        [r_rows],
        in_specs=[far],
        scratch=[VMEM((share_count, width, chunk), BF), pltpu.SemaphoreType.DMA((share_count,))],
    )
    a_rows = times(r_rows, up_here)
    sig = jax.nn.sigmoid(a_rows)
    h_rows = (a_rows * sig).astype(BF)
    h_rows = lax.optimization_barrier(h_rows)
    (down_here,) = call(
        functools.partial(pick_down_body, tp_count, share_count),
        [like(hidden // 2, width, BF)],
        [down_weight],
        [h_rows],
        in_specs=[far],
        scratch=[VMEM((share_count, chunk, width), BF), pltpu.SemaphoreType.DMA((share_count,))],
    )
    strip = chunk // 2
    h_rows = jnp.concatenate(
        [
            h_rows[:, (z * share_count + n) * strip : (z * share_count + n + 1) * strip]
            for n in range(share_count)
            for z in range(2)
        ],
        axis=1,
    )

    glob = [
        inner(own_hot[j * patches : (j + 1) * patches], value)
        for j, value in enumerate(by_slot(global_in_grad))
    ]
    glob = sum(glob[1:], glob[0])
    glob_sent = glob[vocab // 2 :].astype(BF)
    glob_kept = glob[: vocab // 2].astype(BF)
    glob_more = core_swap(glob_sent)

    (grad_own,) = call(
        functools.partial(join_body, part, own, tp_count),
        [like(rows, width, BF)],
        blocks,
        [h_rows, glob_kept, down_here],
    )
    (out_rows,) = call(
        functools.partial(place_body, 1, core_at),
        [like(2 * rows, width, BF)],
        [grad_own, core_swap(grad_own)],
        [],
    )

    seq_steps = [("seq", k) for k in range(stages)]
    tp_steps = [("tp", k) for k in range(levels)]

    class Chain:
        def __init__(self, kept, sent, steps, turned):
            self.kept, self.steps, self.turned, self.at = kept, steps, turned, 0
            self.arrived = go(sent, self.steps[0])
            self.left = len(self.steps)

        def next(self, after):
            self.at += 1
            self.left -= 1
            rows, columns = self.kept.shape
            ins = [self.kept, self.arrived]
            if self.left:
                outs = [like(rows // 2, columns, self.kept.dtype)] * 2
                self.kept, sent = call(add_body, outs, ins, after)
                self.arrived = go(sent, self.steps[self.at])
            elif self.turned:
                (self.kept,) = call(turned_body, [like(columns, rows, F32)], ins, after)
            else:
                (self.kept,) = call(sum_body, [like(rows, columns, F32)], ins, after)
            return self.kept

    class Table:
        def __init__(self, kept, sent):
            self.kept, self.at = kept, 0
            self.plan = (
                [("half", s) for s in seq_steps]
                + [("sum", s) for s in tp_steps]
                + [("join", s) for s in reversed(seq_steps)]
                + [("join", None)]
            )
            self.left = len(self.plan) - 1
            self.arrived = go(sent, self.plan[0][1])

        def next(self, after):
            last, (kind, step) = self.plan[self.at][0], self.plan[self.at + 1]
            rows, columns = self.kept.shape
            ins = [self.kept, self.arrived]
            if last == "half" and kind == "half":
                self.kept, sent = call(add_body, [like(rows // 2, columns, BF)] * 2, ins, after)
            elif last == "join":
                (self.kept,) = call(stack_body, [like(2 * rows, columns, BF)], ins, after)
                sent = self.kept
            else:
                (self.kept,) = call(sum_body, [like(rows, columns, BF)], ins, after)
                sent = self.kept
            self.at += 1
            self.left -= 1
            self.arrived = core_swap(sent) if step is None else go(sent, step)
            return self.kept

    dh_rows = outer(out_rows, down_here)
    da_rows = (dh_rows * sig * (1.0 + a_rows * (1.0 - sig))).astype(BF)
    dr_part = outer(da_rows, up_here)
    dr_sent = dr_part.astype(BF)
    kind = BF if chunk // tp_count % 16 == 0 else F32
    half = h_rows.shape[1] // 2
    down_kept = inner(h_rows[:, :half], out_rows).astype(kind)
    down_sent = inner(h_rows[:, half:], out_rows).astype(kind)
    up_kept = inner(da_rows[:, :half], r_rows).astype(kind)
    up_sent = inner(da_rows[:, half:], r_rows).astype(kind)
    down = Chain(down_kept, down_sent, seq_steps + tp_steps, False)
    up = Chain(up_kept, up_sent, tp_steps[:1] + seq_steps + tp_steps[1:], True)
    dr_more = gate(core_swap(dr_sent), [down_sent, up_sent])
    dr_rows = dr_part + dr_more.astype(F32)

    gain_part = jnp.sum(dr_rows * normed, axis=0, keepdims=True)
    dn_rows = dr_rows * norm_gain
    du_rows = (
        out_rows.astype(F32)
        + scale * (dn_rows - normed * jnp.mean(dn_rows * normed, axis=1, keepdims=True))
    ).astype(BF)
    size = 2 * height + 16
    kept, sent = call(
        functools.partial(tables_in_body, share_count, tp_count, height),
        [like(share_count // 2 * size, width, BF)] * 2,
        [glob_kept, glob_more, inner(prev_here, du_rows), gain_part],
        [up.kept],
    )
    table = Table(kept, sent)
    share = width // seq_count
    kind = BF if share // tp_count % 16 == 0 else F32
    du_here = jnp.concatenate(
        [lax.dynamic_slice_in_dim(du_rows, s * share, share, 1) for s in shares], axis=1
    )
    value = inner(du_here, slot_in)
    kept, sent = call(
        functools.partial(split_body, tp_count, share),
        [like(value.shape[0] // 2, slot, kind)] * 2,
        [value],
        [table.kept],
    )
    proj = Chain(kept, sent, seq_steps + tp_steps, True)
    du_own = lax.dynamic_slice_in_dim(du_rows, core * rows, rows, 0)
    back = outer(du_own, proj_weight).astype(BF)
    glob_out_grad = jnp.concatenate(
        [back[j * patches : (j + 1) * patches] for j in range(own)], axis=1
    )

    last = [up.kept, proj.kept, table.kept, down.kept, glob_out_grad]
    names = {"T": table, "D": down, "U": up, "P": proj}
    queue = [names[c] for c in "TDPTUTPUDTPUTDTUPTD"]
    for chain in queue + [table, proj, down, up] * 16:
        if chain.left:
            last = [chain.next(last)]

    all_numbers = jnp.stack(shares + others)
    inside = jnp.arange(size)[None, :]
    own_row = all_numbers[:, None] * height + inside
    place = jnp.stack(
        [
            jnp.where(inside < height, own_row, -1).reshape(-1),
            jnp.where(
                (inside >= height) & (inside < 2 * height), own_row - height, -1
            ).reshape(-1),
        ]
        + [jnp.broadcast_to(inside == 2 * height, own_row.shape).reshape(-1).astype(jnp.int32)] * 8
    ).astype(jnp.int32)
    emb_global_grad, emb_local_grad, gain_grad = call(
        tables_body,
        [like(vocab, width, F32), like(vocab, width, F32), like(1, width, F32)],
        [table.kept, table.arrived, place],
        last,
    )
    return (
        glob_out_grad,
        emb_global_grad,
        emb_local_grad,
        gain_grad.reshape(width),
        proj.kept,
        up.kept,
        down.kept,
    )


def solution(mesh):
    placed = (
        P("seq", None),
        P("seq", "tp"),
        P("seq", "tp"),
        P(("seq", "tp"), None),
        P(),
        P(),
        P(),
        P(),
        P(),
    )
    return jax.shard_map(
        on_device,
        mesh=mesh,
        in_specs=placed,
        out_specs=(
            P("seq", "tp"),
            P(),
            P(),
            P(),
            P(None, ("seq", "tp")),
            P(None, ("seq", "tp")),
            P(("seq", "tp"), None),
        ),
        check_vma=False,
    )
```

```python
import functools

import jax
import jax.numpy as jnp
from jax import lax
from jax.experimental import pallas as pl
from jax.experimental.pallas import tpu as pltpu
from jax.sharding import PartitionSpec as P

BF = jnp.bfloat16
F32 = jnp.float32
ROOM = 8 * 1024 * 1024
STEP = 6 * 1000 * 1000 * 1000
VMEM = pltpu.VMEM


def inner(left, right):
    return lax.dot_general(
        left, right, (((0,), (0,)), ((), ())), preferred_element_type=F32
    )


def outer(left, right):
    return lax.dot_general(
        left, right, (((1,), (1,)), ((), ())), preferred_element_type=F32
    )


def times(left, right):
    return jnp.dot(left, right, preferred_element_type=F32)


def swap(value, axis, masks):
    count = lax.axis_size(axis)
    pairs = [(i, i ^ masks[i % len(masks)]) for i in range(count)]
    return lax.ppermute(value, axis, pairs)


def like(rows, columns, kind):
    return jax.ShapeDtypeStruct((rows, columns), kind)


def whole(array):
    return pl.BlockSpec(array.shape, lambda n, s: (0,) * len(array.shape))


def run(
    body, outs, ins, after, numbers, in_specs=None, out_specs=None, scratch=(), room=ROOM,
    alias=None, flops=0, grid=1,
):
    count, late = 1 + len(ins), len(after)

    def kernel(*refs):
        body(*refs[:count], *refs[count + late :])

    in_specs = in_specs or [None] * len(ins)
    out_specs = out_specs or [None] * len(outs)
    return pl.pallas_call(
        kernel,
        out_shape=tuple(outs),
        grid_spec=pltpu.PrefetchScalarGridSpec(
            num_scalar_prefetch=1,
            grid=(grid,),
            in_specs=[s or whole(a) for s, a in zip(in_specs, ins)]
            + [pl.BlockSpec(memory_space=pl.ANY)] * late,
            out_specs=tuple(s or whole(a) for s, a in zip(out_specs, outs)),
            scratch_shapes=list(scratch),
        ),
        input_output_aliases=alias or {},
        compiler_params=pltpu.CompilerParams(vmem_limit_bytes=room),
        cost_estimate=pl.CostEstimate(flops=flops, bytes_accessed=0, transcendentals=0),
    )(numbers, *ins, *after)


def sort_body(patch, part, own, numbers, grad, *blocks):
    size = own * part
    row = lax.broadcasted_iota(jnp.int32, (size, grad.shape[0]), 0)
    source = lax.broadcasted_iota(jnp.int32, (size, grad.shape[0]), 1)
    for m, block in enumerate(blocks):
        wanted = (row % part) * patch + numbers[m] * own + row // part
        block[...] = times((source == wanted).astype(BF), grad[...]).astype(BF)


def join_body(part, own, count, numbers, *refs):
    blocks, joined = refs[:-1], refs[-1]
    for m, block in enumerate(blocks):
        for j in range(own):
            start = pl.multiple_of((j * count + numbers[m]) * part, part)
            joined[pl.ds(start, part), :] = block[j * part : (j + 1) * part, :]


def sent_order(count):
    return sorted(range(count), key=lambda m: bin(m + count)[:2:-1])


def id_of(ids, place):
    lane = lax.broadcasted_iota(jnp.int32, ids.shape, 1)
    return jnp.sum(jnp.where(lane == place, ids[...] + 1, 0), axis=1, keepdims=True) - 1


def vocab_line(numbers, first, count, height):
    lane = lax.broadcasted_iota(jnp.int32, (1, count * height), 1)
    line = lane % height
    for n in range(count):
        line = line + jnp.where(lane // height == n, numbers[first + n] * height, 0)
    return line


def hot(ids, line):
    return jnp.where(ids == line, 1.0, 0.0).astype(BF)


def place_body(own, core_at, numbers, mine, other, both):
    patches, width = mine.shape[0], mine.shape[1] // own
    rows = own * patches
    for side, value in ((numbers[core_at], mine), (1 - numbers[core_at], other)):
        for j in range(own):
            start = pl.multiple_of(side * rows + j * patches, patches)
            both[pl.ds(start, patches), :] = value[:, j * width : (j + 1) * width]


def hots_body(own, tp_count, share_count, height, core_at, numbers, ids_own, ids_other, prev, here, mine):
    patches = ids_own.shape[0]
    plain = lax.broadcasted_iota(jnp.int32, (1, prev.shape[1]), 1)
    line = vocab_line(numbers, tp_count, share_count, height)
    both = vocab_line(numbers, tp_count, 2 * share_count, height)
    core = numbers[core_at]
    for side, ids in ((core, ids_own), (1 - core, ids_other)):
        for j in range(own):
            start = pl.multiple_of(side * own * patches + j * patches, patches)
            at = pl.ds(start, patches)
            before = id_of(ids, numbers[0] * own + j - 1)
            prev[at, :] = hot(before, plain)
            here[at, :] = hot(before, line)
            if ids is ids_own:
                wanted = id_of(ids, numbers[0] * own + j)
                mine[j * patches : (j + 1) * patches, :] = hot(wanted, both)


def turn_matrix(tp_count, chunk, numbers):
    unit = chunk // tp_count
    row = lax.broadcasted_iota(jnp.int32, (chunk, chunk), 0)
    column = lax.broadcasted_iota(jnp.int32, (chunk, chunk), 1)
    source = column % unit
    for i, m in enumerate(sent_order(tp_count)):
        source = source + jnp.where(column // unit == i, numbers[m] * unit, 0)
    return (row == source).astype(BF)


def pick_up_body(tp_count, share_count, numbers, up, up_here, ups, ready):
    chunk = ups.shape[2]
    half = chunk // 2
    copies = []
    for n in range(share_count):
        at = pl.ds(pl.multiple_of(numbers[tp_count + n] * chunk, chunk), chunk)
        copies.append(pltpu.make_async_copy(up.at[:, at], ups.at[n], ready.at[n]))
        copies[-1].start()
    turn = turn_matrix(tp_count, chunk, numbers)
    for n in range(share_count):
        copies[n].wait()
        value = times(ups[n], turn).astype(BF)
        for z in range(2):
            first = (z * share_count + n) * half
            up_here[:, first : first + half] = value[:, z * half : (z + 1) * half]


def pick_down_body(tp_count, share_count, numbers, down, down_here, downs, ready):
    chunk = downs.shape[1]
    unit = chunk // tp_count
    half = chunk // 2
    copies = []
    for n in range(share_count):
        at = pl.ds(pl.multiple_of(numbers[tp_count + n] * chunk, chunk), chunk)
        copies.append(pltpu.make_async_copy(down.at[at, :], downs.at[n], ready.at[n]))
        copies[-1].start()
    for n in range(share_count):
        copies[n].wait()
        for i, m in enumerate(sent_order(tp_count)):
            z, place = i // (tp_count // 2), i % (tp_count // 2)
            first = (z * share_count + n) * half + place * unit
            start = pl.multiple_of(numbers[m] * unit, unit)
            down_here[first : first + unit, :] = downs[n, pl.ds(start, unit), :]


def split_body(tp_count, share, numbers, value, kept, sent):
    unit = share // tp_count
    half = kept.shape[0]
    for n in range(value.shape[0] // share):
        for i, m in enumerate(sent_order(tp_count)):
            at = pl.ds(n * share + pl.multiple_of(numbers[m] * unit, unit), unit)
            place = n * share + i * unit
            target = kept if place < half else sent
            row = place % half
            target[row : row + unit, :] = value[at, :].astype(target.dtype)


def tables_in_body(
    share_count, first_share, height, numbers, glob, glob_more, local, gains, kept, sent
):
    width = glob.shape[1]
    strip = width // (2 * share_count)
    lane = lax.broadcasted_iota(jnp.int32, (16, width), 1)
    row = lax.broadcasted_iota(jnp.int32, (16, width), 0)
    both = glob[...].astype(F32) + glob_more[...].astype(F32)
    size = 2 * height + 16
    for n in range(share_count):
        target = kept if n < share_count // 2 else sent
        first = (n % (share_count // 2)) * size
        at = slice(n * height, (n + 1) * height)
        target[first : first + height, :] = both[at, :].astype(BF)
        target[first + height : first + 2 * height, :] = local[at, :].astype(BF)
        mine = (lane // strip == numbers[first_share + n]) & (row == 0)
        target[first + 2 * height : first + size, :] = jnp.where(mine, gains[...], 0.0).astype(BF)


def gate_body(numbers, value, same):
    pass


def add_body(numbers, kept, arrived, keep, send):
    half = keep.shape[0]
    keep[...] = (kept[:half, :].astype(F32) + arrived[:half, :].astype(F32)).astype(keep.dtype)
    send[...] = (kept[half:, :].astype(F32) + arrived[half:, :].astype(F32)).astype(send.dtype)


def sum_body(numbers, kept, arrived, summed):
    summed[...] = (kept[...].astype(F32) + arrived[...].astype(F32)).astype(summed.dtype)


def turned_body(numbers, kept, arrived, summed):
    summed[...] = (kept[...].astype(F32) + arrived[...].astype(F32)).T


def stack_body(numbers, first, second, both):
    rows = first.shape[0]
    both[:rows, :] = first[...]
    both[rows:, :] = second[...]


def tables_body(numbers, first, second, place, glob, local, gain, sort):
    half = first.shape[0]
    vocab = glob.shape[0]

    @pl.when(pl.program_id(0) == 0)
    def _():
        row = lax.broadcasted_iota(jnp.int32, (vocab, 2 * half), 0)
        sort[:vocab, :] = hot(row, place[:1, :])
        sort[vocab : 2 * vocab, :] = hot(row, place[1:2, :])
        sort[2 * vocab :, :] = place[2:, :].astype(F32).astype(BF)

    value = times(sort[:, :half], first[...]) + times(sort[:, half:], second[...])
    glob[...] = value[:vocab]
    local[...] = value[vocab : 2 * vocab]
    gain[...] = value[2 * vocab : 2 * vocab + 1]


def on_device(
    byte_ids,
    global_out,
    global_in_grad,
    out_grad,
    proj_weight,
    emb_local,
    norm_gain,
    up_weight,
    down_weight,
):
    seq_count = lax.axis_size("seq")
    tp_count = lax.axis_size("tp")
    seq_place = lax.axis_index("seq")
    tp_place = lax.axis_index("tp")
    core = seq_place & 1
    chip = seq_place >> 1
    stages = seq_count.bit_length() - 2
    levels = tp_count.bit_length() - 1
    share_count = 1 << stages
    walks = (list(range(1, stages + 1)), list(range(stages, 0, -1)))
    patches, patch = byte_ids.shape
    slot, width = proj_weight.shape
    hidden = up_weight.shape[1]
    vocab = emb_local.shape[0]
    own = patch // tp_count
    part = patches // tp_count
    rows = own * patches
    height = vocab // seq_count
    chunk = hidden // seq_count

    def share_mask(number, walk):
        mask = 0
        for k in range(stages):
            if (number >> (stages - 1 - k)) & 1:
                mask |= 1 << (walk[k] - 1)
        return mask

    def shares_of(which):
        return [
            2 * (chip ^ jnp.where(which == 0, share_mask(n, walks[0]), share_mask(n, walks[1])))
            + which
            for n in range(share_count)
        ]

    shares = shares_of(core)
    others = shares_of(1 - core)
    near = [tp_place ^ m for m in range(tp_count)]
    numbers = jnp.stack(near + shares + others + [core]).astype(jnp.int32)
    core_at = tp_count + 2 * share_count
    call = functools.partial(run, numbers=numbers)

    def core_swap(value):
        return swap(value, "seq", (1,))

    def go(value, step):
        kind, k = step
        if kind == "seq":
            return swap(value, "seq", (1 << walks[0][k], 1 << walks[1][k]))
        return swap(value, "tp", (1 << k,))

    def gate(value, after):
        there = pl.BlockSpec(memory_space=pl.ANY)
        (value,) = call(
            gate_body,
            [like(*value.shape, value.dtype)],
            [value],
            after,
            in_specs=[there],
            out_specs=[there],
            alias={1: 0},
        )
        return value

    ids_other = core_swap(byte_ids)
    out_other = core_swap(global_out)
    blocks = call(
        functools.partial(sort_body, patch, part, own),
        [like(own * part, width, BF)] * tp_count,
        [out_grad],
        [],
    )
    blocks = [swap(b, "tp", (m,)) if m else b for m, b in enumerate(blocks)]
    prev_hot, prev_here, own_hot = call(
        functools.partial(hots_body, own, tp_count, share_count, height, core_at),
        [like(2 * rows, vocab, BF), like(2 * rows, vocab // 2, BF), like(rows, vocab, BF)],
        [byte_ids, ids_other],
        [blocks[0]],
    )

    def by_slot(value):
        return [value[:, j * slot : (j + 1) * slot] for j in range(own)]

    (slot_in,) = call(
        functools.partial(place_body, own, core_at),
        [like(2 * rows, slot, BF)],
        [global_out, out_other],
        [prev_hot],
    )
    u_rows = times(slot_in, proj_weight) + times(prev_hot, emb_local)
    scale = lax.rsqrt(jnp.mean(u_rows * u_rows, axis=1, keepdims=True) + 1e-05)
    normed = u_rows * scale
    r_rows = (normed * norm_gain).astype(BF)
    far = pl.BlockSpec(memory_space=pltpu.HBM)
    (up_here,) = call(
        functools.partial(pick_up_body, tp_count, share_count),
        [like(width, hidden // 2, BF)],
        [up_weight],
        [r_rows],
        in_specs=[far],
        scratch=[VMEM((share_count, width, chunk), BF), pltpu.SemaphoreType.DMA((share_count,))],
    )
    a_rows = times(r_rows, up_here)
    sig = jax.nn.sigmoid(a_rows)
    h_rows = (a_rows * sig).astype(BF)
    slope = (sig * (1.0 + a_rows * (1.0 - sig))).astype(BF)
    h_rows, slope = lax.optimization_barrier((h_rows, slope))
    (down_here,) = call(
        functools.partial(pick_down_body, tp_count, share_count),
        [like(hidden // 2, width, BF)],
        [down_weight],
        [h_rows],
        in_specs=[far],
        scratch=[VMEM((share_count, chunk, width), BF), pltpu.SemaphoreType.DMA((share_count,))],
    )
    strip = chunk // 2
    h_rows = jnp.concatenate(
        [
            h_rows[:, (z * share_count + n) * strip : (z * share_count + n + 1) * strip]
            for n in range(share_count)
            for z in range(2)
        ],
        axis=1,
    )

    (grad_own,) = call(
        functools.partial(join_body, part, own, tp_count),
        [like(rows, width, BF)],
        blocks,
        [h_rows, down_here],
    )
    grad_other = core_swap(grad_own)
    own_hot = gate(own_hot, [grad_own])
    glob = [
        inner(own_hot[j * patches : (j + 1) * patches], value)
        for j, value in enumerate(by_slot(global_in_grad))
    ]
    glob = sum(glob[1:], glob[0])
    glob_sent = glob[vocab // 2 :].astype(BF)
    glob_kept = glob[: vocab // 2].astype(BF)
    glob_more = core_swap(glob_sent)

    (out_rows,) = call(
        functools.partial(place_body, 1, core_at),
        [like(2 * rows, width, BF)],
        [grad_own, grad_other],
        [glob_kept],
    )

    seq_steps = [("seq", k) for k in range(stages)]
    tp_steps = [("tp", k) for k in range(levels)]

    step = functools.partial(call, flops=STEP)

    class Chain:
        def __init__(self, kept, sent, steps, turned):
            self.kept, self.steps, self.turned, self.at = kept, steps, turned, 0
            self.arrived = go(sent, self.steps[0])
            self.left = len(self.steps)

        def next(self, after):
            self.at += 1
            self.left -= 1
            rows, columns = self.kept.shape
            ins = [self.kept, self.arrived]
            if self.left:
                outs = [like(rows // 2, columns, self.kept.dtype)] * 2
                self.kept, sent = step(add_body, outs, ins, after)
                self.arrived = go(sent, self.steps[self.at])
            elif self.turned:
                (self.kept,) = step(turned_body, [like(columns, rows, F32)], ins, after)
            else:
                (self.kept,) = step(sum_body, [like(rows, columns, F32)], ins, after)
            return self.kept

    class Table:
        def __init__(self, kept, sent):
            self.kept, self.at = kept, 0
            self.plan = (
                [("half", s) for s in seq_steps]
                + [("sum", s) for s in tp_steps]
                + [("join", s) for s in reversed(seq_steps)]
                + [("join", None)]
            )
            self.left = len(self.plan) - 1
            self.arrived = go(sent, self.plan[0][1])

        def next(self, after):
            last, (kind, hop) = self.plan[self.at][0], self.plan[self.at + 1]
            rows, columns = self.kept.shape
            ins = [self.kept, self.arrived]
            if last == "half" and kind == "half":
                self.kept, sent = step(add_body, [like(rows // 2, columns, BF)] * 2, ins, after)
            elif last == "join":
                (self.kept,) = step(stack_body, [like(2 * rows, columns, BF)], ins, after)
                sent = self.kept
            else:
                (self.kept,) = step(sum_body, [like(rows, columns, BF)], ins, after)
                sent = self.kept
            self.at += 1
            self.left -= 1
            self.arrived = core_swap(sent) if hop is None else go(sent, hop)
            return self.kept

    dh_rows = outer(out_rows, down_here)
    da_rows = (dh_rows * slope.astype(F32)).astype(BF)
    dr_part = outer(da_rows, up_here)
    dr_sent = dr_part.astype(BF)
    kind = BF if chunk // tp_count % 16 == 0 else F32
    half = h_rows.shape[1] // 2
    down_kept = inner(h_rows[:, :half], out_rows).astype(kind)
    down_sent = inner(h_rows[:, half:], out_rows).astype(kind)
    up_kept = inner(da_rows[:, :half], r_rows).astype(kind)
    up_sent = inner(da_rows[:, half:], r_rows).astype(kind)
    down = Chain(down_kept, down_sent, seq_steps + tp_steps, False)
    up = Chain(up_kept, up_sent, tp_steps[:1] + seq_steps + tp_steps[1:], True)
    dr_more = gate(core_swap(dr_sent), [down_sent, up_sent])
    dr_rows = dr_part + dr_more.astype(F32)

    gain_part = jnp.sum(dr_rows * normed, axis=0, keepdims=True)
    dn_rows = dr_rows * norm_gain
    du_rows = (
        out_rows.astype(F32)
        + scale * (dn_rows - normed * jnp.mean(dn_rows * normed, axis=1, keepdims=True))
    ).astype(BF)
    size = 2 * height + 16
    kept, sent = call(
        functools.partial(tables_in_body, share_count, tp_count, height),
        [like(share_count // 2 * size, width, BF)] * 2,
        [glob_kept, glob_more, inner(prev_here, du_rows), gain_part],
        [up.kept],
    )
    table = Table(kept, sent)
    share = width // seq_count
    kind = BF if share // tp_count % 16 == 0 else F32
    du_here = jnp.concatenate(
        [lax.dynamic_slice_in_dim(du_rows, s * share, share, 1) for s in shares], axis=1
    )
    value = inner(du_here, slot_in)
    kept, sent = call(
        functools.partial(split_body, tp_count, share),
        [like(value.shape[0] // 2, slot, kind)] * 2,
        [value],
        [table.kept],
    )
    proj = Chain(kept, sent, seq_steps + tp_steps, True)
    du_own = lax.dynamic_slice_in_dim(du_rows, core * rows, rows, 0)
    back = outer(du_own, proj_weight).astype(BF)
    glob_out_grad = jnp.concatenate(
        [back[j * patches : (j + 1) * patches] for j in range(own)], axis=1
    )

    last = [up.kept, proj.kept, table.kept, down.kept, glob_out_grad]
    names = {"T": table, "D": down, "U": up, "P": proj}
    queue = [names[c] for c in "TDPTUTPUDTPUTDTUPTD"]
    for chain in queue + [table, proj, down, up] * 16:
        if chain.left:
            last = [chain.next(last)]

    all_numbers = jnp.stack(shares + others)
    inside = jnp.arange(size)[None, :]
    own_row = all_numbers[:, None] * height + inside
    place = jnp.stack(
        [
            jnp.where(inside < height, own_row, -1).reshape(-1),
            jnp.where(
                (inside >= height) & (inside < 2 * height), own_row - height, -1
            ).reshape(-1),
        ]
        + [jnp.broadcast_to(inside == 2 * height, own_row.shape).reshape(-1).astype(jnp.int32)] * 16
    ).astype(jnp.int32)
    parts = 4
    wide = width // parts

    def columns(height):
        return pl.BlockSpec((height, wide), lambda n, s: (0, n))

    count = seq_count * size
    emb_global_grad, emb_local_grad, gain_grad = call(
        tables_body,
        [like(vocab, width, F32), like(vocab, width, F32), like(1, width, F32)],
        [table.kept, table.arrived, place],
        last,
        grid=parts,
        in_specs=[columns(count // 2), columns(count // 2), None],
        out_specs=[columns(vocab), columns(vocab), columns(1)],
        scratch=[VMEM((2 * vocab + 16, count), BF)],
    )
    return (
        glob_out_grad,
        emb_global_grad,
        emb_local_grad,
        gain_grad.reshape(width),
        proj.kept,
        up.kept,
        down.kept,
    )


def solution(mesh):
    placed = (
        P("seq", None),
        P("seq", "tp"),
        P("seq", "tp"),
        P(("seq", "tp"), None),
        P(),
        P(),
        P(),
        P(),
        P(),
    )
    return jax.shard_map(
        on_device,
        mesh=mesh,
        in_specs=placed,
        out_specs=(
            P("seq", "tp"),
            P(),
            P(),
            P(),
            P(None, ("seq", "tp")),
            P(None, ("seq", "tp")),
            P(("seq", "tp"), None),
        ),
        check_vma=False,
    )
```

```python
import functools

import jax
import jax.numpy as jnp
from jax import lax
from jax.experimental import pallas as pl
from jax.experimental.pallas import tpu as pltpu
from jax.sharding import PartitionSpec as P

BF = jnp.bfloat16
F32 = jnp.float32
ROOM = 8 * 1024 * 1024
STEP = 6 * 1000 * 1000 * 1000
VMEM = pltpu.VMEM


def inner(left, right):
    return lax.dot_general(
        left, right, (((0,), (0,)), ((), ())), preferred_element_type=F32
    )


def outer(left, right):
    return lax.dot_general(
        left, right, (((1,), (1,)), ((), ())), preferred_element_type=F32
    )


def times(left, right):
    return jnp.dot(left, right, preferred_element_type=F32)


def swap(value, axis, masks):
    count = lax.axis_size(axis)
    pairs = [(i, i ^ masks[i % len(masks)]) for i in range(count)]
    return lax.ppermute(value, axis, pairs)


def like(rows, columns, kind):
    return jax.ShapeDtypeStruct((rows, columns), kind)


def whole(array):
    return pl.BlockSpec(array.shape, lambda n, s: (0,) * len(array.shape))


def run(
    body, outs, ins, after, numbers, in_specs=None, out_specs=None, scratch=(), room=ROOM,
    alias=None, flops=0, grid=1,
):
    count, late = 1 + len(ins), len(after)

    def kernel(*refs):
        body(*refs[:count], *refs[count + late :])

    in_specs = in_specs or [None] * len(ins)
    out_specs = out_specs or [None] * len(outs)
    return pl.pallas_call(
        kernel,
        out_shape=tuple(outs),
        grid_spec=pltpu.PrefetchScalarGridSpec(
            num_scalar_prefetch=1,
            grid=(grid,),
            in_specs=[s or whole(a) for s, a in zip(in_specs, ins)]
            + [pl.BlockSpec(memory_space=pl.ANY)] * late,
            out_specs=tuple(s or whole(a) for s, a in zip(out_specs, outs)),
            scratch_shapes=list(scratch),
        ),
        input_output_aliases=alias or {},
        compiler_params=pltpu.CompilerParams(vmem_limit_bytes=room),
        cost_estimate=pl.CostEstimate(flops=flops, bytes_accessed=0, transcendentals=0),
    )(numbers, *ins, *after)


def sort_body(patch, part, own, numbers, grad, *blocks):
    size = own * part
    row = lax.broadcasted_iota(jnp.int32, (size, grad.shape[0]), 0)
    source = lax.broadcasted_iota(jnp.int32, (size, grad.shape[0]), 1)
    for m, block in enumerate(blocks):
        wanted = (row % part) * patch + numbers[m] * own + row // part
        block[...] = times((source == wanted).astype(BF), grad[...]).astype(BF)


def join_body(part, own, count, numbers, *refs):
    blocks, joined = refs[:-1], refs[-1]
    for m, block in enumerate(blocks):
        for j in range(own):
            start = pl.multiple_of((j * count + numbers[m]) * part, part)
            joined[pl.ds(start, part), :] = block[j * part : (j + 1) * part, :]


def sent_order(count):
    return sorted(range(count), key=lambda m: bin(m + count)[:2:-1])


def id_of(ids, place):
    lane = lax.broadcasted_iota(jnp.int32, ids.shape, 1)
    return jnp.sum(jnp.where(lane == place, ids + 1, 0), axis=1, keepdims=True) - 1


def vocab_line(numbers, first, count, height):
    lane = lax.broadcasted_iota(jnp.int32, (1, count * height), 1)
    line = lane % height
    for n in range(count):
        line = line + jnp.where(lane // height == n, numbers[first + n] * height, 0)
    return line


def hot(ids, line):
    return jnp.where(ids == line, 1.0, 0.0).astype(BF)


def place_body(own, core_at, numbers, mine, other, both):
    patches, width = mine.shape[0], mine.shape[1] // own
    rows = own * patches
    for side, value in ((numbers[core_at], mine), (1 - numbers[core_at], other)):
        for j in range(own):
            start = pl.multiple_of(side * rows + j * patches, patches)
            both[pl.ds(start, patches), :] = value[:, j * width : (j + 1) * width]


def hots_body(own, tp_count, share_count, height, core_at, numbers, ids_own, ids_other, prev, here, mine):
    patches = ids_own.shape[1]
    plain = lax.broadcasted_iota(jnp.int32, (1, prev.shape[1]), 1)
    line = vocab_line(numbers, tp_count, share_count, height)
    both = vocab_line(numbers, tp_count, 2 * share_count, height)
    core = numbers[core_at]
    for side, which in ((core, ids_own), (1 - core, ids_other)):
        ids = which[...].T
        for j in range(own):
            start = pl.multiple_of(side * own * patches + j * patches, patches)
            at = pl.ds(start, patches)
            before = id_of(ids, numbers[0] * own + j - 1)
            prev[at, :] = hot(before, plain)
            here[at, :] = hot(before, line)
            if which is ids_own:
                wanted = id_of(ids, numbers[0] * own + j)
                mine[j * patches : (j + 1) * patches, :] = hot(wanted, both)


def turn_matrix(tp_count, chunk, numbers):
    unit = chunk // tp_count
    row = lax.broadcasted_iota(jnp.int32, (chunk, chunk), 0)
    column = lax.broadcasted_iota(jnp.int32, (chunk, chunk), 1)
    source = column % unit
    for i, m in enumerate(sent_order(tp_count)):
        source = source + jnp.where(column // unit == i, numbers[m] * unit, 0)
    return (row == source).astype(BF)


def pick_up_body(tp_count, share_count, numbers, up, up_here, ups, ready):
    chunk = ups.shape[2]
    half = chunk // 2
    copies = []
    for n in range(share_count):
        at = pl.ds(pl.multiple_of(numbers[tp_count + n] * chunk, chunk), chunk)
        copies.append(pltpu.make_async_copy(up.at[:, at], ups.at[n], ready.at[n]))
        copies[-1].start()
    turn = turn_matrix(tp_count, chunk, numbers)
    for n in range(share_count):
        copies[n].wait()
        value = times(ups[n], turn).astype(BF)
        for z in range(2):
            first = (z * share_count + n) * half
            up_here[:, first : first + half] = value[:, z * half : (z + 1) * half]


def pick_down_body(tp_count, share_count, numbers, down, down_here, downs, ready):
    chunk = downs.shape[1]
    unit = chunk // tp_count
    half = chunk // 2
    copies = []
    for n in range(share_count):
        at = pl.ds(pl.multiple_of(numbers[tp_count + n] * chunk, chunk), chunk)
        copies.append(pltpu.make_async_copy(down.at[at, :], downs.at[n], ready.at[n]))
        copies[-1].start()
    for n in range(share_count):
        copies[n].wait()
        for i, m in enumerate(sent_order(tp_count)):
            z, place = i // (tp_count // 2), i % (tp_count // 2)
            first = (z * share_count + n) * half + place * unit
            start = pl.multiple_of(numbers[m] * unit, unit)
            down_here[first : first + unit, :] = downs[n, pl.ds(start, unit), :]


def split_body(tp_count, share, numbers, value, kept, sent):
    unit = share // tp_count
    half = kept.shape[0]
    for n in range(value.shape[0] // share):
        for i, m in enumerate(sent_order(tp_count)):
            at = pl.ds(n * share + pl.multiple_of(numbers[m] * unit, unit), unit)
            place = n * share + i * unit
            target = kept if place < half else sent
            row = place % half
            target[row : row + unit, :] = value[at, :].astype(target.dtype)


def tables_in_body(
    share_count, first_share, height, numbers, glob, glob_more, local, gains, kept, sent
):
    width = glob.shape[1]
    strip = width // (2 * share_count)
    lines = width // 128
    lane = lax.broadcasted_iota(jnp.int32, (1, width), 1)
    both = glob[...].astype(F32) + glob_more[...].astype(F32)
    size = 2 * height
    kept[:, width:] = jnp.zeros((kept.shape[0], 128), BF)
    sent[:, width:] = jnp.zeros((sent.shape[0], 128), BF)
    for n in range(share_count):
        target = kept if n < share_count // 2 else sent
        first = (n % (share_count // 2)) * size
        at = slice(n * height, (n + 1) * height)
        target[first : first + height, :width] = both[at, :].astype(BF)
        target[first + height : first + size, :width] = local[at, :].astype(BF)
        mine = jnp.where(lane // strip == numbers[first_share + n], gains[...], 0.0)
        rows = [mine[:, i * 128 : (i + 1) * 128] for i in range(lines)]
        rows.append(jnp.zeros((16 - lines, 128), F32))
        target[first : first + 16, width:] = jnp.concatenate(rows, axis=0).astype(BF)


def gate_body(numbers, value, same):
    pass


def add_body(numbers, kept, arrived, keep, send):
    half = keep.shape[0]
    keep[...] = (kept[:half, :].astype(F32) + arrived[:half, :].astype(F32)).astype(keep.dtype)
    send[...] = (kept[half:, :].astype(F32) + arrived[half:, :].astype(F32)).astype(send.dtype)


def sum_body(numbers, kept, arrived, summed):
    summed[...] = (kept[...].astype(F32) + arrived[...].astype(F32)).astype(summed.dtype)


def stack_body(numbers, first, second, both):
    rows = first.shape[0]
    both[:rows, :] = first[...]
    both[rows:, :] = second[...]


def sort_out_body(numbers, place, sort):
    vocab = (sort.shape[0] - 16) // 2
    row = lax.broadcasted_iota(jnp.int32, (vocab, sort.shape[1]), 0)
    sort[:vocab, :] = hot(row, place[:1, :])
    sort[vocab : 2 * vocab, :] = hot(row, place[1:2, :])
    sort[2 * vocab :, :] = place[2:, :].astype(F32).astype(BF)


def tables_body(numbers, first, second, first_gain, second_gain, sort, glob, local, gain):
    half = first.shape[0]
    vocab = glob.shape[0]
    tall = sort[: 2 * vocab]
    value = times(tall[:, :half], first[...]) + times(tall[:, half:], second[...])
    glob[...] = value[:vocab]
    local[...] = value[vocab:]

    @pl.when(pl.program_id(0) == 0)
    def _():
        flat = sort[2 * vocab :]
        value = times(flat[:, :half], first_gain[...])
        value = value + times(flat[:, half:], second_gain[...])
        gain[...] = value[: gain.shape[0]]


def on_device(
    byte_ids,
    global_out,
    global_in_grad,
    out_grad,
    proj_weight,
    emb_local,
    norm_gain,
    up_weight,
    down_weight,
):
    seq_count = lax.axis_size("seq")
    tp_count = lax.axis_size("tp")
    seq_place = lax.axis_index("seq")
    tp_place = lax.axis_index("tp")
    core = seq_place & 1
    chip = seq_place >> 1
    stages = seq_count.bit_length() - 2
    levels = tp_count.bit_length() - 1
    share_count = 1 << stages
    walks = (list(range(1, stages + 1)), list(range(stages, 0, -1)))
    patches, patch = byte_ids.shape
    slot, width = proj_weight.shape
    hidden = up_weight.shape[1]
    vocab = emb_local.shape[0]
    own = patch // tp_count
    part = patches // tp_count
    rows = own * patches
    height = vocab // seq_count
    chunk = hidden // seq_count

    def share_mask(number, walk):
        mask = 0
        for k in range(stages):
            if (number >> (stages - 1 - k)) & 1:
                mask |= 1 << (walk[k] - 1)
        return mask

    def shares_of(which):
        return [
            2 * (chip ^ jnp.where(which == 0, share_mask(n, walks[0]), share_mask(n, walks[1])))
            + which
            for n in range(share_count)
        ]

    shares = shares_of(core)
    others = shares_of(1 - core)
    near = [tp_place ^ m for m in range(tp_count)]
    numbers = jnp.stack(near + shares + others + [core]).astype(jnp.int32)
    core_at = tp_count + 2 * share_count
    call = functools.partial(run, numbers=numbers)

    def core_swap(value):
        return swap(value, "seq", (1,))

    def go(value, step):
        kind, k = step
        if kind == "seq":
            return swap(value, "seq", (1 << walks[0][k], 1 << walks[1][k]))
        return swap(value, "tp", (1 << k,))

    def gate(value, after):
        there = pl.BlockSpec(memory_space=pl.ANY)
        (value,) = call(
            gate_body,
            [like(*value.shape, value.dtype)],
            [value],
            after,
            in_specs=[there],
            out_specs=[there],
            alias={1: 0},
        )
        return value

    ids_own = byte_ids.T
    ids_other = core_swap(ids_own)
    out_other = core_swap(global_out)
    blocks = call(
        functools.partial(sort_body, patch, part, own),
        [like(own * part, width, BF)] * tp_count,
        [out_grad],
        [],
    )
    blocks = [swap(b, "tp", (m,)) if m else b for m, b in enumerate(blocks)]
    prev_hot, prev_here, own_hot = call(
        functools.partial(hots_body, own, tp_count, share_count, height, core_at),
        [like(2 * rows, vocab, BF), like(2 * rows, vocab // 2, BF), like(rows, vocab, BF)],
        [ids_own, ids_other],
        [blocks[0]],
    )

    def by_slot(value):
        return [value[:, j * slot : (j + 1) * slot] for j in range(own)]

    (slot_in,) = call(
        functools.partial(place_body, own, core_at),
        [like(2 * rows, slot, BF)],
        [global_out, out_other],
        [prev_hot],
    )
    u_rows = times(slot_in, proj_weight) + times(prev_hot, emb_local)
    scale = lax.rsqrt(jnp.mean(u_rows * u_rows, axis=1, keepdims=True) + 1e-05)
    normed = u_rows * scale
    r_rows = (normed * norm_gain).astype(BF)
    far = pl.BlockSpec(memory_space=pltpu.HBM)
    (up_here,) = call(
        functools.partial(pick_up_body, tp_count, share_count),
        [like(width, hidden // 2, BF)],
        [up_weight],
        [r_rows],
        in_specs=[far],
        scratch=[VMEM((share_count, width, chunk), BF), pltpu.SemaphoreType.DMA((share_count,))],
    )
    a_rows = times(r_rows, up_here)
    sig = jax.nn.sigmoid(a_rows)
    h_rows = (a_rows * sig).astype(BF)
    slope = (sig * (1.0 + a_rows * (1.0 - sig))).astype(BF)
    h_rows, slope = lax.optimization_barrier((h_rows, slope))
    (down_here,) = call(
        functools.partial(pick_down_body, tp_count, share_count),
        [like(hidden // 2, width, BF)],
        [down_weight],
        [h_rows],
        in_specs=[far],
        scratch=[VMEM((share_count, chunk, width), BF), pltpu.SemaphoreType.DMA((share_count,))],
    )
    strip = chunk // 2
    h_rows = jnp.concatenate(
        [
            h_rows[:, (z * share_count + n) * strip : (z * share_count + n + 1) * strip]
            for n in range(share_count)
            for z in range(2)
        ],
        axis=1,
    )

    (grad_own,) = call(
        functools.partial(join_body, part, own, tp_count),
        [like(rows, width, BF)],
        blocks,
        [h_rows, down_here],
    )
    grad_other = core_swap(grad_own)
    own_hot = gate(own_hot, [grad_own])
    glob = [
        inner(own_hot[j * patches : (j + 1) * patches], value)
        for j, value in enumerate(by_slot(global_in_grad))
    ]
    glob = sum(glob[1:], glob[0])
    glob_sent = glob[vocab // 2 :].astype(BF)
    glob_kept = glob[: vocab // 2].astype(BF)
    glob_more = core_swap(glob_sent)

    (out_rows,) = call(
        functools.partial(place_body, 1, core_at),
        [like(2 * rows, width, BF)],
        [grad_own, grad_other],
        [glob_kept],
    )

    seq_steps = [("seq", k) for k in range(stages)]
    tp_steps = [("tp", k) for k in range(levels)]

    step = functools.partial(call, flops=STEP)

    class Chain:
        def __init__(self, kept, sent, steps):
            self.kept, self.steps, self.at = kept, steps, 0
            self.arrived = go(sent, self.steps[0])
            self.left = len(self.steps)

        def next(self, after):
            self.at += 1
            self.left -= 1
            rows, columns = self.kept.shape
            ins = [self.kept, self.arrived]
            if self.left:
                outs = [like(rows // 2, columns, self.kept.dtype)] * 2
                self.kept, sent = step(add_body, outs, ins, after)
                self.arrived = go(sent, self.steps[self.at])
            else:
                (self.kept,) = step(sum_body, [like(rows, columns, F32)], ins, after)
            return self.kept

    class Table:
        def __init__(self, kept, sent):
            self.kept, self.at = kept, 0
            self.plan = (
                [("half", s) for s in seq_steps]
                + [("sum", s) for s in tp_steps]
                + [("join", s) for s in reversed(seq_steps)]
                + [("join", None)]
            )
            self.left = len(self.plan) - 1
            self.arrived = go(sent, self.plan[0][1])

        def next(self, after):
            last, (kind, hop) = self.plan[self.at][0], self.plan[self.at + 1]
            rows, columns = self.kept.shape
            ins = [self.kept, self.arrived]
            if last == "half" and kind == "half":
                self.kept, sent = step(add_body, [like(rows // 2, columns, BF)] * 2, ins, after)
            elif last == "join":
                (self.kept,) = step(stack_body, [like(2 * rows, columns, BF)], ins, after)
                sent = self.kept
            else:
                (self.kept,) = step(sum_body, [like(rows, columns, BF)], ins, after)
                sent = self.kept
            self.at += 1
            self.left -= 1
            self.arrived = core_swap(sent) if hop is None else go(sent, hop)
            return self.kept

    dh_rows = outer(out_rows, down_here)
    da_rows = (dh_rows * slope.astype(F32)).astype(BF)
    dr_part = outer(da_rows, up_here)
    dr_sent = dr_part.astype(BF)
    kind = BF if chunk // tp_count % 16 == 0 else F32
    half = h_rows.shape[1] // 2
    down_kept = inner(h_rows[:, :half], out_rows).astype(kind)
    down_sent = inner(h_rows[:, half:], out_rows).astype(kind)
    up_kept = inner(da_rows[:, :half], r_rows).astype(kind)
    up_sent = inner(da_rows[:, half:], r_rows).astype(kind)
    down = Chain(down_kept, down_sent, seq_steps + tp_steps)
    up = Chain(up_kept, up_sent, tp_steps[:1] + seq_steps + tp_steps[1:])
    dr_more = gate(core_swap(dr_sent), [down_sent, up_sent])
    dr_rows = dr_part + dr_more.astype(F32)

    gain_part = jnp.sum(dr_rows * normed, axis=0, keepdims=True)
    dn_rows = dr_rows * norm_gain
    du_rows = (
        out_rows.astype(F32)
        + scale * (dn_rows - normed * jnp.mean(dn_rows * normed, axis=1, keepdims=True))
    ).astype(BF)
    size = 2 * height
    kept, sent = call(
        functools.partial(tables_in_body, share_count, tp_count, height),
        [like(share_count // 2 * size, width + 128, BF)] * 2,
        [glob_kept, glob_more, inner(prev_here, du_rows), gain_part],
        [up.kept],
    )
    table = Table(kept, sent)
    share = width // seq_count
    kind = BF if share // tp_count % 16 == 0 else F32
    du_here = jnp.concatenate(
        [lax.dynamic_slice_in_dim(du_rows, s * share, share, 1) for s in shares], axis=1
    )
    value = inner(du_here, slot_in)
    kept, sent = call(
        functools.partial(split_body, tp_count, share),
        [like(value.shape[0] // 2, slot, kind)] * 2,
        [value],
        [table.kept],
    )
    proj = Chain(kept, sent, seq_steps + tp_steps)
    du_own = lax.dynamic_slice_in_dim(du_rows, core * rows, rows, 0)
    back = outer(du_own, proj_weight).astype(BF)
    glob_out_grad = jnp.concatenate(
        [back[j * patches : (j + 1) * patches] for j in range(own)], axis=1
    )

    all_numbers = jnp.stack(shares + others)
    inside = jnp.arange(size)[None, :]
    own_row = all_numbers[:, None] * height + inside
    place = jnp.stack(
        [
            jnp.where(inside < height, own_row, -1).reshape(-1),
            jnp.where(inside >= height, own_row - height, -1).reshape(-1),
        ]
        + [
            jnp.broadcast_to(inside == line, own_row.shape).reshape(-1).astype(jnp.int32)
            for line in range(16)
        ]
    ).astype(jnp.int32)
    count = seq_count * size
    (sort,) = call(
        sort_out_body, [like(2 * vocab + 16, count, BF)], [place], [table.kept]
    )
    last = [up.kept, proj.kept, table.kept, down.kept, glob_out_grad, sort]
    names = {"T": table, "D": down, "U": up, "P": proj}
    queue = [names[c] for c in "TDTUTPDUPTUTPDTPUTD"]
    for chain in queue + [table, proj, down, up] * 16:
        if chain.left:
            last = [chain.next(last)]

    parts = 4
    wide = width // parts

    def columns(height):
        return pl.BlockSpec((height, wide), lambda n, s: (0, n))

    lines = width // 128
    beside = pl.BlockSpec((count // 2, 128), lambda n, s: (0, lines))
    emb_global_grad, emb_local_grad, gain_grad = call(
        tables_body,
        [like(vocab, width, F32), like(vocab, width, F32), like(lines, 128, F32)],
        [table.kept, table.arrived, table.kept, table.arrived, sort],
        last,
        grid=parts,
        in_specs=[columns(count // 2), columns(count // 2), beside, beside, None],
        out_specs=[columns(vocab), columns(vocab), None],
    )
    return (
        glob_out_grad,
        emb_global_grad,
        emb_local_grad,
        gain_grad.reshape(width),
        proj.kept.T,
        up.kept.T,
        down.kept,
    )


def solution(mesh):
    placed = (
        P("seq", None),
        P("seq", "tp"),
        P("seq", "tp"),
        P(("seq", "tp"), None),
        P(),
        P(),
        P(),
        P(),
        P(),
    )
    return jax.shard_map(
        on_device,
        mesh=mesh,
        in_specs=placed,
        out_specs=(
            P("seq", "tp"),
            P(),
            P(),
            P(),
            P(None, ("seq", "tp")),
            P(None, ("seq", "tp")),
            P(("seq", "tp"), None),
        ),
        check_vma=False,
    )
```

```python
import functools

import jax
import jax.numpy as jnp
from jax import lax
from jax.experimental import pallas as pl
from jax.experimental.pallas import tpu as pltpu
from jax.sharding import PartitionSpec as P

BF = jnp.bfloat16
F32 = jnp.float32
ROOM = 8 * 1024 * 1024
WIDE = 24 * 1024 * 1024
STEP = 6 * 1000 * 1000 * 1000
VMEM = pltpu.VMEM


def inner(left, right):
    return lax.dot_general(
        left, right, (((0,), (0,)), ((), ())), preferred_element_type=F32
    )


def outer(left, right):
    return lax.dot_general(
        left, right, (((1,), (1,)), ((), ())), preferred_element_type=F32
    )


def times(left, right):
    return jnp.dot(left, right, preferred_element_type=F32)


def swap(value, axis, masks):
    count = lax.axis_size(axis)
    pairs = [(i, i ^ masks[i % len(masks)]) for i in range(count)]
    return lax.ppermute(value, axis, pairs)


def like(rows, columns, kind):
    return jax.ShapeDtypeStruct((rows, columns), kind)


def whole(array):
    return pl.BlockSpec(array.shape, lambda n, s: (0,) * len(array.shape))


def run(
    body, outs, ins, after, numbers, in_specs=None, out_specs=None, scratch=(), room=ROOM,
    alias=None, flops=0, grid=1,
):
    count, late = 1 + len(ins), len(after)

    def kernel(*refs):
        body(*refs[:count], *refs[count + late :])

    in_specs = in_specs or [None] * len(ins)
    out_specs = out_specs or [None] * len(outs)
    return pl.pallas_call(
        kernel,
        out_shape=tuple(outs),
        grid_spec=pltpu.PrefetchScalarGridSpec(
            num_scalar_prefetch=1,
            grid=(grid,),
            in_specs=[s or whole(a) for s, a in zip(in_specs, ins)]
            + [pl.BlockSpec(memory_space=pl.ANY)] * late,
            out_specs=tuple(s or whole(a) for s, a in zip(out_specs, outs)),
            scratch_shapes=list(scratch),
        ),
        input_output_aliases=alias or {},
        compiler_params=pltpu.CompilerParams(vmem_limit_bytes=room),
        cost_estimate=pl.CostEstimate(flops=flops, bytes_accessed=0, transcendentals=0),
    )(numbers, *ins, *after)


def sort_body(patch, part, own, numbers, grad, *blocks):
    size = own * part
    row = lax.broadcasted_iota(jnp.int32, (size, grad.shape[0]), 0)
    source = lax.broadcasted_iota(jnp.int32, (size, grad.shape[0]), 1)
    for m, block in enumerate(blocks):
        wanted = (row % part) * patch + numbers[m] * own + row // part
        block[...] = times((source == wanted).astype(BF), grad[...]).astype(BF)


def join_body(part, own, count, numbers, *refs):
    blocks, joined = refs[:-1], refs[-1]
    for m, block in enumerate(blocks):
        for j in range(own):
            start = pl.multiple_of((j * count + numbers[m]) * part, part)
            joined[pl.ds(start, part), :] = block[j * part : (j + 1) * part, :]


def sent_order(count):
    return sorted(range(count), key=lambda m: bin(m + count)[:2:-1])


def id_of(ids, place):
    lane = lax.broadcasted_iota(jnp.int32, ids.shape, 1)
    return jnp.sum(jnp.where(lane == place, ids + 1, 0), axis=1, keepdims=True) - 1


def vocab_line(numbers, first, count, height):
    lane = lax.broadcasted_iota(jnp.int32, (1, count * height), 1)
    line = lane % height
    for n in range(count):
        line = line + jnp.where(lane // height == n, numbers[first + n] * height, 0)
    return line


def hot(ids, line):
    return jnp.where(ids == line, 1.0, 0.0).astype(BF)


def place_body(own, core_at, numbers, mine, other, both):
    patches, width = mine.shape[0], mine.shape[1] // own
    rows = own * patches
    for side, value in ((numbers[core_at], mine), (1 - numbers[core_at], other)):
        for j in range(own):
            start = pl.multiple_of(side * rows + j * patches, patches)
            both[pl.ds(start, patches), :] = value[:, j * width : (j + 1) * width]


def hots(own, tp_count, share_count, height, core_at, numbers, ids_own, ids_other, prev, here, mine):
    patches = ids_own.shape[1]
    plain = lax.broadcasted_iota(jnp.int32, (1, prev.shape[1]), 1)
    line = vocab_line(numbers, tp_count, share_count, height)
    both = vocab_line(numbers, tp_count, 2 * share_count, height)
    core = numbers[core_at]
    for side, which in ((core, ids_own), (1 - core, ids_other)):
        ids = which[...].T
        for j in range(own):
            start = pl.multiple_of(side * own * patches + j * patches, patches)
            at = pl.ds(start, patches)
            before = id_of(ids, numbers[0] * own + j - 1)
            prev[at, :] = hot(before, plain)
            here[at, :] = hot(before, line)
            if which is ids_own:
                wanted = id_of(ids, numbers[0] * own + j)
                mine[j * patches : (j + 1) * patches, :] = hot(wanted, both)


def turn_matrix(tp_count, chunk, numbers):
    unit = chunk // tp_count
    row = lax.broadcasted_iota(jnp.int32, (chunk, chunk), 0)
    column = lax.broadcasted_iota(jnp.int32, (chunk, chunk), 1)
    source = column % unit
    for i, m in enumerate(sent_order(tp_count)):
        source = source + jnp.where(column // unit == i, numbers[m] * unit, 0)
    return (row == source).astype(BF)


def prepare_body(
    own, tp_count, share_count, height, core_at,
    numbers, up, down, ids_own, ids_other,
    prev, here, mine, up_here, down_here, ups, downs, ready,
):
    chunk = ups.shape[2]
    unit = chunk // tp_count
    half = chunk // 2
    copies = []
    for n in range(share_count):
        at = pl.ds(pl.multiple_of(numbers[tp_count + n] * chunk, chunk), chunk)
        copies.append(pltpu.make_async_copy(up.at[:, at], ups.at[n], ready.at[0, n]))
        copies[-1].start()
    for n in range(share_count):
        at = pl.ds(pl.multiple_of(numbers[tp_count + n] * chunk, chunk), chunk)
        copies.append(pltpu.make_async_copy(down.at[at, :], downs.at[n], ready.at[1, n]))
        copies[-1].start()
    hots(
        own, tp_count, share_count, height, core_at, numbers, ids_own, ids_other, prev, here, mine
    )
    turn = turn_matrix(tp_count, chunk, numbers)
    for n in range(share_count):
        copies[n].wait()
        value = times(ups[n], turn).astype(BF)
        for z in range(2):
            first = (z * share_count + n) * half
            up_here[:, first : first + half] = value[:, z * half : (z + 1) * half]
    for n in range(share_count):
        copies[share_count + n].wait()
        for i, m in enumerate(sent_order(tp_count)):
            z, place = i // (tp_count // 2), i % (tp_count // 2)
            first = (z * share_count + n) * half + place * unit
            start = pl.multiple_of(numbers[m] * unit, unit)
            down_here[first : first + unit, :] = downs[n, pl.ds(start, unit), :]


def split_body(tp_count, share, numbers, value, kept, sent):
    unit = share // tp_count
    half = kept.shape[0]
    for n in range(value.shape[0] // share):
        for i, m in enumerate(sent_order(tp_count)):
            at = pl.ds(n * share + pl.multiple_of(numbers[m] * unit, unit), unit)
            place = n * share + i * unit
            target = kept if place < half else sent
            row = place % half
            target[row : row + unit, :] = value[at, :].astype(target.dtype)


def tables_in_body(
    share_count, first_share, height, numbers, glob, glob_more, local, gains, kept, sent
):
    width = glob.shape[1]
    strip = width // (2 * share_count)
    lines = width // 128
    lane = lax.broadcasted_iota(jnp.int32, (1, width), 1)
    both = glob[...].astype(F32) + glob_more[...].astype(F32)
    size = 2 * height
    kept[:, width:] = jnp.zeros((kept.shape[0], 128), BF)
    sent[:, width:] = jnp.zeros((sent.shape[0], 128), BF)
    for n in range(share_count):
        target = kept if n < share_count // 2 else sent
        first = (n % (share_count // 2)) * size
        at = slice(n * height, (n + 1) * height)
        target[first : first + height, :width] = both[at, :].astype(BF)
        target[first + height : first + size, :width] = local[at, :].astype(BF)
        mine = jnp.where(lane // strip == numbers[first_share + n], gains[...], 0.0)
        rows = [mine[:, i * 128 : (i + 1) * 128] for i in range(lines)]
        rows.append(jnp.zeros((16 - lines, 128), F32))
        target[first : first + 16, width:] = jnp.concatenate(rows, axis=0).astype(BF)


def gate_body(numbers, value, same):
    pass


def add_body(numbers, kept, arrived, keep, send):
    half = keep.shape[0]
    keep[...] = (kept[:half, :].astype(F32) + arrived[:half, :].astype(F32)).astype(keep.dtype)
    send[...] = (kept[half:, :].astype(F32) + arrived[half:, :].astype(F32)).astype(send.dtype)


def sum_body(numbers, kept, arrived, summed):
    summed[...] = (kept[...].astype(F32) + arrived[...].astype(F32)).astype(summed.dtype)


def stack_body(numbers, first, second, both):
    rows = first.shape[0]
    both[:rows, :] = first[...]
    both[rows:, :] = second[...]


def tables_body(
    share_count, first_share, height, numbers, first, second, first_gain, second_gain,
    glob, local, gain,
):
    gains = None
    for side, (value, line) in enumerate(((first, first_gain), (second, second_gain))):
        for n in range(share_count):
            start = numbers[first_share + side * share_count + n] * height
            at = pl.ds(pl.multiple_of(start, height), height)
            row = 2 * n * height
            glob[at, :] = value[row : row + height, :].astype(F32)
            local[at, :] = value[row + height : row + 2 * height, :].astype(F32)
            term = line[row : row + 16, :].astype(F32)
            gains = term if gains is None else gains + term
    gain[...] = gains[: gain.shape[0]]


def finals_body(numbers, *refs):
    for i in range(len(refs) // 3):
        kept, arrived, whole = refs[2 * i], refs[2 * i + 1], refs[len(refs) // 3 * 2 + i]
        whole[...] = kept[...].astype(F32) + arrived[...].astype(F32)


def on_device(
    byte_ids,
    global_out,
    global_in_grad,
    out_grad,
    proj_weight,
    emb_local,
    norm_gain,
    up_weight,
    down_weight,
):
    seq_count = lax.axis_size("seq")
    tp_count = lax.axis_size("tp")
    seq_place = lax.axis_index("seq")
    tp_place = lax.axis_index("tp")
    core = seq_place & 1
    chip = seq_place >> 1
    stages = seq_count.bit_length() - 2
    levels = tp_count.bit_length() - 1
    share_count = 1 << stages
    walks = (list(range(1, stages + 1)), list(range(stages, 0, -1)))
    patches, patch = byte_ids.shape
    slot, width = proj_weight.shape
    hidden = up_weight.shape[1]
    vocab = emb_local.shape[0]
    own = patch // tp_count
    part = patches // tp_count
    rows = own * patches
    height = vocab // seq_count
    chunk = hidden // seq_count

    def share_mask(number, walk):
        mask = 0
        for k in range(stages):
            if (number >> (stages - 1 - k)) & 1:
                mask |= 1 << (walk[k] - 1)
        return mask

    def shares_of(which):
        return [
            2 * (chip ^ jnp.where(which == 0, share_mask(n, walks[0]), share_mask(n, walks[1])))
            + which
            for n in range(share_count)
        ]

    shares = shares_of(core)
    others = shares_of(1 - core)
    near = [tp_place ^ m for m in range(tp_count)]
    numbers = jnp.stack(near + shares + others + [core]).astype(jnp.int32)
    core_at = tp_count + 2 * share_count
    call = functools.partial(run, numbers=numbers)

    def core_swap(value):
        return swap(value, "seq", (1,))

    def go(value, step):
        kind, k = step
        if kind == "seq":
            return swap(value, "seq", (1 << walks[0][k], 1 << walks[1][k]))
        return swap(value, "tp", (1 << k,))

    def gate(value, after):
        there = pl.BlockSpec(memory_space=pl.ANY)
        (value,) = call(
            gate_body,
            [like(*value.shape, value.dtype)],
            [value],
            after,
            in_specs=[there],
            out_specs=[there],
            alias={1: 0},
        )
        return value

    ids_own = byte_ids.T
    ids_other = core_swap(ids_own)
    out_other = core_swap(global_out)
    blocks = call(
        functools.partial(sort_body, patch, part, own),
        [like(own * part, width, BF)] * tp_count,
        [out_grad],
        [],
    )
    blocks = [swap(b, "tp", (m,)) if m else b for m, b in enumerate(blocks)]
    far = pl.BlockSpec(memory_space=pltpu.HBM)
    prev_hot, prev_here, own_hot, up_here, down_here = call(
        functools.partial(prepare_body, own, tp_count, share_count, height, core_at),
        [
            like(2 * rows, vocab, BF),
            like(2 * rows, vocab // 2, BF),
            like(rows, vocab, BF),
            like(width, hidden // 2, BF),
            like(hidden // 2, width, BF),
        ],
        [up_weight, down_weight, ids_own, ids_other],
        [blocks[0]],
        in_specs=[far, far, None, None],
        scratch=[
            VMEM((share_count, width, chunk), BF),
            VMEM((share_count, chunk, width), BF),
            pltpu.SemaphoreType.DMA((2, share_count)),
        ],
        room=WIDE,
    )

    def by_slot(value):
        return [value[:, j * slot : (j + 1) * slot] for j in range(own)]

    (slot_in,) = call(
        functools.partial(place_body, own, core_at),
        [like(2 * rows, slot, BF)],
        [global_out, out_other],
        [prev_hot],
    )
    u_rows = times(slot_in, proj_weight) + times(prev_hot, emb_local)
    scale = lax.rsqrt(jnp.mean(u_rows * u_rows, axis=1, keepdims=True) + 1e-05)
    normed = u_rows * scale
    r_rows = (normed * norm_gain).astype(BF)
    a_rows = times(r_rows, up_here)
    sig = jax.nn.sigmoid(a_rows)
    h_rows = (a_rows * sig).astype(BF)
    slope = (sig * (1.0 + a_rows * (1.0 - sig))).astype(BF)
    h_rows, slope = lax.optimization_barrier((h_rows, slope))
    strip = chunk // 2
    h_rows = jnp.concatenate(
        [
            h_rows[:, (z * share_count + n) * strip : (z * share_count + n + 1) * strip]
            for n in range(share_count)
            for z in range(2)
        ],
        axis=1,
    )

    (grad_own,) = call(
        functools.partial(join_body, part, own, tp_count),
        [like(rows, width, BF)],
        blocks,
        [h_rows],
    )
    grad_other = core_swap(grad_own)
    own_hot = gate(own_hot, [grad_own])
    glob = [
        inner(own_hot[j * patches : (j + 1) * patches], value)
        for j, value in enumerate(by_slot(global_in_grad))
    ]
    glob = sum(glob[1:], glob[0])
    glob_sent = glob[vocab // 2 :].astype(BF)
    glob_kept = glob[: vocab // 2].astype(BF)
    glob_more = core_swap(glob_sent)

    (out_rows,) = call(
        functools.partial(place_body, 1, core_at),
        [like(2 * rows, width, BF)],
        [grad_own, grad_other],
        [glob_kept],
    )

    seq_steps = [("seq", k) for k in range(stages)]
    tp_steps = [("tp", k) for k in range(levels)]

    step = functools.partial(call, flops=STEP)

    class Chain:
        def __init__(self, kept, sent, steps):
            self.kept, self.steps, self.at = kept, steps, 0
            self.arrived = go(sent, self.steps[0])
            self.left = len(self.steps) - 1

        def next(self, after):
            self.at += 1
            self.left -= 1
            rows, columns = self.kept.shape
            ins = [self.kept, self.arrived]
            outs = [like(rows // 2, columns, self.kept.dtype)] * 2
            self.kept, sent = step(add_body, outs, ins, after)
            self.arrived = go(sent, self.steps[self.at])
            return self.kept

    class Table:
        def __init__(self, kept, sent):
            self.kept, self.at = kept, 0
            self.plan = (
                [("half", s) for s in seq_steps]
                + [("sum", s) for s in tp_steps]
                + [("join", s) for s in reversed(seq_steps)]
                + [("join", None)]
            )
            self.left = len(self.plan) - 1
            self.arrived = go(sent, self.plan[0][1])

        def next(self, after):
            last, (kind, hop) = self.plan[self.at][0], self.plan[self.at + 1]
            rows, columns = self.kept.shape
            ins = [self.kept, self.arrived]
            if last == "half" and kind == "half":
                self.kept, sent = step(add_body, [like(rows // 2, columns, BF)] * 2, ins, after)
            elif last == "join":
                (self.kept,) = step(stack_body, [like(2 * rows, columns, BF)], ins, after)
                sent = self.kept
            else:
                (self.kept,) = step(sum_body, [like(rows, columns, BF)], ins, after)
                sent = self.kept
            self.at += 1
            self.left -= 1
            self.arrived = core_swap(sent) if hop is None else go(sent, hop)
            return self.kept

    dh_rows = outer(out_rows, down_here)
    da_rows = (dh_rows * slope.astype(F32)).astype(BF)
    dr_part = outer(da_rows, up_here)
    dr_sent = dr_part.astype(BF)
    kind = BF if chunk // tp_count % 16 == 0 else F32
    half = h_rows.shape[1] // 2
    down_kept = inner(h_rows[:, :half], out_rows).astype(kind)
    down_sent = inner(h_rows[:, half:], out_rows).astype(kind)
    up_kept = inner(da_rows[:, :half], r_rows).astype(kind)
    up_sent = inner(da_rows[:, half:], r_rows).astype(kind)
    down = Chain(down_kept, down_sent, seq_steps + tp_steps)
    up = Chain(up_kept, up_sent, tp_steps[:1] + seq_steps + tp_steps[1:])
    dr_more = gate(core_swap(dr_sent), [down_sent, up_sent])
    dr_rows = dr_part + dr_more.astype(F32)

    gain_part = jnp.sum(dr_rows * normed, axis=0, keepdims=True)
    dn_rows = dr_rows * norm_gain
    du_rows = (
        out_rows.astype(F32)
        + scale * (dn_rows - normed * jnp.mean(dn_rows * normed, axis=1, keepdims=True))
    ).astype(BF)
    size = 2 * height
    kept, sent = call(
        functools.partial(tables_in_body, share_count, tp_count, height),
        [like(share_count // 2 * size, width + 128, BF)] * 2,
        [glob_kept, glob_more, inner(prev_here, du_rows), gain_part],
        [up.kept],
    )
    table = Table(kept, sent)
    share = width // seq_count
    kind = BF if share // tp_count % 16 == 0 else F32
    du_here = jnp.concatenate(
        [lax.dynamic_slice_in_dim(du_rows, s * share, share, 1) for s in shares], axis=1
    )
    value = inner(du_here, slot_in)
    kept, sent = call(
        functools.partial(split_body, tp_count, share),
        [like(value.shape[0] // 2, slot, kind)] * 2,
        [value],
        [table.kept],
    )
    proj = Chain(kept, sent, seq_steps + tp_steps)
    du_own = lax.dynamic_slice_in_dim(du_rows, core * rows, rows, 0)
    back = outer(du_own, proj_weight).astype(BF)
    glob_out_grad = jnp.concatenate(
        [back[j * patches : (j + 1) * patches] for j in range(own)], axis=1
    )

    last = [up.kept, proj.kept, table.kept, down.kept, glob_out_grad]
    names = {"T": table, "D": down, "U": up, "P": proj}
    queue = [names[c] for c in "TDTUTPDUPTUTPDTPUTD"]
    for chain in queue + [table, proj, down, up] * 16:
        if chain.left:
            last = [chain.next(last)]

    parts = 4
    wide = width // parts

    def columns(height):
        return pl.BlockSpec((height, wide), lambda n, s: (0, n))

    count = table.kept.shape[0]
    lines = width // 128
    beside = pl.BlockSpec((count, 128), lambda n, s: (0, lines))
    emb_global_grad, emb_local_grad, gain_grad = call(
        functools.partial(tables_body, share_count, tp_count, height),
        [like(vocab, width, F32), like(vocab, width, F32), like(lines, 128, F32)],
        [table.kept, table.arrived, table.kept, table.arrived],
        last,
        grid=parts,
        in_specs=[columns(count), columns(count), beside, beside],
        out_specs=[columns(vocab), columns(vocab), None],
    )
    ends = [down, up, proj]
    down_grad, up_grad, proj_grad = call(
        finals_body,
        [like(*c.kept.shape, F32) for c in ends],
        [x for c in ends for x in (c.kept, c.arrived)],
        [emb_global_grad],
    )
    return (
        glob_out_grad,
        emb_global_grad,
        emb_local_grad,
        gain_grad.reshape(width),
        proj_grad.T,
        up_grad.T,
        down_grad,
    )


def solution(mesh):
    placed = (
        P("seq", None),
        P("seq", "tp"),
        P("seq", "tp"),
        P(("seq", "tp"), None),
        P(),
        P(),
        P(),
        P(),
        P(),
    )
    return jax.shard_map(
        on_device,
        mesh=mesh,
        in_specs=placed,
        out_specs=(
            P("seq", "tp"),
            P(),
            P(),
            P(),
            P(None, ("seq", "tp")),
            P(None, ("seq", "tp")),
            P(("seq", "tp"), None),
        ),
        check_vma=False,
    )
```

```python
import functools

import jax
import jax.numpy as jnp
from jax import lax
from jax.experimental import pallas as pl
from jax.experimental.pallas import tpu as pltpu
from jax.sharding import PartitionSpec as P

BF = jnp.bfloat16
F32 = jnp.float32
ROOM = 8 * 1024 * 1024
WIDE = 24 * 1024 * 1024
STEP = 6 * 1000 * 1000 * 1000
VMEM = pltpu.VMEM


def inner(left, right):
    return lax.dot_general(
        left, right, (((0,), (0,)), ((), ())), preferred_element_type=F32
    )


def outer(left, right):
    return lax.dot_general(
        left, right, (((1,), (1,)), ((), ())), preferred_element_type=F32
    )


def times(left, right):
    return jnp.dot(left, right, preferred_element_type=F32)


def swap(value, axis, masks):
    count = lax.axis_size(axis)
    pairs = [(i, i ^ masks[i % len(masks)]) for i in range(count)]
    return lax.ppermute(value, axis, pairs)


def like(rows, columns, kind):
    return jax.ShapeDtypeStruct((rows, columns), kind)


def whole(array):
    return pl.BlockSpec(array.shape, lambda n, s: (0,) * len(array.shape))


def run(
    body, outs, ins, after, numbers, in_specs=None, out_specs=None, scratch=(), room=ROOM,
    alias=None, flops=0, grid=1,
):
    count, late = 1 + len(ins), len(after)

    def kernel(*refs):
        body(*refs[:count], *refs[count + late :])

    in_specs = in_specs or [None] * len(ins)
    out_specs = out_specs or [None] * len(outs)
    return pl.pallas_call(
        kernel,
        out_shape=tuple(outs),
        grid_spec=pltpu.PrefetchScalarGridSpec(
            num_scalar_prefetch=1,
            grid=(grid,),
            in_specs=[s or whole(a) for s, a in zip(in_specs, ins)]
            + [pl.BlockSpec(memory_space=pl.ANY)] * late,
            out_specs=tuple(s or whole(a) for s, a in zip(out_specs, outs)),
            scratch_shapes=list(scratch),
        ),
        input_output_aliases=alias or {},
        compiler_params=pltpu.CompilerParams(vmem_limit_bytes=room),
        cost_estimate=pl.CostEstimate(flops=flops, bytes_accessed=0, transcendentals=0),
    )(numbers, *ins, *after)


def sort_body(patch, part, own, numbers, grad, *blocks):
    size = own * part
    row = lax.broadcasted_iota(jnp.int32, (size, grad.shape[0]), 0)
    source = lax.broadcasted_iota(jnp.int32, (size, grad.shape[0]), 1)
    for m, block in enumerate(blocks):
        wanted = (row % part) * patch + numbers[m] * own + row // part
        block[...] = times((source == wanted).astype(BF), grad[...]).astype(BF)


def join_body(part, own, count, numbers, *refs):
    blocks, joined = refs[:-1], refs[-1]
    for m, block in enumerate(blocks):
        for j in range(own):
            start = pl.multiple_of((j * count + numbers[m]) * part, part)
            joined[pl.ds(start, part), :] = block[j * part : (j + 1) * part, :]


def sent_order(count):
    return sorted(range(count), key=lambda m: bin(m + count)[:2:-1])


def id_of(ids, place):
    lane = lax.broadcasted_iota(jnp.int32, ids.shape, 1)
    return jnp.sum(jnp.where(lane == place, ids + 1, 0), axis=1, keepdims=True) - 1


def vocab_line(numbers, first, count, height):
    lane = lax.broadcasted_iota(jnp.int32, (1, count * height), 1)
    line = lane % height
    for n in range(count):
        line = line + jnp.where(lane // height == n, numbers[first + n] * height, 0)
    return line


def hot(ids, line):
    return jnp.where(ids == line, 1.0, 0.0).astype(BF)


def place_body(own, core_at, numbers, mine, other, both):
    patches, width = mine.shape[0], mine.shape[1] // own
    rows = own * patches
    for side, value in ((numbers[core_at], mine), (1 - numbers[core_at], other)):
        for j in range(own):
            start = pl.multiple_of(side * rows + j * patches, patches)
            both[pl.ds(start, patches), :] = value[:, j * width : (j + 1) * width]


def hots(own, tp_count, share_count, height, core_at, numbers, ids_own, ids_other, prev, here, mine):
    patches = ids_own.shape[1]
    plain = lax.broadcasted_iota(jnp.int32, (1, prev.shape[1]), 1)
    line = vocab_line(numbers, tp_count, share_count, height)
    both = vocab_line(numbers, tp_count, 2 * share_count, height)
    core = numbers[core_at]
    for side, which in ((core, ids_own), (1 - core, ids_other)):
        ids = which[...].T
        for j in range(own):
            start = pl.multiple_of(side * own * patches + j * patches, patches)
            at = pl.ds(start, patches)
            before = id_of(ids, numbers[0] * own + j - 1)
            prev[at, :] = hot(before, plain)
            here[at, :] = hot(before, line)
            if which is ids_own:
                wanted = id_of(ids, numbers[0] * own + j)
                mine[j * patches : (j + 1) * patches, :] = hot(wanted, both)


def turn_matrix(tp_count, chunk, numbers):
    unit = chunk // tp_count
    row = lax.broadcasted_iota(jnp.int32, (chunk, chunk), 0)
    column = lax.broadcasted_iota(jnp.int32, (chunk, chunk), 1)
    source = column % unit
    for i, m in enumerate(sent_order(tp_count)):
        source = source + jnp.where(column // unit == i, numbers[m] * unit, 0)
    return (row == source).astype(BF)


def prepare_body(
    own, tp_count, share_count, height, core_at,
    numbers, up, down, ids_own, ids_other,
    prev, here, mine, up_here, down_here, ups, downs, ready,
):
    chunk = ups.shape[2]
    unit = chunk // tp_count
    half = chunk // 2
    copies = []
    for n in range(share_count):
        at = pl.ds(pl.multiple_of(numbers[tp_count + n] * chunk, chunk), chunk)
        copies.append(pltpu.make_async_copy(up.at[:, at], ups.at[n], ready.at[0, n]))
        copies[-1].start()
    for n in range(share_count):
        at = pl.ds(pl.multiple_of(numbers[tp_count + n] * chunk, chunk), chunk)
        copies.append(pltpu.make_async_copy(down.at[at, :], downs.at[n], ready.at[1, n]))
        copies[-1].start()
    hots(
        own, tp_count, share_count, height, core_at, numbers, ids_own, ids_other, prev, here, mine
    )
    turn = turn_matrix(tp_count, chunk, numbers)
    for n in range(share_count):
        copies[n].wait()
        value = times(ups[n], turn).astype(BF)
        for z in range(2):
            first = (z * share_count + n) * half
            up_here[:, first : first + half] = value[:, z * half : (z + 1) * half]
    for n in range(share_count):
        copies[share_count + n].wait()
        for i, m in enumerate(sent_order(tp_count)):
            z, place = i // (tp_count // 2), i % (tp_count // 2)
            first = (z * share_count + n) * half + place * unit
            start = pl.multiple_of(numbers[m] * unit, unit)
            down_here[first : first + unit, :] = downs[n, pl.ds(start, unit), :]


def split_body(tp_count, share, numbers, value, kept, sent):
    unit = share // tp_count
    half = kept.shape[0]
    for n in range(value.shape[0] // share):
        for i, m in enumerate(sent_order(tp_count)):
            at = pl.ds(n * share + pl.multiple_of(numbers[m] * unit, unit), unit)
            place = n * share + i * unit
            target = kept if place < half else sent
            row = place % half
            target[row : row + unit, :] = value[at, :].astype(target.dtype)


def tables_in_body(
    share_count, first_share, height, numbers, glob, glob_more, local, gains, kept, sent
):
    width = glob.shape[1]
    strip = width // (2 * share_count)
    lines = width // 128
    lane = lax.broadcasted_iota(jnp.int32, (1, width), 1)
    both = glob[...].astype(F32) + glob_more[...].astype(F32)
    size = 2 * height
    kept[:, width:] = jnp.zeros((kept.shape[0], 128), BF)
    sent[:, width:] = jnp.zeros((sent.shape[0], 128), BF)
    for n in range(share_count):
        target = kept if n < share_count // 2 else sent
        first = (n % (share_count // 2)) * size
        at = slice(n * height, (n + 1) * height)
        target[first : first + height, :width] = both[at, :].astype(BF)
        target[first + height : first + size, :width] = local[at, :].astype(BF)
        mine = jnp.where(lane // strip == numbers[first_share + n], gains[...], 0.0)
        rows = [mine[:, i * 128 : (i + 1) * 128] for i in range(lines)]
        rows.append(jnp.zeros((16 - lines, 128), F32))
        target[first : first + 16, width:] = jnp.concatenate(rows, axis=0).astype(BF)


def gate_body(numbers, value, same):
    pass


def add_body(numbers, kept, arrived, keep, send):
    half = keep.shape[0]
    keep[...] = (kept[:half, :].astype(F32) + arrived[:half, :].astype(F32)).astype(keep.dtype)
    send[...] = (kept[half:, :].astype(F32) + arrived[half:, :].astype(F32)).astype(send.dtype)


def sum_body(numbers, kept, arrived, summed):
    summed[...] = (kept[...].astype(F32) + arrived[...].astype(F32)).astype(summed.dtype)


def stack_body(numbers, first, second, both):
    rows = first.shape[0]
    both[:rows, :] = first[...]
    both[rows:, :] = second[...]


def tables_body(
    share_count, first_share, height, numbers, first, second, first_gain, second_gain,
    glob, local, gain,
):
    gains = None
    for side, (value, line) in enumerate(((first, first_gain), (second, second_gain))):
        for n in range(share_count):
            start = numbers[first_share + side * share_count + n] * height
            at = pl.ds(pl.multiple_of(start, height), height)
            row = 2 * n * height
            glob[at, :] = value[row : row + height, :].astype(F32)
            local[at, :] = value[row + height : row + 2 * height, :].astype(F32)
            term = line[row : row + 16, :].astype(F32)
            gains = term if gains is None else gains + term
    gain[...] = gains[: gain.shape[0]]


def finals_body(numbers, *refs):
    count = len(refs) // 3
    for i in range(count):
        kept, arrived, total = refs[2 * i], refs[2 * i + 1], refs[2 * count + i]
        total[...] = kept[...].astype(F32) + arrived[...].astype(F32)
    refs[-1][...] = jnp.zeros(refs[-1].shape, F32)


def on_device(
    byte_ids,
    global_out,
    global_in_grad,
    out_grad,
    proj_weight,
    emb_local,
    norm_gain,
    up_weight,
    down_weight,
):
    seq_count = lax.axis_size("seq")
    tp_count = lax.axis_size("tp")
    seq_place = lax.axis_index("seq")
    tp_place = lax.axis_index("tp")
    core = seq_place & 1
    chip = seq_place >> 1
    stages = seq_count.bit_length() - 2
    levels = tp_count.bit_length() - 1
    share_count = 1 << stages
    walks = (list(range(1, stages + 1)), list(range(stages, 0, -1)))
    patches, patch = byte_ids.shape
    slot, width = proj_weight.shape
    hidden = up_weight.shape[1]
    vocab = emb_local.shape[0]
    own = patch // tp_count
    part = patches // tp_count
    rows = own * patches
    height = vocab // seq_count
    chunk = hidden // seq_count

    def share_mask(number, walk):
        mask = 0
        for k in range(stages):
            if (number >> (stages - 1 - k)) & 1:
                mask |= 1 << (walk[k] - 1)
        return mask

    def shares_of(which):
        return [
            2 * (chip ^ jnp.where(which == 0, share_mask(n, walks[0]), share_mask(n, walks[1])))
            + which
            for n in range(share_count)
        ]

    shares = shares_of(core)
    others = shares_of(1 - core)
    near = [tp_place ^ m for m in range(tp_count)]
    numbers = jnp.stack(near + shares + others + [core]).astype(jnp.int32)
    core_at = tp_count + 2 * share_count
    call = functools.partial(run, numbers=numbers)

    def core_swap(value):
        return swap(value, "seq", (1,))

    def go(value, step):
        kind, k = step
        if kind == "seq":
            return swap(value, "seq", (1 << walks[0][k], 1 << walks[1][k]))
        return swap(value, "tp", (1 << k,))

    def gate(value, after):
        there = pl.BlockSpec(memory_space=pl.ANY)
        (value,) = call(
            gate_body,
            [like(*value.shape, value.dtype)],
            [value],
            after,
            in_specs=[there],
            out_specs=[there],
            alias={1: 0},
        )
        return value

    ids_own = byte_ids.T
    ids_other = core_swap(ids_own)
    out_other = core_swap(global_out)
    blocks = call(
        functools.partial(sort_body, patch, part, own),
        [like(own * part, width, BF)] * tp_count,
        [out_grad],
        [],
        flops=STEP,
    )
    blocks = [swap(b, "tp", (m,)) if m else b for m, b in enumerate(blocks)]
    far = pl.BlockSpec(memory_space=pltpu.HBM)
    prev_hot, prev_here, own_hot, up_here, down_here = call(
        functools.partial(prepare_body, own, tp_count, share_count, height, core_at),
        [
            like(2 * rows, vocab, BF),
            like(2 * rows, vocab // 2, BF),
            like(rows, vocab, BF),
            like(width, hidden // 2, BF),
            like(hidden // 2, width, BF),
        ],
        [up_weight, down_weight, ids_own, ids_other],
        [blocks[0]],
        in_specs=[far, far, None, None],
        scratch=[
            VMEM((share_count, width, chunk), BF),
            VMEM((share_count, chunk, width), BF),
            pltpu.SemaphoreType.DMA((2, share_count)),
        ],
        room=WIDE,
    )

    def by_slot(value):
        return [value[:, j * slot : (j + 1) * slot] for j in range(own)]

    (slot_in,) = call(
        functools.partial(place_body, own, core_at),
        [like(2 * rows, slot, BF)],
        [global_out, out_other],
        [prev_hot],
    )
    u_rows = times(slot_in, proj_weight) + times(prev_hot, emb_local)
    scale = lax.rsqrt(jnp.mean(u_rows * u_rows, axis=1, keepdims=True) + 1e-05)
    normed = u_rows * scale
    r_rows = (normed * norm_gain).astype(BF)
    a_rows = times(r_rows, up_here)
    sig = jax.nn.sigmoid(a_rows)
    h_rows = (a_rows * sig).astype(BF)
    slope = (sig * (1.0 + a_rows * (1.0 - sig))).astype(BF)
    h_rows, slope = lax.optimization_barrier((h_rows, slope))
    strip = chunk // 2
    h_rows = jnp.concatenate(
        [
            h_rows[:, (z * share_count + n) * strip : (z * share_count + n + 1) * strip]
            for n in range(share_count)
            for z in range(2)
        ],
        axis=1,
    )

    (grad_own,) = call(
        functools.partial(join_body, part, own, tp_count),
        [like(rows, width, BF)],
        blocks,
        [h_rows],
    )
    grad_other = core_swap(grad_own)
    own_hot = gate(own_hot, [grad_own])
    glob = [
        inner(own_hot[j * patches : (j + 1) * patches], value)
        for j, value in enumerate(by_slot(global_in_grad))
    ]
    glob = sum(glob[1:], glob[0])
    glob_sent = glob[vocab // 2 :].astype(BF)
    glob_kept = glob[: vocab // 2].astype(BF)
    glob_more = core_swap(glob_sent)

    (out_rows,) = call(
        functools.partial(place_body, 1, core_at),
        [like(2 * rows, width, BF)],
        [grad_own, grad_other],
        [glob_kept],
    )

    seq_steps = [("seq", k) for k in range(stages)]
    tp_steps = [("tp", k) for k in range(levels)]

    step = functools.partial(call, flops=STEP)

    class Chain:
        def __init__(self, kept, sent, steps):
            self.kept, self.steps, self.at = kept, steps, 0
            self.arrived = go(sent, self.steps[0])
            self.left = len(self.steps) - 1

        def next(self, after):
            self.at += 1
            self.left -= 1
            rows, columns = self.kept.shape
            ins = [self.kept, self.arrived]
            outs = [like(rows // 2, columns, self.kept.dtype)] * 2
            self.kept, sent = step(add_body, outs, ins, after)
            self.arrived = go(sent, self.steps[self.at])
            return self.kept

    class Table:
        def __init__(self, kept, sent):
            self.kept, self.at = kept, 0
            self.plan = (
                [("half", s) for s in seq_steps]
                + [("sum", s) for s in tp_steps]
                + [("join", s) for s in reversed(seq_steps)]
                + [("join", None)]
            )
            self.left = len(self.plan) - 1
            self.arrived = go(sent, self.plan[0][1])

        def next(self, after):
            last, (kind, hop) = self.plan[self.at][0], self.plan[self.at + 1]
            rows, columns = self.kept.shape
            ins = [self.kept, self.arrived]
            if last == "half" and kind == "half":
                self.kept, sent = step(add_body, [like(rows // 2, columns, BF)] * 2, ins, after)
            elif last == "join":
                (self.kept,) = step(stack_body, [like(2 * rows, columns, BF)], ins, after)
                sent = self.kept
            else:
                (self.kept,) = step(sum_body, [like(rows, columns, BF)], ins, after)
                sent = self.kept
            self.at += 1
            self.left -= 1
            self.arrived = core_swap(sent) if hop is None else go(sent, hop)
            return self.kept

    dh_rows = outer(out_rows, down_here)
    da_rows = (dh_rows * slope.astype(F32)).astype(BF)
    dr_part = outer(da_rows, up_here)
    dr_sent = dr_part.astype(BF)
    kind = BF if chunk // tp_count % 16 == 0 else F32
    half = h_rows.shape[1] // 2
    down_kept = inner(h_rows[:, :half], out_rows).astype(kind)
    down_sent = inner(h_rows[:, half:], out_rows).astype(kind)
    up_kept = inner(da_rows[:, :half], r_rows).astype(kind)
    up_sent = inner(da_rows[:, half:], r_rows).astype(kind)
    down = Chain(down_kept, down_sent, seq_steps + tp_steps)
    up = Chain(up_kept, up_sent, tp_steps[:1] + seq_steps + tp_steps[1:])
    dr_more = gate(core_swap(dr_sent), [down_sent, up_sent])
    dr_rows = dr_part + dr_more.astype(F32)

    gain_part = jnp.sum(dr_rows * normed, axis=0, keepdims=True)
    dn_rows = dr_rows * norm_gain
    du_rows = (
        out_rows.astype(F32)
        + scale * (dn_rows - normed * jnp.mean(dn_rows * normed, axis=1, keepdims=True))
    ).astype(BF)
    size = 2 * height
    kept, sent = call(
        functools.partial(tables_in_body, share_count, tp_count, height),
        [like(share_count // 2 * size, width + 128, BF)] * 2,
        [glob_kept, glob_more, inner(prev_here, du_rows), gain_part],
        [up.kept],
    )
    table = Table(kept, sent)
    share = width // seq_count
    kind = BF if share // tp_count % 16 == 0 else F32
    du_here = jnp.concatenate(
        [lax.dynamic_slice_in_dim(du_rows, s * share, share, 1) for s in shares], axis=1
    )
    value = inner(du_here, slot_in)
    kept, sent = call(
        functools.partial(split_body, tp_count, share),
        [like(value.shape[0] // 2, slot, kind)] * 2,
        [value],
        [table.kept],
    )
    proj = Chain(kept, sent, seq_steps + tp_steps)
    du_own = lax.dynamic_slice_in_dim(du_rows, core * rows, rows, 0)
    back = outer(du_own, proj_weight).astype(BF)
    glob_out_grad = jnp.concatenate(
        [back[j * patches : (j + 1) * patches] for j in range(own)], axis=1
    )

    last = [up.kept, proj.kept, table.kept, down.kept, glob_out_grad]
    names = {"T": table, "D": down, "U": up, "P": proj}
    queue = [names[c] for c in "TDTUTPDUPTUTPDTPUTD"]
    for chain in queue + [table, proj, down, up] * 16:
        if chain.left:
            last = [chain.next(last)]

    parts = 4
    wide = width // parts

    def columns(height):
        return pl.BlockSpec((height, wide), lambda n, s: (0, n))

    count = table.kept.shape[0]
    lines = width // 128
    beside = pl.BlockSpec((count, 128), lambda n, s: (0, lines))
    ends = [down, up, proj]
    down_grad, up_grad, proj_grad, token = call(
        finals_body,
        [like(*c.kept.shape, F32) for c in ends] + [like(8, 128, F32)],
        [x for c in ends for x in (c.kept, c.arrived)],
        last,
        flops=STEP,
    )
    emb_global_grad, emb_local_grad, gain_grad = call(
        functools.partial(tables_body, share_count, tp_count, height),
        [like(vocab, width, F32), like(vocab, width, F32), like(lines, 128, F32)],
        [table.kept, table.arrived, table.kept, table.arrived],
        [token],
        flops=STEP,
        grid=parts,
        in_specs=[columns(count), columns(count), beside, beside],
        out_specs=[columns(vocab), columns(vocab), None],
    )
    return (
        glob_out_grad,
        emb_global_grad,
        emb_local_grad,
        gain_grad.reshape(width),
        proj_grad.T,
        up_grad.T,
        down_grad,
    )


def solution(mesh):
    placed = (
        P("seq", None),
        P("seq", "tp"),
        P("seq", "tp"),
        P(("seq", "tp"), None),
        P(),
        P(),
        P(),
        P(),
        P(),
    )
    return jax.shard_map(
        on_device,
        mesh=mesh,
        in_specs=placed,
        out_specs=(
            P("seq", "tp"),
            P(),
            P(),
            P(),
            P(None, ("seq", "tp")),
            P(None, ("seq", "tp")),
            P(("seq", "tp"), None),
        ),
        check_vma=False,
    )
```

```python
import functools

import jax
import jax.numpy as jnp
from jax import lax
from jax.experimental import pallas as pl
from jax.experimental.pallas import tpu as pltpu
from jax.sharding import PartitionSpec as P

BF = jnp.bfloat16
F32 = jnp.float32
ROOM = 8 * 1024 * 1024
PARTS = 3
ORDER = "TDTUPTDUPTFTT"
STEP = 6 * 1000 * 1000 * 1000
VMEM = pltpu.VMEM


def inner(left, right):
    return lax.dot_general(
        left, right, (((0,), (0,)), ((), ())), preferred_element_type=F32
    )


def outer(left, right):
    return lax.dot_general(
        left, right, (((1,), (1,)), ((), ())), preferred_element_type=F32
    )


def times(left, right):
    return jnp.dot(left, right, preferred_element_type=F32)


def swap(value, axis, masks):
    count = lax.axis_size(axis)
    pairs = [(i, i ^ masks[i % len(masks)]) for i in range(count)]
    return lax.ppermute(value, axis, pairs)


def like(rows, columns, kind):
    return jax.ShapeDtypeStruct((rows, columns), kind)


def whole(array):
    return pl.BlockSpec(array.shape, lambda n, s: (0,) * len(array.shape))


def run(
    body, outs, ins, after, numbers, in_specs=None, out_specs=None, scratch=(), room=ROOM,
    alias=None, flops=0, grid=1,
):
    count, late = 1 + len(ins), len(after)

    def kernel(*refs):
        body(*refs[:count], *refs[count + late :])

    in_specs = in_specs or [None] * len(ins)
    out_specs = out_specs or [None] * len(outs)
    return pl.pallas_call(
        kernel,
        out_shape=tuple(outs),
        grid_spec=pltpu.PrefetchScalarGridSpec(
            num_scalar_prefetch=1,
            grid=(grid,),
            in_specs=[s or whole(a) for s, a in zip(in_specs, ins)]
            + [pl.BlockSpec(memory_space=pl.ANY)] * late,
            out_specs=tuple(s or whole(a) for s, a in zip(out_specs, outs)),
            scratch_shapes=list(scratch),
        ),
        input_output_aliases=alias or {},
        compiler_params=pltpu.CompilerParams(vmem_limit_bytes=room),
        cost_estimate=pl.CostEstimate(flops=flops, bytes_accessed=0, transcendentals=0),
    )(numbers, *ins, *after)


def sort_body(patch, part, own, numbers, grad, *blocks):
    size = own * part
    row = lax.broadcasted_iota(jnp.int32, (size, grad.shape[0]), 0)
    source = lax.broadcasted_iota(jnp.int32, (size, grad.shape[0]), 1)
    for m, block in enumerate(blocks):
        wanted = (row % part) * patch + numbers[m] * own + row // part
        block[...] = times((source == wanted).astype(BF), grad[...]).astype(BF)


def join_body(part, own, count, numbers, *refs):
    blocks, joined = refs[:-1], refs[-1]
    for m, block in enumerate(blocks):
        for j in range(own):
            start = pl.multiple_of((j * count + numbers[m]) * part, part)
            joined[pl.ds(start, part), :] = block[j * part : (j + 1) * part, :]


def sent_order(count):
    return sorted(range(count), key=lambda m: bin(m + count)[:2:-1])


def id_of(ids, place):
    lane = lax.broadcasted_iota(jnp.int32, ids.shape, 1)
    return jnp.sum(jnp.where(lane == place, ids + 1, 0), axis=1, keepdims=True) - 1


def vocab_line(numbers, first, count, height):
    lane = lax.broadcasted_iota(jnp.int32, (1, count * height), 1)
    line = lane % height
    for n in range(count):
        line = line + jnp.where(lane // height == n, numbers[first + n] * height, 0)
    return line


def hot(ids, line):
    return jnp.where(ids == line, 1.0, 0.0).astype(BF)


def place_body(own, core_at, numbers, mine, other, both):
    patches, width = mine.shape[0], mine.shape[1] // own
    rows = own * patches
    for side, value in ((numbers[core_at], mine), (1 - numbers[core_at], other)):
        for j in range(own):
            start = pl.multiple_of(side * rows + j * patches, patches)
            both[pl.ds(start, patches), :] = value[:, j * width : (j + 1) * width]


def hots_body(own, tp_count, share_count, height, core_at, numbers, ids_own, ids_other, prev, here, mine):
    patches = ids_own.shape[1]
    plain = lax.broadcasted_iota(jnp.int32, (1, prev.shape[1]), 1)
    line = vocab_line(numbers, tp_count, share_count, height)
    both = vocab_line(numbers, tp_count, 2 * share_count, height)
    core = numbers[core_at]
    for side, which in ((core, ids_own), (1 - core, ids_other)):
        ids = which[...].T
        for j in range(own):
            start = pl.multiple_of(side * own * patches + j * patches, patches)
            at = pl.ds(start, patches)
            before = id_of(ids, numbers[0] * own + j - 1)
            prev[at, :] = hot(before, plain)
            here[at, :] = hot(before, line)
            if which is ids_own:
                wanted = id_of(ids, numbers[0] * own + j)
                mine[j * patches : (j + 1) * patches, :] = hot(wanted, both)


def turn_matrix(tp_count, chunk, numbers):
    unit = chunk // tp_count
    row = lax.broadcasted_iota(jnp.int32, (chunk, chunk), 0)
    column = lax.broadcasted_iota(jnp.int32, (chunk, chunk), 1)
    source = column % unit
    for i, m in enumerate(sent_order(tp_count)):
        source = source + jnp.where(column // unit == i, numbers[m] * unit, 0)
    return (row == source).astype(BF)


def pick_up_body(tp_count, share_count, numbers, up, up_here, ups, ready):
    chunk = ups.shape[2]
    half = chunk // 2
    copies = []
    for n in range(share_count):
        at = pl.ds(pl.multiple_of(numbers[tp_count + n] * chunk, chunk), chunk)
        copies.append(pltpu.make_async_copy(up.at[:, at], ups.at[n], ready.at[n]))
        copies[-1].start()
    turn = turn_matrix(tp_count, chunk, numbers)
    for n in range(share_count):
        copies[n].wait()
        value = times(ups[n], turn).astype(BF)
        for z in range(2):
            first = (z * share_count + n) * half
            up_here[:, first : first + half] = value[:, z * half : (z + 1) * half]


def pick_down_body(tp_count, share_count, numbers, down, down_here, ready):
    chunk = down_here.shape[0] // share_count
    unit = chunk // tp_count
    half = chunk // 2
    copies = []
    for n in range(share_count):
        for i, m in enumerate(sent_order(tp_count)):
            z, place = i // (tp_count // 2), i % (tp_count // 2)
            first = (z * share_count + n) * half + place * unit
            start = numbers[tp_count + n] * chunk + numbers[m] * unit
            source = down.at[pl.ds(pl.multiple_of(start, unit), unit), :]
            target = down_here.at[pl.ds(first, unit), :]
            copies.append(pltpu.make_async_copy(source, target, ready.at[n, i]))
            copies[-1].start()
    for copy in copies:
        copy.wait()


def split_body(tp_count, share, numbers, value, kept, sent):
    unit = share // tp_count
    half = kept.shape[0]
    inner_shares = value.shape[0] // share // 2
    inner_places = tp_count // 2
    for n in range(2 * inner_shares):
        for i, m in enumerate(sent_order(tp_count)):
            at = pl.ds(n * share + pl.multiple_of(numbers[m] * unit, unit), unit)
            place = 2 * (n // inner_shares) + i // inner_places
            place = place * inner_shares + n % inner_shares
            place = (place * inner_places + i % inner_places) * unit
            target = kept if place < half else sent
            row = place % half
            target[row : row + unit, :] = value[at, :].astype(target.dtype)


def tables_in_body(
    share_count, first_share, height, numbers, glob, glob_more, local, gains, kept, sent
):
    width = glob.shape[1]
    strip = width // (2 * share_count)
    lines = width // 128
    lane = lax.broadcasted_iota(jnp.int32, (1, width), 1)
    both = glob[...].astype(F32) + glob_more[...].astype(F32)
    size = 2 * height
    kept[:, width:] = jnp.zeros((kept.shape[0], 128), BF)
    sent[:, width:] = jnp.zeros((sent.shape[0], 128), BF)
    for n in range(share_count):
        target = kept if n < share_count // 2 else sent
        first = (n % (share_count // 2)) * size
        at = slice(n * height, (n + 1) * height)
        target[first : first + height, :width] = both[at, :].astype(BF)
        target[first + height : first + size, :width] = local[at, :].astype(BF)
        mine = jnp.where(lane // strip == numbers[first_share + n], gains[...], 0.0)
        rows = [mine[:, i * 128 : (i + 1) * 128] for i in range(lines)]
        rows.append(jnp.zeros((16 - lines, 128), F32))
        target[first : first + 16, width:] = jnp.concatenate(rows, axis=0).astype(BF)


def gate_body(numbers, value, same):
    pass


def add_body(numbers, kept, arrived, keep, send):
    half = keep.shape[0]
    keep[...] = (kept[:half, :].astype(F32) + arrived[:half, :].astype(F32)).astype(keep.dtype)
    send[...] = (kept[half:, :].astype(F32) + arrived[half:, :].astype(F32)).astype(send.dtype)


def sum_body(numbers, kept, arrived, summed):
    summed[...] = (kept[...].astype(F32) + arrived[...].astype(F32)).astype(summed.dtype)


def stack_body(numbers, first, second, *parts):
    rows = first.shape[0]
    column = 0
    for part in parts:
        at = slice(column, column + part.shape[1])
        part[:rows, :] = first[:, at]
        part[rows:, :] = second[:, at]
        column += part.shape[1]


def tables_body(share_count, first_share, height, count, numbers, *refs):
    sides = (refs[:count], refs[count : 2 * count])
    glob, local, gain = refs[2 * count :]
    width = glob.shape[1]
    gains = None
    for side, parts in enumerate(sides):
        for n in range(share_count):
            start = numbers[first_share + side * share_count + n] * height
            at = pl.ds(pl.multiple_of(start, height), height)
            row = 2 * n * height
            column = 0
            for part in parts:
                inside = min(part.shape[1], width - column)
                to = slice(column, column + inside)
                glob[at, to] = part[row : row + height, :inside].astype(F32)
                local[at, to] = part[row + height : row + 2 * height, :inside].astype(F32)
                column += inside
            term = parts[-1][row : row + 16, parts[-1].shape[1] - 128 :].astype(F32)
            gains = term if gains is None else gains + term
    gain[...] = gains[: gain.shape[0]]


def last_body(numbers, *refs):
    keep, send = refs[-2:]
    row = 0
    for i in range(len(refs) // 2 - 1):
        kept, arrived = refs[2 * i], refs[2 * i + 1]
        half = kept.shape[0] // 2
        at = slice(row, row + half)
        for target, part in ((keep, slice(0, half)), (send, slice(half, 2 * half))):
            value = kept[part, :].astype(F32) + arrived[part, :].astype(F32)
            target[at, :] = value.astype(target.dtype)
        row += half


def finals_body(numbers, kept, arrived, *wholes):
    row = 0
    for whole in wholes:
        at = slice(row, row + whole.shape[0])
        whole[...] = kept[at, :].astype(F32) + arrived[at, :].astype(F32)
        row += whole.shape[0]


def on_device(
    byte_ids,
    global_out,
    global_in_grad,
    out_grad,
    proj_weight,
    emb_local,
    norm_gain,
    up_weight,
    down_weight,
):
    seq_count = lax.axis_size("seq")
    tp_count = lax.axis_size("tp")
    seq_place = lax.axis_index("seq")
    tp_place = lax.axis_index("tp")
    core = seq_place & 1
    chip = seq_place >> 1
    stages = seq_count.bit_length() - 2
    levels = tp_count.bit_length() - 1
    share_count = 1 << stages
    walks = (list(range(1, stages + 1)), list(range(stages, 0, -1)))
    patches, patch = byte_ids.shape
    slot, width = proj_weight.shape
    hidden = up_weight.shape[1]
    vocab = emb_local.shape[0]
    own = patch // tp_count
    part = patches // tp_count
    rows = own * patches
    height = vocab // seq_count
    chunk = hidden // seq_count

    def share_mask(number, walk):
        mask = 0
        for k in range(stages):
            if (number >> (stages - 1 - k)) & 1:
                mask |= 1 << (walk[k] - 1)
        return mask

    def shares_of(which):
        return [
            2 * (chip ^ jnp.where(which == 0, share_mask(n, walks[0]), share_mask(n, walks[1])))
            + which
            for n in range(share_count)
        ]

    shares = shares_of(core)
    others = shares_of(1 - core)
    near = [tp_place ^ m for m in range(tp_count)]
    numbers = jnp.stack(near + shares + others + [core]).astype(jnp.int32)
    core_at = tp_count + 2 * share_count
    call = functools.partial(run, numbers=numbers)

    def core_swap(value):
        return swap(value, "seq", (1,))

    def go(value, step):
        kind, k = step
        if kind == "seq":
            return swap(value, "seq", (1 << walks[0][k], 1 << walks[1][k]))
        return swap(value, "tp", (1 << k,))

    def gate(value, after):
        there = pl.BlockSpec(memory_space=pl.ANY)
        (value,) = call(
            gate_body,
            [like(*value.shape, value.dtype)],
            [value],
            after,
            in_specs=[there],
            out_specs=[there],
            alias={1: 0},
        )
        return value

    ids_own = byte_ids.T
    ids_other = core_swap(ids_own)
    out_other = core_swap(global_out)
    blocks = call(
        functools.partial(sort_body, patch, part, own),
        [like(own * part, width, BF)] * tp_count,
        [out_grad],
        [],
        flops=STEP,
    )
    blocks = [swap(b, "tp", (m,)) if m else b for m, b in enumerate(blocks)]
    far = pl.BlockSpec(memory_space=pltpu.HBM)
    prev_hot, prev_here, own_hot = call(
        functools.partial(hots_body, own, tp_count, share_count, height, core_at),
        [like(2 * rows, vocab, BF), like(2 * rows, vocab // 2, BF), like(rows, vocab, BF)],
        [ids_own, ids_other],
        [blocks[0]],
    )

    def by_slot(value):
        return [value[:, j * slot : (j + 1) * slot] for j in range(own)]

    (slot_in,) = call(
        functools.partial(place_body, own, core_at),
        [like(2 * rows, slot, BF)],
        [global_out, out_other],
        [prev_hot],
    )
    u_rows = times(slot_in, proj_weight) + times(prev_hot, emb_local)
    scale = lax.rsqrt(jnp.mean(u_rows * u_rows, axis=1, keepdims=True) + 1e-05)
    normed = u_rows * scale
    r_rows = (normed * norm_gain).astype(BF)
    (up_here,) = call(
        functools.partial(pick_up_body, tp_count, share_count),
        [like(width, hidden // 2, BF)],
        [up_weight],
        [r_rows],
        in_specs=[far],
        scratch=[VMEM((share_count, width, chunk), BF), pltpu.SemaphoreType.DMA((share_count,))],
    )
    a_rows = times(r_rows, up_here)
    sig = jax.nn.sigmoid(a_rows)
    h_rows = (a_rows * sig).astype(BF)
    slope = (sig * (1.0 + a_rows * (1.0 - sig))).astype(BF)
    h_rows, slope = lax.optimization_barrier((h_rows, slope))
    (down_here,) = call(
        functools.partial(pick_down_body, tp_count, share_count),
        [like(hidden // 2, width, BF)],
        [down_weight],
        [h_rows],
        in_specs=[far],
        scratch=[pltpu.SemaphoreType.DMA((share_count, tp_count))],
    )
    strip = chunk // 2
    h_rows = jnp.concatenate(
        [
            h_rows[:, (z * share_count + n) * strip : (z * share_count + n + 1) * strip]
            for n in range(share_count)
            for z in range(2)
        ],
        axis=1,
    )

    (grad_own,) = call(
        functools.partial(join_body, part, own, tp_count),
        [like(rows, width, BF)],
        blocks,
        [h_rows],
    )
    grad_other = core_swap(grad_own)
    own_hot = gate(own_hot, [grad_own])
    glob = [
        inner(own_hot[j * patches : (j + 1) * patches], value)
        for j, value in enumerate(by_slot(global_in_grad))
    ]
    glob = sum(glob[1:], glob[0])
    glob_sent = glob[vocab // 2 :].astype(BF)
    glob_kept = glob[: vocab // 2].astype(BF)
    glob_more = core_swap(glob_sent)

    (out_rows,) = call(
        functools.partial(place_body, 1, core_at),
        [like(2 * rows, width, BF)],
        [grad_own, grad_other],
        [glob_kept],
    )

    seq_steps = [("seq", k) for k in range(stages)]
    tp_steps = [("tp", k) for k in range(levels)]

    step = functools.partial(call, flops=STEP)

    class Chain:
        def __init__(self, kept, sent, steps):
            self.kept, self.steps, self.at = kept, steps, 0
            self.arrived = go(sent, self.steps[0])
            self.left = len(self.steps) - 2

        def next(self, after):
            self.at += 1
            self.left -= 1
            rows, columns = self.kept.shape
            ins = [self.kept, self.arrived]
            outs = [like(rows // 2, columns, self.kept.dtype)] * 2
            self.kept, sent = step(add_body, outs, ins, after)
            self.arrived = go(sent, self.steps[self.at])
            return self.kept

    class Table:
        def __init__(self, kept, sent):
            self.kept, self.at = kept, 0
            self.plan = (
                [("half", s) for s in seq_steps]
                + [("sum", s) for s in tp_steps]
                + [("join", s) for s in reversed(seq_steps)]
                + [("join", None)]
            )
            self.left = len(self.plan) - 1
            self.arrived = go(sent, self.plan[0][1])

        def next(self, after):
            last, (kind, hop) = self.plan[self.at][0], self.plan[self.at + 1]
            rows, columns = self.kept.shape
            ins = [self.kept, self.arrived]
            if last == "half" and kind == "half":
                self.kept, sent = step(add_body, [like(rows // 2, columns, BF)] * 2, ins, after)
            elif last == "join":
                cut = columns // PARTS if hop is None else columns
                outs = [like(2 * rows, cut, BF)] * (columns // cut)
                self.parts = step(stack_body, outs, ins, after)
                self.kept = sent = self.parts[0]
            else:
                (self.kept,) = step(sum_body, [like(rows, columns, BF)], ins, after)
                sent = self.kept
            self.at += 1
            self.left -= 1
            if hop is None:
                self.arrived = [core_swap(part) for part in self.parts]
            else:
                self.arrived = go(sent, hop)
            return self.kept

    dh_rows = outer(out_rows, down_here)
    da_rows = (dh_rows * slope.astype(F32)).astype(BF)
    dr_part = outer(da_rows, up_here)
    dr_sent = dr_part.astype(BF)
    kind = BF if chunk // tp_count % 16 == 0 else F32
    half = h_rows.shape[1] // 2
    down_kept = inner(h_rows[:, :half], out_rows).astype(kind)
    down_sent = inner(h_rows[:, half:], out_rows).astype(kind)
    up_kept = inner(da_rows[:, :half], r_rows).astype(kind)
    up_sent = inner(da_rows[:, half:], r_rows).astype(kind)
    down = Chain(down_kept, down_sent, seq_steps + tp_steps)
    up = Chain(up_kept, up_sent, tp_steps[:1] + seq_steps + tp_steps[1:])
    dr_more = gate(core_swap(dr_sent), [down_sent, up_sent])
    dr_rows = dr_part + dr_more.astype(F32)

    gain_part = jnp.sum(dr_rows * normed, axis=0, keepdims=True)
    dn_rows = dr_rows * norm_gain
    du_rows = (
        out_rows.astype(F32)
        + scale * (dn_rows - normed * jnp.mean(dn_rows * normed, axis=1, keepdims=True))
    ).astype(BF)
    size = 2 * height
    kept, sent = call(
        functools.partial(tables_in_body, share_count, tp_count, height),
        [like(share_count // 2 * size, width + 128, BF)] * 2,
        [glob_kept, glob_more, inner(prev_here, du_rows), gain_part],
        [up.kept],
    )
    table = Table(kept, sent)
    share = width // seq_count
    kind = BF if share // tp_count % 16 == 0 else F32
    du_here = jnp.concatenate(
        [lax.dynamic_slice_in_dim(du_rows, s * share, share, 1) for s in shares], axis=1
    )
    value = inner(du_here, slot_in)
    kept, sent = call(
        functools.partial(split_body, tp_count, share),
        [like(value.shape[0] // 2, slot, kind)] * 2,
        [value],
        [table.kept],
    )
    proj = Chain(kept, sent, seq_steps[:1] + tp_steps[:1] + seq_steps[1:] + tp_steps[1:])
    du_own = lax.dynamic_slice_in_dim(du_rows, core * rows, rows, 0)
    back = outer(du_own, proj_weight).astype(BF)
    glob_out_grad = jnp.concatenate(
        [back[j * patches : (j + 1) * patches] for j in range(own)], axis=1
    )

    last = [up.kept, proj.kept, table.kept, down.kept, glob_out_grad]
    names = {"T": table, "D": down, "U": up, "P": proj}
    ends = [down, up, proj]
    heights = [c.kept.shape[0] >> c.left + 1 for c in ends]
    merged = None

    def last_sums(after):
        kind = down.kept.dtype if down.kept.dtype == proj.kept.dtype else F32
        keep, sent = step(
            last_body,
            [like(sum(heights), width, kind)] * 2,
            [x for c in ends for x in (c.kept, c.arrived)],
            after,
        )
        return keep, go(sent, tp_steps[-1])

    for name in ORDER:
        chain = names.get(name)
        if chain is not None and chain.left:
            last = [chain.next(last)]
        elif name == "F":
            while any(c.left for c in ends):
                for c in ends:
                    if c.left:
                        last = [c.next(last)]
            merged = last_sums(last)
            last = [merged[0]]
    while table.left:
        last = [table.next(last)]

    lines = width // 128
    emb_global_grad, emb_local_grad, gain_grad = call(
        functools.partial(tables_body, share_count, tp_count, height, PARTS),
        [like(vocab, width, F32), like(vocab, width, F32), like(lines, 128, F32)],
        [*table.parts, *table.arrived],
        last,
    )
    down_grad, up_grad, proj_grad = call(
        finals_body,
        [like(h, width, F32) for h in heights],
        [*merged],
        [gain_grad],
    )
    return (
        glob_out_grad,
        emb_global_grad,
        emb_local_grad,
        gain_grad.reshape(width),
        proj_grad.T,
        up_grad.T,
        down_grad,
    )


def solution(mesh):
    placed = (
        P("seq", None),
        P("seq", "tp"),
        P("seq", "tp"),
        P(("seq", "tp"), None),
        P(),
        P(),
        P(),
        P(),
        P(),
    )
    return jax.shard_map(
        on_device,
        mesh=mesh,
        in_specs=placed,
        out_specs=(
            P("seq", "tp"),
            P(),
            P(),
            P(),
            P(None, ("seq", "tp")),
            P(None, ("seq", "tp")),
            P(("seq", "tp"), None),
        ),
        check_vma=False,
    )
```

```python
import functools

import jax
import jax.numpy as jnp
from jax import lax
from jax.experimental import pallas as pl
from jax.experimental.pallas import tpu as pltpu
from jax.sharding import PartitionSpec as P

BF = jnp.bfloat16
F32 = jnp.float32
ROOM = 8 * 1024 * 1024
PARTS = 3
ORDER = "TDTUPTDUPTFTT"
STEP = 6 * 1000 * 1000 * 1000
VMEM = pltpu.VMEM


def inner(left, right):
    return lax.dot_general(
        left, right, (((0,), (0,)), ((), ())), preferred_element_type=F32
    )


def outer(left, right):
    return lax.dot_general(
        left, right, (((1,), (1,)), ((), ())), preferred_element_type=F32
    )


def times(left, right):
    return jnp.dot(left, right, preferred_element_type=F32)


def swap(value, axis, masks):
    count = lax.axis_size(axis)
    pairs = [(i, i ^ masks[i % len(masks)]) for i in range(count)]
    return lax.ppermute(value, axis, pairs)


def like(rows, columns, kind):
    return jax.ShapeDtypeStruct((rows, columns), kind)


def whole(array):
    return pl.BlockSpec(array.shape, lambda n, s: (0,) * len(array.shape))


def run(
    body, outs, ins, after, numbers, in_specs=None, out_specs=None, scratch=(), room=ROOM,
    alias=None, flops=0, grid=1,
):
    count, late = 1 + len(ins), len(after)

    def kernel(*refs):
        body(*refs[:count], *refs[count + late :])

    in_specs = in_specs or [None] * len(ins)
    out_specs = out_specs or [None] * len(outs)
    return pl.pallas_call(
        kernel,
        out_shape=tuple(outs),
        grid_spec=pltpu.PrefetchScalarGridSpec(
            num_scalar_prefetch=1,
            grid=(grid,),
            in_specs=[s or whole(a) for s, a in zip(in_specs, ins)]
            + [pl.BlockSpec(memory_space=pl.ANY)] * late,
            out_specs=tuple(s or whole(a) for s, a in zip(out_specs, outs)),
            scratch_shapes=list(scratch),
        ),
        input_output_aliases=alias or {},
        compiler_params=pltpu.CompilerParams(vmem_limit_bytes=room),
        cost_estimate=pl.CostEstimate(flops=flops, bytes_accessed=0, transcendentals=0),
    )(numbers, *ins, *after)


def sort_body(patch, part, own, numbers, grad, *blocks):
    size = own * part
    row = lax.broadcasted_iota(jnp.int32, (size, grad.shape[0]), 0)
    source = lax.broadcasted_iota(jnp.int32, (size, grad.shape[0]), 1)
    for m, block in enumerate(blocks):
        wanted = (row % part) * patch + numbers[m] * own + row // part
        block[...] = times((source == wanted).astype(BF), grad[...]).astype(BF)


def join_body(part, own, count, numbers, *refs):
    blocks, joined = refs[:-1], refs[-1]
    for m, block in enumerate(blocks):
        for j in range(own):
            start = pl.multiple_of((j * count + numbers[m]) * part, part)
            joined[pl.ds(start, part), :] = block[j * part : (j + 1) * part, :]


def sent_order(count):
    return sorted(range(count), key=lambda m: bin(m + count)[:2:-1])


def id_of(ids, place):
    lane = lax.broadcasted_iota(jnp.int32, ids.shape, 1)
    return jnp.sum(jnp.where(lane == place, ids + 1, 0), axis=1, keepdims=True) - 1


def vocab_line(numbers, first, count, height):
    lane = lax.broadcasted_iota(jnp.int32, (1, count * height), 1)
    line = lane % height
    for n in range(count):
        line = line + jnp.where(lane // height == n, numbers[first + n] * height, 0)
    return line


def hot(ids, line):
    return jnp.where(ids == line, 1.0, 0.0).astype(BF)


def place_body(own, core_at, numbers, mine, other, both):
    patches, width = mine.shape[0], mine.shape[1] // own
    rows = own * patches
    for side, value in ((numbers[core_at], mine), (1 - numbers[core_at], other)):
        for j in range(own):
            start = pl.multiple_of(side * rows + j * patches, patches)
            both[pl.ds(start, patches), :] = value[:, j * width : (j + 1) * width]


def hots_body(own, tp_count, share_count, height, core_at, numbers, ids_own, ids_other, prev, here, mine):
    patches = ids_own.shape[1]
    plain = lax.broadcasted_iota(jnp.int32, (1, prev.shape[1]), 1)
    line = vocab_line(numbers, tp_count, share_count, height)
    both = vocab_line(numbers, tp_count, 2 * share_count, height)
    core = numbers[core_at]
    for side, which in ((core, ids_own), (1 - core, ids_other)):
        ids = which[...].T
        for j in range(own):
            start = pl.multiple_of(side * own * patches + j * patches, patches)
            at = pl.ds(start, patches)
            before = id_of(ids, numbers[0] * own + j - 1)
            prev[at, :] = hot(before, plain)
            here[at, :] = hot(before, line)
            if which is ids_own:
                wanted = id_of(ids, numbers[0] * own + j)
                mine[j * patches : (j + 1) * patches, :] = hot(wanted, both)


def turn_matrix(tp_count, chunk, numbers):
    unit = chunk // tp_count
    row = lax.broadcasted_iota(jnp.int32, (chunk, chunk), 0)
    column = lax.broadcasted_iota(jnp.int32, (chunk, chunk), 1)
    source = column % unit
    for i, m in enumerate(sent_order(tp_count)):
        source = source + jnp.where(column // unit == i, numbers[m] * unit, 0)
    return (row == source).astype(BF)


def pick_up_body(tp_count, share_count, numbers, up, up_here, ups, ready):
    chunk = ups.shape[2]
    half = chunk // 2
    copies = []
    for n in range(share_count):
        at = pl.ds(pl.multiple_of(numbers[tp_count + n] * chunk, chunk), chunk)
        copies.append(pltpu.make_async_copy(up.at[:, at], ups.at[n], ready.at[n]))
        copies[-1].start()
    turn = turn_matrix(tp_count, chunk, numbers)
    for n in range(share_count):
        copies[n].wait()
        value = times(ups[n], turn).astype(BF)
        for z in range(2):
            first = (z * share_count + n) * half
            up_here[:, first : first + half] = value[:, z * half : (z + 1) * half]


def pick_down_body(tp_count, share_count, numbers, down, down_here, downs, ready):
    chunk = downs.shape[1]
    unit = chunk // tp_count
    half = chunk // 2
    copies = []
    for n in range(share_count):
        at = pl.ds(pl.multiple_of(numbers[tp_count + n] * chunk, chunk), chunk)
        copies.append(pltpu.make_async_copy(down.at[at, :], downs.at[n], ready.at[n]))
        copies[-1].start()
    for n in range(share_count):
        copies[n].wait()
        for i, m in enumerate(sent_order(tp_count)):
            z, place = i // (tp_count // 2), i % (tp_count // 2)
            first = (z * share_count + n) * half + place * unit
            start = pl.multiple_of(numbers[m] * unit, unit)
            down_here[first : first + unit, :] = downs[n, pl.ds(start, unit), :]


def split_body(tp_count, share, numbers, value, kept, sent):
    unit = share // tp_count
    half = kept.shape[0]
    inner_shares = value.shape[0] // share // 2
    inner_places = tp_count // 2
    for n in range(2 * inner_shares):
        for i, m in enumerate(sent_order(tp_count)):
            at = pl.ds(n * share + pl.multiple_of(numbers[m] * unit, unit), unit)
            place = 2 * (n // inner_shares) + i // inner_places
            place = place * inner_shares + n % inner_shares
            place = (place * inner_places + i % inner_places) * unit
            target = kept if place < half else sent
            row = place % half
            target[row : row + unit, :] = value[at, :].astype(target.dtype)


def tables_in_body(
    share_count, first_share, height, numbers, glob, glob_more, local, gains, kept, sent
):
    width = glob.shape[1]
    strip = width // (2 * share_count)
    lines = width // 128
    lane = lax.broadcasted_iota(jnp.int32, (1, width), 1)
    both = glob[...].astype(F32) + glob_more[...].astype(F32)
    size = 2 * height
    kept[:, width:] = jnp.zeros((kept.shape[0], 128), BF)
    sent[:, width:] = jnp.zeros((sent.shape[0], 128), BF)
    for n in range(share_count):
        target = kept if n < share_count // 2 else sent
        first = (n % (share_count // 2)) * size
        at = slice(n * height, (n + 1) * height)
        target[first : first + height, :width] = both[at, :].astype(BF)
        target[first + height : first + size, :width] = local[at, :].astype(BF)
        mine = jnp.where(lane // strip == numbers[first_share + n], gains[...], 0.0)
        rows = [mine[:, i * 128 : (i + 1) * 128] for i in range(lines)]
        rows.append(jnp.zeros((16 - lines, 128), F32))
        target[first : first + 16, width:] = jnp.concatenate(rows, axis=0).astype(BF)


def gate_body(numbers, value, same):
    pass


def add_body(numbers, kept, arrived, keep, send):
    half = keep.shape[0]
    keep[...] = (kept[:half, :].astype(F32) + arrived[:half, :].astype(F32)).astype(keep.dtype)
    send[...] = (kept[half:, :].astype(F32) + arrived[half:, :].astype(F32)).astype(send.dtype)


def sum_body(numbers, kept, arrived, summed):
    summed[...] = (kept[...].astype(F32) + arrived[...].astype(F32)).astype(summed.dtype)


def stack_body(count, numbers, *refs):
    firsts, seconds, parts = refs[:count], refs[count : 2 * count], refs[2 * count :]
    column = 0
    for i, part in enumerate(parts):
        first, second = firsts[min(i, count - 1)], seconds[min(i, count - 1)]
        at = slice(column, column + part.shape[1])
        rows = first.shape[0]
        part[:rows, :] = first[:, at]
        part[rows:, :] = second[:, at]
        if count == 1:
            column += part.shape[1]


def tables_body(share_count, first_share, height, count, numbers, *refs):
    sides = (refs[:count], refs[count : 2 * count])
    glob, local, gain = refs[2 * count :]
    width = glob.shape[1]
    gains = None
    for side, parts in enumerate(sides):
        for n in range(share_count):
            start = numbers[first_share + side * share_count + n] * height
            at = pl.ds(pl.multiple_of(start, height), height)
            row = 2 * n * height
            column = 0
            for part in parts:
                inside = min(part.shape[1], width - column)
                to = slice(column, column + inside)
                glob[at, to] = part[row : row + height, :inside].astype(F32)
                local[at, to] = part[row + height : row + 2 * height, :inside].astype(F32)
                column += inside
            term = parts[-1][row : row + 16, parts[-1].shape[1] - 128 :].astype(F32)
            gains = term if gains is None else gains + term
    gain[...] = gains[: gain.shape[0]]


def last_body(numbers, *refs):
    keep, send = refs[-2:]
    row = 0
    for i in range(len(refs) // 2 - 1):
        kept, arrived = refs[2 * i], refs[2 * i + 1]
        half = kept.shape[0] // 2
        at = slice(row, row + half)
        for target, part in ((keep, slice(0, half)), (send, slice(half, 2 * half))):
            value = kept[part, :].astype(F32) + arrived[part, :].astype(F32)
            target[at, :] = value.astype(target.dtype)
        row += half


def finals_body(numbers, kept, arrived, *wholes):
    row = 0
    for whole in wholes:
        at = slice(row, row + whole.shape[0])
        whole[...] = kept[at, :].astype(F32) + arrived[at, :].astype(F32)
        row += whole.shape[0]


def on_device(
    byte_ids,
    global_out,
    global_in_grad,
    out_grad,
    proj_weight,
    emb_local,
    norm_gain,
    up_weight,
    down_weight,
):
    seq_count = lax.axis_size("seq")
    tp_count = lax.axis_size("tp")
    seq_place = lax.axis_index("seq")
    tp_place = lax.axis_index("tp")
    core = seq_place & 1
    chip = seq_place >> 1
    stages = seq_count.bit_length() - 2
    levels = tp_count.bit_length() - 1
    share_count = 1 << stages
    walks = (list(range(1, stages + 1)), list(range(stages, 0, -1)))
    patches, patch = byte_ids.shape
    slot, width = proj_weight.shape
    hidden = up_weight.shape[1]
    vocab = emb_local.shape[0]
    own = patch // tp_count
    part = patches // tp_count
    rows = own * patches
    height = vocab // seq_count
    chunk = hidden // seq_count

    def share_mask(number, walk):
        mask = 0
        for k in range(stages):
            if (number >> (stages - 1 - k)) & 1:
                mask |= 1 << (walk[k] - 1)
        return mask

    def shares_of(which):
        return [
            2 * (chip ^ jnp.where(which == 0, share_mask(n, walks[0]), share_mask(n, walks[1])))
            + which
            for n in range(share_count)
        ]

    shares = shares_of(core)
    others = shares_of(1 - core)
    near = [tp_place ^ m for m in range(tp_count)]
    numbers = jnp.stack(near + shares + others + [core]).astype(jnp.int32)
    core_at = tp_count + 2 * share_count
    call = functools.partial(run, numbers=numbers)

    def core_swap(value):
        return swap(value, "seq", (1,))

    def go(value, step):
        kind, k = step
        if kind == "seq":
            return swap(value, "seq", (1 << walks[0][k], 1 << walks[1][k]))
        return swap(value, "tp", (1 << k,))

    def gate(value, after):
        there = pl.BlockSpec(memory_space=pl.ANY)
        (value,) = call(
            gate_body,
            [like(*value.shape, value.dtype)],
            [value],
            after,
            in_specs=[there],
            out_specs=[there],
            alias={1: 0},
        )
        return value

    ids_own = byte_ids.T
    ids_other = core_swap(ids_own)
    out_other = core_swap(global_out)
    blocks = call(
        functools.partial(sort_body, patch, part, own),
        [like(own * part, width, BF)] * tp_count,
        [out_grad],
        [],
        flops=STEP,
    )
    blocks = [swap(b, "tp", (m,)) if m else b for m, b in enumerate(blocks)]
    far = pl.BlockSpec(memory_space=pltpu.HBM)
    prev_hot, prev_here, own_hot = call(
        functools.partial(hots_body, own, tp_count, share_count, height, core_at),
        [like(2 * rows, vocab, BF), like(2 * rows, vocab // 2, BF), like(rows, vocab, BF)],
        [ids_own, ids_other],
        [blocks[0]],
    )

    def by_slot(value):
        return [value[:, j * slot : (j + 1) * slot] for j in range(own)]

    (slot_in,) = call(
        functools.partial(place_body, own, core_at),
        [like(2 * rows, slot, BF)],
        [global_out, out_other],
        [prev_hot],
    )
    u_rows = times(slot_in, proj_weight) + times(prev_hot, emb_local)
    scale = lax.rsqrt(jnp.mean(u_rows * u_rows, axis=1, keepdims=True) + 1e-05)
    normed = u_rows * scale
    r_rows = (normed * norm_gain).astype(BF)
    (up_here,) = call(
        functools.partial(pick_up_body, tp_count, share_count),
        [like(width, hidden // 2, BF)],
        [up_weight],
        [r_rows],
        in_specs=[far],
        scratch=[VMEM((share_count, width, chunk), BF), pltpu.SemaphoreType.DMA((share_count,))],
    )
    a_rows = times(r_rows, up_here)
    sig = jax.nn.sigmoid(a_rows)
    h_rows = (a_rows * sig).astype(BF)
    slope = (sig * (1.0 + a_rows * (1.0 - sig))).astype(BF)
    h_rows, slope = lax.optimization_barrier((h_rows, slope))
    (down_here,) = call(
        functools.partial(pick_down_body, tp_count, share_count),
        [like(hidden // 2, width, BF)],
        [down_weight],
        [h_rows],
        in_specs=[far],
        scratch=[VMEM((share_count, chunk, width), BF), pltpu.SemaphoreType.DMA((share_count,))],
    )
    strip = chunk // 2
    h_rows = jnp.concatenate(
        [
            h_rows[:, (z * share_count + n) * strip : (z * share_count + n + 1) * strip]
            for n in range(share_count)
            for z in range(2)
        ],
        axis=1,
    )

    (grad_own,) = call(
        functools.partial(join_body, part, own, tp_count),
        [like(rows, width, BF)],
        blocks,
        [h_rows],
    )
    grad_other = core_swap(grad_own)
    own_hot = gate(own_hot, [grad_own])
    glob = [
        inner(own_hot[j * patches : (j + 1) * patches], value)
        for j, value in enumerate(by_slot(global_in_grad))
    ]
    glob = sum(glob[1:], glob[0])
    glob_sent = glob[vocab // 2 :].astype(BF)
    glob_kept = glob[: vocab // 2].astype(BF)
    glob_more = core_swap(glob_sent)

    (out_rows,) = call(
        functools.partial(place_body, 1, core_at),
        [like(2 * rows, width, BF)],
        [grad_own, grad_other],
        [glob_kept],
    )

    seq_steps = [("seq", k) for k in range(stages)]
    tp_steps = [("tp", k) for k in range(levels)]

    step = functools.partial(call, flops=STEP)

    class Chain:
        def __init__(self, kept, sent, steps):
            self.kept, self.steps, self.at = kept, steps, 0
            self.arrived = go(sent, self.steps[0])
            self.left = len(self.steps) - 2

        def next(self, after):
            self.at += 1
            self.left -= 1
            rows, columns = self.kept.shape
            ins = [self.kept, self.arrived]
            outs = [like(rows // 2, columns, self.kept.dtype)] * 2
            self.kept, sent = step(add_body, outs, ins, after)
            self.arrived = go(sent, self.steps[self.at])
            return self.kept

    class Table:
        def __init__(self, kept, sent):
            self.kept, self.at = kept, 0
            self.plan = (
                [("half", s) for s in seq_steps]
                + [("sum", s) for s in tp_steps]
                + [("join", s) for s in reversed(seq_steps)]
                + [("join", None)]
            )
            self.left = len(self.plan) - 1
            self.arrived = go(sent, self.plan[0][1])

        def next(self, after):
            last, (kind, hop) = self.plan[self.at][0], self.plan[self.at + 1]
            rows, columns = self.kept.shape
            ins = [self.kept, self.arrived]
            if last == "half" and kind == "half":
                self.kept, sent = step(add_body, [like(rows // 2, columns, BF)] * 2, ins, after)
            elif last == "join":
                many = self.plan[self.at + 1 :]
                cut = columns if len(many) > 2 or len(self.parts) > 1 else columns // PARTS
                outs = [like(2 * rows, cut, BF)] * (PARTS if len(many) <= 2 else 1)
                body = functools.partial(stack_body, len(self.parts))
                build = step if len(many) > 2 else call
                self.parts = build(body, outs, [*self.parts, *self.arrived], after)
                self.kept = self.parts[0]
            else:
                (self.kept,) = step(sum_body, [like(rows, columns, BF)], ins, after)
                sent = self.kept
            self.at += 1
            self.left -= 1
            if kind == "join":
                if last != "join":
                    self.parts = [sent]
                self.arrived = [
                    core_swap(part) if hop is None else go(part, hop) for part in self.parts
                ]
            else:
                self.arrived = go(sent, hop)
            return self.kept

    dh_rows = outer(out_rows, down_here)
    da_rows = (dh_rows * slope.astype(F32)).astype(BF)
    dr_part = outer(da_rows, up_here)
    dr_sent = dr_part.astype(BF)
    kind = BF if chunk // tp_count % 16 == 0 else F32
    half = h_rows.shape[1] // 2
    down_kept = inner(h_rows[:, :half], out_rows).astype(kind)
    down_sent = inner(h_rows[:, half:], out_rows).astype(kind)
    up_kept = inner(da_rows[:, :half], r_rows).astype(kind)
    up_sent = inner(da_rows[:, half:], r_rows).astype(kind)
    down = Chain(down_kept, down_sent, seq_steps + tp_steps)
    up = Chain(up_kept, up_sent, tp_steps[:1] + seq_steps + tp_steps[1:])
    dr_more = gate(core_swap(dr_sent), [down_sent, up_sent])
    dr_rows = dr_part + dr_more.astype(F32)

    gain_part = jnp.sum(dr_rows * normed, axis=0, keepdims=True)
    dn_rows = dr_rows * norm_gain
    du_rows = (
        out_rows.astype(F32)
        + scale * (dn_rows - normed * jnp.mean(dn_rows * normed, axis=1, keepdims=True))
    ).astype(BF)
    size = 2 * height
    kept, sent = call(
        functools.partial(tables_in_body, share_count, tp_count, height),
        [like(share_count // 2 * size, width + 128, BF)] * 2,
        [glob_kept, glob_more, inner(prev_here, du_rows), gain_part],
        [up.kept],
    )
    table = Table(kept, sent)
    share = width // seq_count
    kind = BF if share // tp_count % 16 == 0 else F32
    du_here = jnp.concatenate(
        [lax.dynamic_slice_in_dim(du_rows, s * share, share, 1) for s in shares], axis=1
    )
    value = inner(du_here, slot_in)
    kept, sent = call(
        functools.partial(split_body, tp_count, share),
        [like(value.shape[0] // 2, slot, kind)] * 2,
        [value],
        [table.kept],
    )
    proj = Chain(kept, sent, seq_steps[:1] + tp_steps[:1] + seq_steps[1:] + tp_steps[1:])
    du_own = lax.dynamic_slice_in_dim(du_rows, core * rows, rows, 0)
    back = outer(du_own, proj_weight).astype(BF)
    glob_out_grad = jnp.concatenate(
        [back[j * patches : (j + 1) * patches] for j in range(own)], axis=1
    )

    last = [up.kept, proj.kept, table.kept, down.kept, glob_out_grad]
    names = {"T": table, "D": down, "U": up, "P": proj}
    ends = [down, up, proj]
    heights = [c.kept.shape[0] >> c.left + 1 for c in ends]
    merged = None

    def last_sums(after):
        kind = down.kept.dtype if down.kept.dtype == proj.kept.dtype else F32
        keep, sent = step(
            last_body,
            [like(sum(heights), width, kind)] * 2,
            [x for c in ends for x in (c.kept, c.arrived)],
            after,
        )
        return keep, go(sent, tp_steps[-1])

    for name in ORDER:
        chain = names.get(name)
        if chain is not None and chain.left:
            last = [chain.next(last)]
        elif name == "F":
            while any(c.left for c in ends):
                for c in ends:
                    if c.left:
                        last = [c.next(last)]
            merged = last_sums(last)
            last = [merged[0]]
    while table.left:
        last = [table.next(last)]

    lines = width // 128
    emb_global_grad, emb_local_grad, gain_grad = call(
        functools.partial(tables_body, share_count, tp_count, height, PARTS),
        [like(vocab, width, F32), like(vocab, width, F32), like(lines, 128, F32)],
        [*table.parts, *table.arrived],
        last,
    )
    down_grad, up_grad, proj_grad = call(
        finals_body,
        [like(h, width, F32) for h in heights],
        [*merged],
        [gain_grad],
    )
    return (
        glob_out_grad,
        emb_global_grad,
        emb_local_grad,
        gain_grad.reshape(width),
        proj_grad.T,
        up_grad.T,
        down_grad,
    )


def solution(mesh):
    placed = (
        P("seq", None),
        P("seq", "tp"),
        P("seq", "tp"),
        P(("seq", "tp"), None),
        P(),
        P(),
        P(),
        P(),
        P(),
    )
    return jax.shard_map(
        on_device,
        mesh=mesh,
        in_specs=placed,
        out_specs=(
            P("seq", "tp"),
            P(),
            P(),
            P(),
            P(None, ("seq", "tp")),
            P(None, ("seq", "tp")),
            P(("seq", "tp"), None),
        ),
        check_vma=False,
    )
```

```python
import functools

import jax
import jax.numpy as jnp
from jax import lax
from jax.experimental import pallas as pl
from jax.experimental.pallas import tpu as pltpu
from jax.sharding import PartitionSpec as P

BF = jnp.bfloat16
F32 = jnp.float32
ROOM = 8 * 1024 * 1024
PARTS = 3
ORDER = "TDTUPTDUPTFTT"
STEP = 6 * 1000 * 1000 * 1000
VMEM = pltpu.VMEM


def inner(left, right):
    return lax.dot_general(
        left, right, (((0,), (0,)), ((), ())), preferred_element_type=F32
    )


def outer(left, right):
    return lax.dot_general(
        left, right, (((1,), (1,)), ((), ())), preferred_element_type=F32
    )


def times(left, right):
    return jnp.dot(left, right, preferred_element_type=F32)


def swap(value, axis, masks):
    count = lax.axis_size(axis)
    pairs = [(i, i ^ masks[i % len(masks)]) for i in range(count)]
    return lax.ppermute(value, axis, pairs)


def like(rows, columns, kind):
    return jax.ShapeDtypeStruct((rows, columns), kind)


def whole(array):
    return pl.BlockSpec(array.shape, lambda n, s: (0,) * len(array.shape))


def run(
    body, outs, ins, after, numbers, in_specs=None, out_specs=None, scratch=(), room=ROOM,
    alias=None, flops=0, grid=1,
):
    count, late = 1 + len(ins), len(after)

    def kernel(*refs):
        body(*refs[:count], *refs[count + late :])

    in_specs = in_specs or [None] * len(ins)
    out_specs = out_specs or [None] * len(outs)
    return pl.pallas_call(
        kernel,
        out_shape=tuple(outs),
        grid_spec=pltpu.PrefetchScalarGridSpec(
            num_scalar_prefetch=1,
            grid=(grid,),
            in_specs=[s or whole(a) for s, a in zip(in_specs, ins)]
            + [pl.BlockSpec(memory_space=pl.ANY)] * late,
            out_specs=tuple(s or whole(a) for s, a in zip(out_specs, outs)),
            scratch_shapes=list(scratch),
        ),
        input_output_aliases=alias or {},
        compiler_params=pltpu.CompilerParams(vmem_limit_bytes=room),
        cost_estimate=pl.CostEstimate(flops=flops, bytes_accessed=0, transcendentals=0),
    )(numbers, *ins, *after)


def sort_body(patch, part, own, masks, numbers, grad, *blocks):
    size = own * part
    row = lax.broadcasted_iota(jnp.int32, (size, grad.shape[0]), 0)
    source = lax.broadcasted_iota(jnp.int32, (size, grad.shape[0]), 1)
    for m, block in zip(masks, blocks):
        wanted = (row % part) * patch + numbers[m] * own + row // part
        block[...] = times((source == wanted).astype(BF), grad[...]).astype(BF)


def join_body(part, own, count, share_count, height, numbers, ids_own, *refs):
    blocks, joined, mine = refs[:-2], refs[-2], refs[-1]
    for m, block in enumerate(blocks):
        for j in range(own):
            start = pl.multiple_of((j * count + numbers[m]) * part, part)
            joined[pl.ds(start, part), :] = block[j * part : (j + 1) * part, :]
    line = vocab_line(numbers, count, 2 * share_count, height)
    ids = ids_own[...].T
    patches = ids.shape[0]
    for j in range(own):
        wanted = id_of(ids, numbers[0] * own + j)
        mine[j * patches : (j + 1) * patches, :] = hot(wanted, line)


def sent_order(count):
    return sorted(range(count), key=lambda m: bin(m + count)[:2:-1])


def id_of(ids, place):
    lane = lax.broadcasted_iota(jnp.int32, ids.shape, 1)
    return jnp.sum(jnp.where(lane == place, ids + 1, 0), axis=1, keepdims=True) - 1


def vocab_line(numbers, first, count, height):
    lane = lax.broadcasted_iota(jnp.int32, (1, count * height), 1)
    line = lane % height
    for n in range(count):
        line = line + jnp.where(lane // height == n, numbers[first + n] * height, 0)
    return line


def hot(ids, line):
    return jnp.where(ids == line, 1.0, 0.0).astype(BF)


def place_body(own, core_at, numbers, mine, other, both):
    patches, width = mine.shape[0], mine.shape[1] // own
    rows = own * patches
    for side, value in ((numbers[core_at], mine), (1 - numbers[core_at], other)):
        for j in range(own):
            start = pl.multiple_of(side * rows + j * patches, patches)
            both[pl.ds(start, patches), :] = value[:, j * width : (j + 1) * width]


def hots_body(own, tp_count, share_count, height, core_at, numbers, ids_own, ids_other, prev, here):
    patches = ids_own.shape[1]
    plain = lax.broadcasted_iota(jnp.int32, (1, prev.shape[1]), 1)
    line = vocab_line(numbers, tp_count, share_count, height)
    core = numbers[core_at]
    for side, which in ((core, ids_own), (1 - core, ids_other)):
        ids = which[...].T
        for j in range(own):
            start = pl.multiple_of(side * own * patches + j * patches, patches)
            at = pl.ds(start, patches)
            before = id_of(ids, numbers[0] * own + j - 1)
            prev[at, :] = hot(before, plain)
            here[at, :] = hot(before, line)


def turn_matrix(tp_count, chunk, numbers):
    unit = chunk // tp_count
    row = lax.broadcasted_iota(jnp.int32, (chunk, chunk), 0)
    column = lax.broadcasted_iota(jnp.int32, (chunk, chunk), 1)
    source = column % unit
    for i, m in enumerate(sent_order(tp_count)):
        source = source + jnp.where(column // unit == i, numbers[m] * unit, 0)
    return (row == source).astype(BF)


def pick_up_body(tp_count, share_count, numbers, up, up_here, ups, ready):
    chunk = ups.shape[2]
    half = chunk // 2
    copies = []
    for n in range(share_count):
        at = pl.ds(pl.multiple_of(numbers[tp_count + n] * chunk, chunk), chunk)
        copies.append(pltpu.make_async_copy(up.at[:, at], ups.at[n], ready.at[n]))
        copies[-1].start()
    turn = turn_matrix(tp_count, chunk, numbers)
    for n in range(share_count):
        copies[n].wait()
        value = times(ups[n], turn).astype(BF)
        for z in range(2):
            first = (z * share_count + n) * half
            up_here[:, first : first + half] = value[:, z * half : (z + 1) * half]


def pick_down_body(tp_count, share_count, numbers, down, down_here, downs, ready):
    chunk = downs.shape[1]
    unit = chunk // tp_count
    half = chunk // 2
    copies = []
    for n in range(share_count):
        at = pl.ds(pl.multiple_of(numbers[tp_count + n] * chunk, chunk), chunk)
        copies.append(pltpu.make_async_copy(down.at[at, :], downs.at[n], ready.at[n]))
        copies[-1].start()
    for n in range(share_count):
        copies[n].wait()
        for i, m in enumerate(sent_order(tp_count)):
            z, place = i // (tp_count // 2), i % (tp_count // 2)
            first = (z * share_count + n) * half + place * unit
            start = pl.multiple_of(numbers[m] * unit, unit)
            down_here[first : first + unit, :] = downs[n, pl.ds(start, unit), :]


def split_body(tp_count, share, numbers, value, kept, sent):
    unit = share // tp_count
    half = kept.shape[0]
    inner_shares = value.shape[0] // share // 2
    inner_places = tp_count // 2
    for n in range(2 * inner_shares):
        for i, m in enumerate(sent_order(tp_count)):
            at = pl.ds(n * share + pl.multiple_of(numbers[m] * unit, unit), unit)
            place = 2 * (n // inner_shares) + i // inner_places
            place = place * inner_shares + n % inner_shares
            place = (place * inner_places + i % inner_places) * unit
            target = kept if place < half else sent
            row = place % half
            target[row : row + unit, :] = value[at, :].astype(target.dtype)


def tables_in_body(
    share_count, first_share, height, numbers, glob, glob_more, local, gains, kept, sent
):
    width = glob.shape[1]
    strip = width // (2 * share_count)
    lines = width // 128
    lane = lax.broadcasted_iota(jnp.int32, (1, width), 1)
    both = glob[...].astype(F32) + glob_more[...].astype(F32)
    size = 2 * height
    kept[:, width:] = jnp.zeros((kept.shape[0], 128), BF)
    sent[:, width:] = jnp.zeros((sent.shape[0], 128), BF)
    for n in range(share_count):
        target = kept if n < share_count // 2 else sent
        first = (n % (share_count // 2)) * size
        at = slice(n * height, (n + 1) * height)
        target[first : first + height, :width] = both[at, :].astype(BF)
        target[first + height : first + size, :width] = local[at, :].astype(BF)
        mine = jnp.where(lane // strip == numbers[first_share + n], gains[...], 0.0)
        rows = [mine[:, i * 128 : (i + 1) * 128] for i in range(lines)]
        rows.append(jnp.zeros((16 - lines, 128), F32))
        target[first : first + 16, width:] = jnp.concatenate(rows, axis=0).astype(BF)


def add_body(numbers, kept, arrived, keep, send):
    half = keep.shape[0]
    keep[...] = (kept[:half, :].astype(F32) + arrived[:half, :].astype(F32)).astype(keep.dtype)
    send[...] = (kept[half:, :].astype(F32) + arrived[half:, :].astype(F32)).astype(send.dtype)


def sum_body(numbers, kept, arrived, summed):
    summed[...] = (kept[...].astype(F32) + arrived[...].astype(F32)).astype(summed.dtype)


def stack_body(count, numbers, *refs):
    firsts, seconds, parts = refs[:count], refs[count : 2 * count], refs[2 * count :]
    column = 0
    for i, part in enumerate(parts):
        first, second = firsts[min(i, count - 1)], seconds[min(i, count - 1)]
        at = slice(column, column + part.shape[1])
        rows = first.shape[0]
        part[:rows, :] = first[:, at]
        part[rows:, :] = second[:, at]
        if count == 1:
            column += part.shape[1]


def tables_body(share_count, first_share, height, count, numbers, *refs):
    sides = (refs[:count], refs[count : 2 * count])
    glob, local, gain = refs[2 * count :]
    width = glob.shape[1]
    gains = None
    for side, parts in enumerate(sides):
        for n in range(share_count):
            start = numbers[first_share + side * share_count + n] * height
            at = pl.ds(pl.multiple_of(start, height), height)
            row = 2 * n * height
            column = 0
            for part in parts:
                inside = min(part.shape[1], width - column)
                to = slice(column, column + inside)
                glob[at, to] = part[row : row + height, :inside].astype(F32)
                local[at, to] = part[row + height : row + 2 * height, :inside].astype(F32)
                column += inside
            term = parts[-1][row : row + 16, parts[-1].shape[1] - 128 :].astype(F32)
            gains = term if gains is None else gains + term
    gain[...] = gains[: gain.shape[0]]


def last_body(numbers, *refs):
    keep, send = refs[-2:]
    row = 0
    for i in range(len(refs) // 2 - 1):
        kept, arrived = refs[2 * i], refs[2 * i + 1]
        half = kept.shape[0] // 2
        at = slice(row, row + half)
        for target, part in ((keep, slice(0, half)), (send, slice(half, 2 * half))):
            value = kept[part, :].astype(F32) + arrived[part, :].astype(F32)
            target[at, :] = value.astype(target.dtype)
        row += half


def finals_body(numbers, kept, arrived, *wholes):
    row = 0
    for whole in wholes:
        at = slice(row, row + whole.shape[0])
        whole[...] = kept[at, :].astype(F32) + arrived[at, :].astype(F32)
        row += whole.shape[0]


def on_device(
    byte_ids,
    global_out,
    global_in_grad,
    out_grad,
    proj_weight,
    emb_local,
    norm_gain,
    up_weight,
    down_weight,
):
    seq_count = lax.axis_size("seq")
    tp_count = lax.axis_size("tp")
    seq_place = lax.axis_index("seq")
    tp_place = lax.axis_index("tp")
    core = seq_place & 1
    chip = seq_place >> 1
    stages = seq_count.bit_length() - 2
    levels = tp_count.bit_length() - 1
    share_count = 1 << stages
    walks = (list(range(1, stages + 1)), list(range(stages, 0, -1)))
    patches, patch = byte_ids.shape
    slot, width = proj_weight.shape
    hidden = up_weight.shape[1]
    vocab = emb_local.shape[0]
    own = patch // tp_count
    part = patches // tp_count
    rows = own * patches
    height = vocab // seq_count
    chunk = hidden // seq_count

    def share_mask(number, walk):
        mask = 0
        for k in range(stages):
            if (number >> (stages - 1 - k)) & 1:
                mask |= 1 << (walk[k] - 1)
        return mask

    def shares_of(which):
        return [
            2 * (chip ^ jnp.where(which == 0, share_mask(n, walks[0]), share_mask(n, walks[1])))
            + which
            for n in range(share_count)
        ]

    shares = shares_of(core)
    others = shares_of(1 - core)
    near = [tp_place ^ m for m in range(tp_count)]
    numbers = jnp.stack(near + shares + others + [core]).astype(jnp.int32)
    core_at = tp_count + 2 * share_count
    call = functools.partial(run, numbers=numbers)

    def core_swap(value):
        return swap(value, "seq", (1,))

    def go(value, step):
        kind, k = step
        if kind == "seq":
            return swap(value, "seq", (1 << walks[0][k], 1 << walks[1][k]))
        return swap(value, "tp", (1 << k,))

    ids_own = byte_ids.T
    ids_other = core_swap(ids_own)
    out_other = core_swap(global_out)
    blocks, first_rows = {}, []
    for masks in (list(range(2, tp_count)), [1, 0]):
        sorted_rows = call(
            functools.partial(sort_body, patch, part, own, masks),
            [like(own * part, width, BF)] * len(masks),
            [out_grad],
            first_rows,
            flops=STEP,
        )
        first_rows = sorted_rows[:1]
        for m, value in zip(masks, sorted_rows):
            blocks[m] = swap(value, "tp", (m,)) if m else value
    blocks = [blocks[m] for m in range(tp_count)]
    far = pl.BlockSpec(memory_space=pltpu.HBM)
    prev_hot, prev_here = call(
        functools.partial(hots_body, own, tp_count, share_count, height, core_at),
        [like(2 * rows, vocab, BF), like(2 * rows, vocab // 2, BF)],
        [ids_own, ids_other],
        [blocks[0]],
    )

    def by_slot(value):
        return [value[:, j * slot : (j + 1) * slot] for j in range(own)]

    (slot_in,) = call(
        functools.partial(place_body, own, core_at),
        [like(2 * rows, slot, BF)],
        [global_out, out_other],
        [prev_hot],
    )
    before = jnp.dot(prev_hot, emb_local, preferred_element_type=BF)
    u_rows = times(slot_in, proj_weight) + before.astype(F32)
    scale = lax.rsqrt(jnp.mean(u_rows * u_rows, axis=1, keepdims=True) + 1e-05)
    normed = u_rows * scale
    r_rows = (normed * norm_gain).astype(BF)
    (up_here,) = call(
        functools.partial(pick_up_body, tp_count, share_count),
        [like(width, hidden // 2, BF)],
        [up_weight],
        [r_rows],
        in_specs=[far],
        scratch=[VMEM((share_count, width, chunk), BF), pltpu.SemaphoreType.DMA((share_count,))],
    )
    grad_own, own_hot = call(
        functools.partial(join_body, part, own, tp_count, share_count, height),
        [like(rows, width, BF), like(rows, vocab, BF)],
        [ids_own, *blocks],
        [up_here],
        numbers=numbers,
    )
    up_later, _ = lax.optimization_barrier((up_here, grad_own))
    a_rows = times(r_rows, up_later)
    sig = jax.nn.sigmoid(a_rows)
    h_rows = (a_rows * sig).astype(BF)
    slope = (sig * (1.0 + a_rows * (1.0 - sig))).astype(BF)
    h_rows, slope = lax.optimization_barrier((h_rows, slope))
    (down_here,) = call(
        functools.partial(pick_down_body, tp_count, share_count),
        [like(hidden // 2, width, BF)],
        [down_weight],
        [h_rows],
        in_specs=[far],
        scratch=[VMEM((share_count, chunk, width), BF), pltpu.SemaphoreType.DMA((share_count,))],
    )
    strip = chunk // 2
    h_rows = jnp.concatenate(
        [
            h_rows[:, (z * share_count + n) * strip : (z * share_count + n + 1) * strip]
            for n in range(share_count)
            for z in range(2)
        ],
        axis=1,
    )

    grad_other = core_swap(grad_own)
    glob = [
        inner(own_hot[j * patches : (j + 1) * patches], value)
        for j, value in enumerate(by_slot(global_in_grad))
    ]
    glob = sum(glob[1:], glob[0])
    glob_sent = glob[vocab // 2 :].astype(BF)
    glob_kept = glob[: vocab // 2].astype(BF)
    glob_more = core_swap(glob_sent)

    (out_rows,) = call(
        functools.partial(place_body, 1, core_at),
        [like(2 * rows, width, BF)],
        [grad_own, grad_other],
        [glob_kept],
    )

    seq_steps = [("seq", k) for k in range(stages)]
    tp_steps = [("tp", k) for k in range(levels)]

    step = functools.partial(call, flops=STEP)

    class Chain:
        def __init__(self, kept, sent, steps):
            self.kept, self.steps, self.at = kept, steps, 0
            self.arrived = go(sent, self.steps[0])
            self.left = len(self.steps) - 2

        def next(self, after):
            self.at += 1
            self.left -= 1
            rows, columns = self.kept.shape
            ins = [self.kept, self.arrived]
            outs = [like(rows // 2, columns, self.kept.dtype)] * 2
            self.kept, sent = step(add_body, outs, ins, after)
            self.arrived = go(sent, self.steps[self.at])
            return self.kept

    class Table:
        def __init__(self, kept, sent):
            self.kept, self.at = kept, 0
            self.plan = (
                [("half", s) for s in seq_steps]
                + [("sum", s) for s in tp_steps]
                + [("join", s) for s in reversed(seq_steps)]
                + [("join", None)]
            )
            self.left = len(self.plan) - 1
            self.arrived = go(sent, self.plan[0][1])

        def next(self, after):
            last, (kind, hop) = self.plan[self.at][0], self.plan[self.at + 1]
            rows, columns = self.kept.shape
            ins = [self.kept, self.arrived]
            if last == "half" and kind == "half":
                self.kept, sent = step(add_body, [like(rows // 2, columns, BF)] * 2, ins, after)
            elif last == "join":
                many = self.plan[self.at + 1 :]
                cut = columns if len(many) > 2 or len(self.parts) > 1 else columns // PARTS
                outs = [like(2 * rows, cut, BF)] * (PARTS if len(many) <= 2 else 1)
                body = functools.partial(stack_body, len(self.parts))
                build = step if len(many) > 2 else call
                self.parts = build(body, outs, [*self.parts, *self.arrived], after)
                self.kept = self.parts[0]
            else:
                (self.kept,) = step(sum_body, [like(rows, columns, BF)], ins, after)
                sent = self.kept
            self.at += 1
            self.left -= 1
            if kind == "join":
                if last != "join":
                    self.parts = [sent]
                self.arrived = [
                    core_swap(part) if hop is None else go(part, hop) for part in self.parts
                ]
            else:
                self.arrived = go(sent, hop)
            return self.kept

    dh_rows = outer(out_rows, down_here)
    da_rows = (dh_rows * slope.astype(F32)).astype(BF)
    dr_part = outer(da_rows, up_here)
    dr_sent = dr_part.astype(BF)
    kind = BF if chunk // tp_count % 16 == 0 else F32
    half = h_rows.shape[1] // 2
    down_kept = inner(h_rows[:, :half], out_rows).astype(kind)
    down_sent = inner(h_rows[:, half:], out_rows).astype(kind)
    up_kept = inner(da_rows[:, :half], r_rows).astype(kind)
    up_sent = inner(da_rows[:, half:], r_rows).astype(kind)
    down = Chain(down_kept, down_sent, seq_steps + tp_steps)
    up = Chain(up_kept, up_sent, tp_steps[:1] + seq_steps + tp_steps[1:])
    dr_more = core_swap(dr_sent)
    dr_rows = dr_part + dr_more.astype(F32)

    gain_part = jnp.sum(dr_rows * normed, axis=0, keepdims=True)
    dn_rows = dr_rows * norm_gain
    du_rows = (
        out_rows.astype(F32)
        + scale * (dn_rows - normed * jnp.mean(dn_rows * normed, axis=1, keepdims=True))
    ).astype(BF)
    size = 2 * height
    kept, sent = call(
        functools.partial(tables_in_body, share_count, tp_count, height),
        [like(share_count // 2 * size, width + 128, BF)] * 2,
        [glob_kept, glob_more, inner(prev_here, du_rows), gain_part],
        [up.kept],
    )
    table = Table(kept, sent)
    share = width // seq_count
    kind = BF if share // tp_count % 16 == 0 else F32
    du_here = jnp.concatenate(
        [lax.dynamic_slice_in_dim(du_rows, s * share, share, 1) for s in shares], axis=1
    )
    value = inner(du_here, slot_in)
    kept, sent = call(
        functools.partial(split_body, tp_count, share),
        [like(value.shape[0] // 2, slot, kind)] * 2,
        [value],
        [table.kept],
    )
    proj = Chain(kept, sent, seq_steps[:1] + tp_steps[:1] + seq_steps[1:] + tp_steps[1:])
    du_later, _ = lax.optimization_barrier((du_rows, proj.kept))
    du_own = lax.dynamic_slice_in_dim(du_later, core * rows, rows, 0)
    back = outer(du_own, proj_weight).astype(BF)
    glob_out_grad = jnp.concatenate(
        [back[j * patches : (j + 1) * patches] for j in range(own)], axis=1
    )

    last = [up.kept, proj.kept, table.kept, down.kept, glob_out_grad]
    names = {"T": table, "D": down, "U": up, "P": proj}
    ends = [down, up, proj]
    heights = [c.kept.shape[0] >> c.left + 1 for c in ends]
    merged = None

    def last_sums(after):
        kind = down.kept.dtype if down.kept.dtype == proj.kept.dtype else F32
        keep, sent = step(
            last_body,
            [like(sum(heights), width, kind)] * 2,
            [x for c in ends for x in (c.kept, c.arrived)],
            after,
        )
        return keep, go(sent, tp_steps[-1])

    for name in ORDER:
        chain = names.get(name)
        if chain is not None and chain.left:
            last = [chain.next(last)]
        elif name == "F":
            while any(c.left for c in ends):
                for c in ends:
                    if c.left:
                        last = [c.next(last)]
            merged = last_sums(last)
            last = [merged[0]]
    while table.left:
        last = [table.next(last)]

    lines = width // 128
    emb_global_grad, emb_local_grad, gain_grad = call(
        functools.partial(tables_body, share_count, tp_count, height, PARTS),
        [like(vocab, width, F32), like(vocab, width, F32), like(lines, 128, F32)],
        [*table.parts, *table.arrived],
        last,
    )
    down_grad, up_grad, proj_grad = call(
        finals_body,
        [like(h, width, F32) for h in heights],
        [*merged],
        [gain_grad],
    )
    return (
        glob_out_grad,
        emb_global_grad,
        emb_local_grad,
        gain_grad.reshape(width),
        proj_grad.T,
        up_grad.T,
        down_grad,
    )


def solution(mesh):
    placed = (
        P("seq", None),
        P("seq", "tp"),
        P("seq", "tp"),
        P(("seq", "tp"), None),
        P(),
        P(),
        P(),
        P(),
        P(),
    )
    return jax.shard_map(
        on_device,
        mesh=mesh,
        in_specs=placed,
        out_specs=(
            P("seq", "tp"),
            P(),
            P(),
            P(),
            P(None, ("seq", "tp")),
            P(None, ("seq", "tp")),
            P(("seq", "tp"), None),
        ),
        check_vma=False,
    )
```

```python
import functools

import jax
import jax.numpy as jnp
from jax import lax
from jax.experimental import pallas as pl
from jax.experimental.pallas import tpu as pltpu
from jax.sharding import PartitionSpec as P

BF = jnp.bfloat16
F32 = jnp.float32
ROOM = 8 * 1024 * 1024
PARTS = 3
ORDER = "TDTUPTDUPTFTT"
STEP = 6 * 1000 * 1000 * 1000
VMEM = pltpu.VMEM


def inner(left, right):
    return lax.dot_general(
        left, right, (((0,), (0,)), ((), ())), preferred_element_type=F32
    )


def outer(left, right):
    return lax.dot_general(
        left, right, (((1,), (1,)), ((), ())), preferred_element_type=F32
    )


def times(left, right):
    return jnp.dot(left, right, preferred_element_type=F32)


def swap(value, axis, masks):
    count = lax.axis_size(axis)
    pairs = [(i, i ^ masks[i % len(masks)]) for i in range(count)]
    return lax.ppermute(value, axis, pairs)


def like(rows, columns, kind):
    return jax.ShapeDtypeStruct((rows, columns), kind)


def whole(array):
    return pl.BlockSpec(array.shape, lambda n, s: (0,) * len(array.shape))


def run(
    body, outs, ins, after, numbers, in_specs=None, out_specs=None, scratch=(), room=ROOM,
    alias=None, flops=0, grid=1,
):
    count, late = 1 + len(ins), len(after)

    def kernel(*refs):
        body(*refs[:count], *refs[count + late :])

    in_specs = in_specs or [None] * len(ins)
    out_specs = out_specs or [None] * len(outs)
    return pl.pallas_call(
        kernel,
        out_shape=tuple(outs),
        grid_spec=pltpu.PrefetchScalarGridSpec(
            num_scalar_prefetch=1,
            grid=(grid,),
            in_specs=[s or whole(a) for s, a in zip(in_specs, ins)]
            + [pl.BlockSpec(memory_space=pl.ANY)] * late,
            out_specs=tuple(s or whole(a) for s, a in zip(out_specs, outs)),
            scratch_shapes=list(scratch),
        ),
        input_output_aliases=alias or {},
        compiler_params=pltpu.CompilerParams(vmem_limit_bytes=room),
        cost_estimate=pl.CostEstimate(flops=flops, bytes_accessed=0, transcendentals=0),
    )(numbers, *ins, *after)


def sort_body(patch, part, own, numbers, grad, *blocks):
    size = own * part
    row = lax.broadcasted_iota(jnp.int32, (size, grad.shape[0]), 0)
    source = lax.broadcasted_iota(jnp.int32, (size, grad.shape[0]), 1)
    for m, block in enumerate(blocks):
        wanted = (row % part) * patch + numbers[m] * own + row // part
        block[...] = times((source == wanted).astype(BF), grad[...]).astype(BF)


def join_body(part, own, count, share_count, height, numbers, ids_own, *refs):
    blocks, joined, mine = refs[:-2], refs[-2], refs[-1]
    for m, block in enumerate(blocks):
        for j in range(own):
            start = pl.multiple_of((j * count + numbers[m]) * part, part)
            joined[pl.ds(start, part), :] = block[j * part : (j + 1) * part, :]
    line = vocab_line(numbers, count, 2 * share_count, height)
    ids = ids_own[...].T
    patches = ids.shape[0]
    for j in range(own):
        wanted = id_of(ids, numbers[0] * own + j)
        mine[j * patches : (j + 1) * patches, :] = hot(wanted, line)


def sent_order(count):
    return sorted(range(count), key=lambda m: bin(m + count)[:2:-1])


def id_of(ids, place):
    lane = lax.broadcasted_iota(jnp.int32, ids.shape, 1)
    return jnp.sum(jnp.where(lane == place, ids + 1, 0), axis=1, keepdims=True) - 1


def vocab_line(numbers, first, count, height):
    lane = lax.broadcasted_iota(jnp.int32, (1, count * height), 1)
    line = lane % height
    for n in range(count):
        line = line + jnp.where(lane // height == n, numbers[first + n] * height, 0)
    return line


def hot(ids, line):
    return jnp.where(ids == line, 1.0, 0.0).astype(BF)


def place_body(own, core_at, numbers, mine, other, both):
    patches, width = mine.shape[0], mine.shape[1] // own
    rows = own * patches
    for side, value in ((numbers[core_at], mine), (1 - numbers[core_at], other)):
        for j in range(own):
            start = pl.multiple_of(side * rows + j * patches, patches)
            both[pl.ds(start, patches), :] = value[:, j * width : (j + 1) * width]


def hots_body(own, tp_count, share_count, height, core_at, numbers, ids_own, ids_other, prev, here):
    patches = ids_own.shape[1]
    plain = lax.broadcasted_iota(jnp.int32, (1, prev.shape[1]), 1)
    line = vocab_line(numbers, tp_count, share_count, height)
    core = numbers[core_at]
    for side, which in ((core, ids_own), (1 - core, ids_other)):
        ids = which[...].T
        for j in range(own):
            start = pl.multiple_of(side * own * patches + j * patches, patches)
            at = pl.ds(start, patches)
            before = id_of(ids, numbers[0] * own + j - 1)
            prev[at, :] = hot(before, plain)
            here[at, :] = hot(before, line)


def turn_matrix(tp_count, chunk, numbers):
    unit = chunk // tp_count
    row = lax.broadcasted_iota(jnp.int32, (chunk, chunk), 0)
    column = lax.broadcasted_iota(jnp.int32, (chunk, chunk), 1)
    source = column % unit
    for i, m in enumerate(sent_order(tp_count)):
        source = source + jnp.where(column // unit == i, numbers[m] * unit, 0)
    return (row == source).astype(BF)


def pick_up_body(tp_count, share_count, numbers, up, up_here, ups, ready):
    chunk = ups.shape[2]
    half = chunk // 2
    copies = []
    for n in range(share_count):
        at = pl.ds(pl.multiple_of(numbers[tp_count + n] * chunk, chunk), chunk)
        copies.append(pltpu.make_async_copy(up.at[:, at], ups.at[n], ready.at[n]))
        copies[-1].start()
    turn = turn_matrix(tp_count, chunk, numbers)
    for n in range(share_count):
        copies[n].wait()
        value = times(ups[n], turn).astype(BF)
        for z in range(2):
            first = (z * share_count + n) * half
            up_here[:, first : first + half] = value[:, z * half : (z + 1) * half]


def pick_down_body(tp_count, share_count, numbers, down, down_here, downs, ready):
    chunk = downs.shape[1]
    unit = chunk // tp_count
    half = chunk // 2
    copies = []
    for n in range(share_count):
        at = pl.ds(pl.multiple_of(numbers[tp_count + n] * chunk, chunk), chunk)
        copies.append(pltpu.make_async_copy(down.at[at, :], downs.at[n], ready.at[n]))
        copies[-1].start()
    for n in range(share_count):
        copies[n].wait()
        for i, m in enumerate(sent_order(tp_count)):
            z, place = i // (tp_count // 2), i % (tp_count // 2)
            first = (z * share_count + n) * half + place * unit
            start = pl.multiple_of(numbers[m] * unit, unit)
            down_here[first : first + unit, :] = downs[n, pl.ds(start, unit), :]


def split_body(tp_count, share, numbers, value, kept, sent):
    unit = share // tp_count
    half = kept.shape[0]
    inner_shares = value.shape[0] // share // 2
    inner_places = tp_count // 2
    for n in range(2 * inner_shares):
        for i, m in enumerate(sent_order(tp_count)):
            at = pl.ds(n * share + pl.multiple_of(numbers[m] * unit, unit), unit)
            place = 2 * (n // inner_shares) + i // inner_places
            place = place * inner_shares + n % inner_shares
            place = (place * inner_places + i % inner_places) * unit
            target = kept if place < half else sent
            row = place % half
            target[row : row + unit, :] = value[at, :].astype(target.dtype)


def tables_in_body(
    share_count, first_share, height, numbers, glob, glob_more, local, gains, kept, sent
):
    width = glob.shape[1]
    strip = width // (2 * share_count)
    lines = width // 128
    lane = lax.broadcasted_iota(jnp.int32, (1, width), 1)
    both = glob[...].astype(F32) + glob_more[...].astype(F32)
    size = 2 * height
    kept[:, width:] = jnp.zeros((kept.shape[0], 128), BF)
    sent[:, width:] = jnp.zeros((sent.shape[0], 128), BF)
    for n in range(share_count):
        target = kept if n < share_count // 2 else sent
        first = (n % (share_count // 2)) * size
        at = slice(n * height, (n + 1) * height)
        target[first : first + height, :width] = both[at, :].astype(BF)
        target[first + height : first + size, :width] = local[at, :].astype(BF)
        mine = jnp.where(lane // strip == numbers[first_share + n], gains[...], 0.0)
        rows = [mine[:, i * 128 : (i + 1) * 128] for i in range(lines)]
        rows.append(jnp.zeros((16 - lines, 128), F32))
        target[first : first + 16, width:] = jnp.concatenate(rows, axis=0).astype(BF)


def add_body(numbers, kept, arrived, keep, send):
    half = keep.shape[0]
    keep[...] = (kept[:half, :].astype(F32) + arrived[:half, :].astype(F32)).astype(keep.dtype)
    send[...] = (kept[half:, :].astype(F32) + arrived[half:, :].astype(F32)).astype(send.dtype)


def sum_body(numbers, kept, arrived, summed):
    summed[...] = (kept[...].astype(F32) + arrived[...].astype(F32)).astype(summed.dtype)


def stack_body(count, numbers, *refs):
    firsts, seconds, parts = refs[:count], refs[count : 2 * count], refs[2 * count :]
    column = 0
    for i, part in enumerate(parts):
        first, second = firsts[min(i, count - 1)], seconds[min(i, count - 1)]
        at = slice(column, column + part.shape[1])
        rows = first.shape[0]
        part[:rows, :] = first[:, at]
        part[rows:, :] = second[:, at]
        if count == 1:
            column += part.shape[1]


def tables_body(share_count, first_share, height, count, numbers, *refs):
    sides = (refs[:count], refs[count : 2 * count])
    glob, local, gain = refs[2 * count :]
    width = glob.shape[1]
    gains = None
    for side, parts in enumerate(sides):
        for n in range(share_count):
            start = numbers[first_share + side * share_count + n] * height
            at = pl.ds(pl.multiple_of(start, height), height)
            row = 2 * n * height
            column = 0
            for part in parts:
                inside = min(part.shape[1], width - column)
                to = slice(column, column + inside)
                glob[at, to] = part[row : row + height, :inside].astype(F32)
                local[at, to] = part[row + height : row + 2 * height, :inside].astype(F32)
                column += inside
            term = parts[-1][row : row + 16, parts[-1].shape[1] - 128 :].astype(F32)
            gains = term if gains is None else gains + term
    gain[...] = gains[: gain.shape[0]]


def last_body(numbers, *refs):
    keep, send = refs[-2:]
    row = 0
    for i in range(len(refs) // 2 - 1):
        kept, arrived = refs[2 * i], refs[2 * i + 1]
        half = kept.shape[0] // 2
        at = slice(row, row + half)
        for target, part in ((keep, slice(0, half)), (send, slice(half, 2 * half))):
            value = kept[part, :].astype(F32) + arrived[part, :].astype(F32)
            target[at, :] = value.astype(target.dtype)
        row += half


def finals_body(numbers, kept, arrived, *wholes):
    row = 0
    for whole in wholes:
        at = slice(row, row + whole.shape[0])
        whole[...] = kept[at, :].astype(F32) + arrived[at, :].astype(F32)
        row += whole.shape[0]


def on_device(
    byte_ids,
    global_out,
    global_in_grad,
    out_grad,
    proj_weight,
    emb_local,
    norm_gain,
    up_weight,
    down_weight,
):
    seq_count = lax.axis_size("seq")
    tp_count = lax.axis_size("tp")
    seq_place = lax.axis_index("seq")
    tp_place = lax.axis_index("tp")
    core = seq_place & 1
    chip = seq_place >> 1
    stages = seq_count.bit_length() - 2
    levels = tp_count.bit_length() - 1
    share_count = 1 << stages
    walks = (list(range(1, stages + 1)), list(range(stages, 0, -1)))
    patches, patch = byte_ids.shape
    slot, width = proj_weight.shape
    hidden = up_weight.shape[1]
    vocab = emb_local.shape[0]
    own = patch // tp_count
    part = patches // tp_count
    rows = own * patches
    height = vocab // seq_count
    chunk = hidden // seq_count

    def share_mask(number, walk):
        mask = 0
        for k in range(stages):
            if (number >> (stages - 1 - k)) & 1:
                mask |= 1 << (walk[k] - 1)
        return mask

    def shares_of(which):
        return [
            2 * (chip ^ jnp.where(which == 0, share_mask(n, walks[0]), share_mask(n, walks[1])))
            + which
            for n in range(share_count)
        ]

    shares = shares_of(core)
    others = shares_of(1 - core)
    near = [tp_place ^ m for m in range(tp_count)]
    numbers = jnp.stack(near + shares + others + [core]).astype(jnp.int32)
    core_at = tp_count + 2 * share_count
    call = functools.partial(run, numbers=numbers)

    def core_swap(value):
        return swap(value, "seq", (1,))

    def go(value, step):
        kind, k = step
        if kind == "seq":
            return swap(value, "seq", (1 << walks[0][k], 1 << walks[1][k]))
        return swap(value, "tp", (1 << k,))

    ids_own = byte_ids.T
    ids_other = core_swap(ids_own)
    out_other = core_swap(global_out)
    blocks = call(
        functools.partial(sort_body, patch, part, own),
        [like(own * part, width, BF)] * tp_count,
        [out_grad],
        [],
        flops=STEP,
    )
    blocks = [swap(b, "tp", (m,)) if m else b for m, b in enumerate(blocks)]
    far = pl.BlockSpec(memory_space=pltpu.HBM)
    prev_hot, prev_here = call(
        functools.partial(hots_body, own, tp_count, share_count, height, core_at),
        [like(2 * rows, vocab, BF), like(2 * rows, vocab // 2, BF)],
        [ids_own, ids_other],
        [blocks[0]],
    )

    def by_slot(value):
        return [value[:, j * slot : (j + 1) * slot] for j in range(own)]

    (slot_in,) = call(
        functools.partial(place_body, own, core_at),
        [like(2 * rows, slot, BF)],
        [global_out, out_other],
        [prev_hot],
    )
    before = jnp.dot(prev_hot, emb_local, preferred_element_type=BF)
    u_rows = times(slot_in, proj_weight) + before.astype(F32)
    scale = lax.rsqrt(jnp.mean(u_rows * u_rows, axis=1, keepdims=True) + 1e-05)
    normed = u_rows * scale
    r_rows = (normed * norm_gain).astype(BF)
    (up_here,) = call(
        functools.partial(pick_up_body, tp_count, share_count),
        [like(width, hidden // 2, BF)],
        [up_weight],
        [r_rows],
        in_specs=[far],
        scratch=[VMEM((share_count, width, chunk), BF), pltpu.SemaphoreType.DMA((share_count,))],
    )
    a_rows = times(r_rows, up_here)
    sig = jax.nn.sigmoid(a_rows)
    h_rows = (a_rows * sig).astype(BF)
    slope = (sig * (1.0 + a_rows * (1.0 - sig))).astype(BF)
    h_rows, slope = lax.optimization_barrier((h_rows, slope))
    (down_here,) = call(
        functools.partial(pick_down_body, tp_count, share_count),
        [like(hidden // 2, width, BF)],
        [down_weight],
        [h_rows],
        in_specs=[far],
        scratch=[VMEM((share_count, chunk, width), BF), pltpu.SemaphoreType.DMA((share_count,))],
    )
    strip = chunk // 2
    h_rows = jnp.concatenate(
        [
            h_rows[:, (z * share_count + n) * strip : (z * share_count + n + 1) * strip]
            for n in range(share_count)
            for z in range(2)
        ],
        axis=1,
    )

    grad_own, own_hot = call(
        functools.partial(join_body, part, own, tp_count, share_count, height),
        [like(rows, width, BF), like(rows, vocab, BF)],
        [ids_own, *blocks],
        [h_rows],
        numbers=numbers,
    )
    grad_other = core_swap(grad_own)
    glob = [
        inner(own_hot[j * patches : (j + 1) * patches], value)
        for j, value in enumerate(by_slot(global_in_grad))
    ]
    glob = sum(glob[1:], glob[0])
    glob_sent = glob[vocab // 2 :].astype(BF)
    glob_kept = glob[: vocab // 2].astype(BF)
    glob_more = core_swap(glob_sent)

    (out_rows,) = call(
        functools.partial(place_body, 1, core_at),
        [like(2 * rows, width, BF)],
        [grad_own, grad_other],
        [glob_kept],
    )

    seq_steps = [("seq", k) for k in range(stages)]
    tp_steps = [("tp", k) for k in range(levels)]

    step = functools.partial(call, flops=STEP)

    class Chain:
        def __init__(self, kept, sent, steps):
            self.kept, self.steps, self.at = kept, steps, 0
            self.arrived = go(sent, self.steps[0])
            self.left = self.first = len(self.steps) - 2

        def next(self, after):
            self.at += 1
            self.left -= 1
            rows, columns = self.kept.shape
            ins = [self.kept, self.arrived]
            outs = [like(rows // 2, columns, self.kept.dtype)] * 2
            self.kept, sent = step(add_body, outs, ins, after)
            self.arrived = go(sent, self.steps[self.at])
            return self.kept

    class Table:
        def __init__(self, kept, sent):
            self.kept, self.at = kept, 0
            self.plan = (
                [("half", s) for s in seq_steps]
                + [("sum", s) for s in tp_steps]
                + [("join", s) for s in reversed(seq_steps)]
                + [("join", None)]
            )
            self.left = len(self.plan) - 1
            self.arrived = go(sent, self.plan[0][1])

        def next(self, after):
            last, (kind, hop) = self.plan[self.at][0], self.plan[self.at + 1]
            rows, columns = self.kept.shape
            ins = [self.kept, self.arrived]
            if last == "half" and kind == "half":
                self.kept, sent = step(add_body, [like(rows // 2, columns, BF)] * 2, ins, after)
            elif last == "join":
                many = self.plan[self.at + 1 :]
                cut = columns if len(many) > 2 or len(self.parts) > 1 else columns // PARTS
                outs = [like(2 * rows, cut, BF)] * (PARTS if len(many) <= 2 else 1)
                body = functools.partial(stack_body, len(self.parts))
                build = step if len(many) > 2 else call
                self.parts = build(body, outs, [*self.parts, *self.arrived], after)
                self.kept = self.parts[0]
            else:
                (self.kept,) = step(sum_body, [like(rows, columns, BF)], ins, after)
                sent = self.kept
            self.at += 1
            self.left -= 1
            if kind == "join":
                if last != "join":
                    self.parts = [sent]
                self.arrived = [
                    core_swap(part) if hop is None else go(part, hop) for part in self.parts
                ]
            else:
                self.arrived = go(sent, hop)
            return self.kept

    dh_rows = outer(out_rows, down_here)
    da_rows = (dh_rows * slope.astype(F32)).astype(BF)
    dr_part = outer(da_rows, up_here)
    dr_sent = dr_part.astype(BF)
    kind = BF if chunk // tp_count % 16 == 0 else F32
    half = h_rows.shape[1] // 2
    down_kept = inner(h_rows[:, :half], out_rows).astype(kind)
    down_sent = inner(h_rows[:, half:], out_rows).astype(kind)
    up_kept = inner(da_rows[:, :half], r_rows).astype(kind)
    up_sent = inner(da_rows[:, half:], r_rows).astype(kind)
    down = Chain(down_kept, down_sent, seq_steps + tp_steps)
    up = Chain(up_kept, up_sent, tp_steps[:1] + seq_steps + tp_steps[1:])
    dr_more = core_swap(dr_sent)
    dr_rows = dr_part + dr_more.astype(F32)

    gain_part = jnp.sum(dr_rows * normed, axis=0, keepdims=True)
    dn_rows = dr_rows * norm_gain
    du_rows = (
        out_rows.astype(F32)
        + scale * (dn_rows - normed * jnp.mean(dn_rows * normed, axis=1, keepdims=True))
    ).astype(BF)
    size = 2 * height
    kept, sent = call(
        functools.partial(tables_in_body, share_count, tp_count, height),
        [like(share_count // 2 * size, width + 128, BF)] * 2,
        [glob_kept, glob_more, inner(prev_here, du_rows), gain_part],
        [up.kept],
    )
    table = Table(kept, sent)
    share = width // seq_count
    kind = BF if share // tp_count % 16 == 0 else F32
    du_later, _ = lax.optimization_barrier((du_rows, table.kept))
    du_here = jnp.concatenate(
        [lax.dynamic_slice_in_dim(du_later, s * share, share, 1) for s in shares], axis=1
    )
    value = inner(du_here, slot_in)
    kept, sent = call(
        functools.partial(split_body, tp_count, share),
        [like(value.shape[0] // 2, slot, kind)] * 2,
        [value],
        [table.kept],
    )
    proj = Chain(kept, sent, seq_steps[:1] + tp_steps[:1] + seq_steps[1:] + tp_steps[1:])
    last = [up.kept, proj.kept, table.kept, down.kept]
    names = {"T": table, "D": down, "U": up, "P": proj}
    ends = [down, up, proj]
    heights = [c.kept.shape[0] >> c.left + 1 for c in ends]
    merged = None

    def last_sums(after):
        kind = down.kept.dtype if down.kept.dtype == proj.kept.dtype else F32
        keep, sent = step(
            last_body,
            [like(sum(heights), width, kind)] * 2,
            [x for c in ends for x in (c.kept, c.arrived)],
            after,
        )
        return keep, go(sent, tp_steps[-1])

    def spread(after):
        du_own, _ = lax.optimization_barrier((du_rows, after))
        du_own = lax.dynamic_slice_in_dim(du_own, core * rows, rows, 0)
        back = outer(du_own, proj_weight).astype(BF)
        return jnp.concatenate(
            [back[j * patches : (j + 1) * patches] for j in range(own)], axis=1
        )

    glob_out_grad = None
    for name in ORDER:
        chain = names.get(name)
        if chain is not None and chain.left:
            last = [chain.next(last)]
            if chain is up and glob_out_grad is None and up.left <= max(0, up.first - 2):
                glob_out_grad = spread(up.kept)
                last.append(glob_out_grad)
        elif name == "F":
            while any(c.left for c in ends):
                for c in ends:
                    if c.left:
                        last = [c.next(last)]
            merged = last_sums(last)
            last = [merged[0]]
    while table.left:
        last = [table.next(last)]

    lines = width // 128
    emb_global_grad, emb_local_grad, gain_grad = call(
        functools.partial(tables_body, share_count, tp_count, height, PARTS),
        [like(vocab, width, F32), like(vocab, width, F32), like(lines, 128, F32)],
        [*table.parts, *table.arrived],
        last,
    )
    down_grad, up_grad, proj_grad = call(
        finals_body,
        [like(h, width, F32) for h in heights],
        [*merged],
        [gain_grad],
    )
    return (
        glob_out_grad,
        emb_global_grad,
        emb_local_grad,
        gain_grad.reshape(width),
        proj_grad.T,
        up_grad.T,
        down_grad,
    )


def solution(mesh):
    placed = (
        P("seq", None),
        P("seq", "tp"),
        P("seq", "tp"),
        P(("seq", "tp"), None),
        P(),
        P(),
        P(),
        P(),
        P(),
    )
    return jax.shard_map(
        on_device,
        mesh=mesh,
        in_specs=placed,
        out_specs=(
            P("seq", "tp"),
            P(),
            P(),
            P(),
            P(None, ("seq", "tp")),
            P(None, ("seq", "tp")),
            P(("seq", "tp"), None),
        ),
        check_vma=False,
    )
```

```python
import functools

import jax
import jax.numpy as jnp
from jax import lax
from jax.experimental import pallas as pl
from jax.experimental.pallas import tpu as pltpu
from jax.sharding import PartitionSpec as P

BF = jnp.bfloat16
F32 = jnp.float32
ROOM = 8 * 1024 * 1024
PARTS = 3
ORDER = "TDTUPTDUPTFTT"
STEP = 6 * 1000 * 1000 * 1000
VMEM = pltpu.VMEM


def inner(left, right):
    return lax.dot_general(
        left, right, (((0,), (0,)), ((), ())), preferred_element_type=F32
    )


def outer(left, right):
    return lax.dot_general(
        left, right, (((1,), (1,)), ((), ())), preferred_element_type=F32
    )


def times(left, right):
    return jnp.dot(left, right, preferred_element_type=F32)


def swap(value, axis, masks):
    count = lax.axis_size(axis)
    pairs = [(i, i ^ masks[i % len(masks)]) for i in range(count)]
    return lax.ppermute(value, axis, pairs)


def like(rows, columns, kind):
    return jax.ShapeDtypeStruct((rows, columns), kind)


def whole(array):
    return pl.BlockSpec(array.shape, lambda n, s: (0,) * len(array.shape))


def run(
    body, outs, ins, after, numbers, in_specs=None, out_specs=None, scratch=(), room=ROOM,
    alias=None, flops=0, grid=1,
):
    count, late = 1 + len(ins), len(after)

    def kernel(*refs):
        body(*refs[:count], *refs[count + late :])

    in_specs = in_specs or [None] * len(ins)
    out_specs = out_specs or [None] * len(outs)
    return pl.pallas_call(
        kernel,
        out_shape=tuple(outs),
        grid_spec=pltpu.PrefetchScalarGridSpec(
            num_scalar_prefetch=1,
            grid=(grid,),
            in_specs=[s or whole(a) for s, a in zip(in_specs, ins)]
            + [pl.BlockSpec(memory_space=pl.ANY)] * late,
            out_specs=tuple(s or whole(a) for s, a in zip(out_specs, outs)),
            scratch_shapes=list(scratch),
        ),
        input_output_aliases=alias or {},
        compiler_params=pltpu.CompilerParams(vmem_limit_bytes=room),
        cost_estimate=pl.CostEstimate(flops=flops, bytes_accessed=0, transcendentals=0),
    )(numbers, *ins, *after)


def sort_body(patch, part, own, numbers, grad, *blocks):
    size = own * part
    row = lax.broadcasted_iota(jnp.int32, (size, grad.shape[0]), 0)
    source = lax.broadcasted_iota(jnp.int32, (size, grad.shape[0]), 1)
    for m, block in enumerate(blocks):
        wanted = (row % part) * patch + numbers[m] * own + row // part
        block[...] = times((source == wanted).astype(BF), grad[...]).astype(BF)


def join_body(part, own, count, share_count, height, numbers, ids_own, *refs):
    blocks, joined, mine = refs[:-2], refs[-2], refs[-1]
    for m, block in enumerate(blocks):
        for j in range(own):
            start = pl.multiple_of((j * count + numbers[m]) * part, part)
            joined[pl.ds(start, part), :] = block[j * part : (j + 1) * part, :]
    line = vocab_line(numbers, count, 2 * share_count, height)
    ids = ids_own[...].T
    patches = ids.shape[0]
    for j in range(own):
        wanted = id_of(ids, numbers[0] * own + j)
        mine[j * patches : (j + 1) * patches, :] = hot(wanted, line)


def sent_order(count):
    return sorted(range(count), key=lambda m: bin(m + count)[:2:-1])


def id_of(ids, place):
    lane = lax.broadcasted_iota(jnp.int32, ids.shape, 1)
    return jnp.sum(jnp.where(lane == place, ids + 1, 0), axis=1, keepdims=True) - 1


def vocab_line(numbers, first, count, height):
    lane = lax.broadcasted_iota(jnp.int32, (1, count * height), 1)
    line = lane % height
    for n in range(count):
        line = line + jnp.where(lane // height == n, numbers[first + n] * height, 0)
    return line


def hot(ids, line):
    return jnp.where(ids == line, 1.0, 0.0).astype(BF)


def place_body(own, core_at, numbers, mine, other, both):
    patches, width = mine.shape[0], mine.shape[1] // own
    rows = own * patches
    for side, value in ((numbers[core_at], mine), (1 - numbers[core_at], other)):
        for j in range(own):
            start = pl.multiple_of(side * rows + j * patches, patches)
            both[pl.ds(start, patches), :] = value[:, j * width : (j + 1) * width]


def hots_body(own, tp_count, share_count, height, core_at, numbers, ids_own, ids_other, prev, here):
    patches = ids_own.shape[1]
    plain = lax.broadcasted_iota(jnp.int32, (1, prev.shape[1]), 1)
    line = vocab_line(numbers, tp_count, share_count, height)
    core = numbers[core_at]
    for side, which in ((core, ids_own), (1 - core, ids_other)):
        ids = which[...].T
        for j in range(own):
            start = pl.multiple_of(side * own * patches + j * patches, patches)
            at = pl.ds(start, patches)
            before = id_of(ids, numbers[0] * own + j - 1)
            prev[at, :] = hot(before, plain)
            here[at, :] = hot(before, line)


def turn_matrix(tp_count, chunk, numbers):
    unit = chunk // tp_count
    row = lax.broadcasted_iota(jnp.int32, (chunk, chunk), 0)
    column = lax.broadcasted_iota(jnp.int32, (chunk, chunk), 1)
    source = column % unit
    for i, m in enumerate(sent_order(tp_count)):
        source = source + jnp.where(column // unit == i, numbers[m] * unit, 0)
    return (row == source).astype(BF)


def pick_up_body(tp_count, share_count, numbers, up, up_here, ups, ready):
    chunk = ups.shape[2]
    half = chunk // 2
    copies = []
    for n in range(share_count):
        at = pl.ds(pl.multiple_of(numbers[tp_count + n] * chunk, chunk), chunk)
        copies.append(pltpu.make_async_copy(up.at[:, at], ups.at[n], ready.at[n]))
        copies[-1].start()
    turn = turn_matrix(tp_count, chunk, numbers)
    for n in range(share_count):
        copies[n].wait()
        value = times(ups[n], turn).astype(BF)
        for z in range(2):
            first = (z * share_count + n) * half
            up_here[:, first : first + half] = value[:, z * half : (z + 1) * half]


def pick_down_body(tp_count, share_count, numbers, down, down_here, downs, ready):
    chunk = downs.shape[1]
    unit = chunk // tp_count
    half = chunk // 2
    copies = []
    for n in range(share_count):
        at = pl.ds(pl.multiple_of(numbers[tp_count + n] * chunk, chunk), chunk)
        copies.append(pltpu.make_async_copy(down.at[at, :], downs.at[n], ready.at[n]))
        copies[-1].start()
    for n in range(share_count):
        copies[n].wait()
        for i, m in enumerate(sent_order(tp_count)):
            z, place = i // (tp_count // 2), i % (tp_count // 2)
            first = (z * share_count + n) * half + place * unit
            start = pl.multiple_of(numbers[m] * unit, unit)
            down_here[first : first + unit, :] = downs[n, pl.ds(start, unit), :]


def split_body(tp_count, share, numbers, value, kept, sent):
    unit = share // tp_count
    half = kept.shape[0]
    inner_shares = value.shape[0] // share // 2
    inner_places = tp_count // 2
    for n in range(2 * inner_shares):
        for i, m in enumerate(sent_order(tp_count)):
            at = pl.ds(n * share + pl.multiple_of(numbers[m] * unit, unit), unit)
            place = 2 * (n // inner_shares) + i // inner_places
            place = place * inner_shares + n % inner_shares
            place = (place * inner_places + i % inner_places) * unit
            target = kept if place < half else sent
            row = place % half
            target[row : row + unit, :] = value[at, :].astype(target.dtype)


def tables_in_body(
    share_count, first_share, height, numbers, glob, glob_more, local, gains, kept, sent
):
    width = glob.shape[1]
    strip = width // (2 * share_count)
    lines = width // 128
    lane = lax.broadcasted_iota(jnp.int32, (1, width), 1)
    both = glob[...].astype(F32) + glob_more[...].astype(F32)
    size = 2 * height
    kept[:, width:] = jnp.zeros((kept.shape[0], 128), BF)
    sent[:, width:] = jnp.zeros((sent.shape[0], 128), BF)
    for n in range(share_count):
        target = kept if n < share_count // 2 else sent
        first = (n % (share_count // 2)) * size
        at = slice(n * height, (n + 1) * height)
        target[first : first + height, :width] = both[at, :].astype(BF)
        target[first + height : first + size, :width] = local[at, :].astype(BF)
        mine = jnp.where(lane // strip == numbers[first_share + n], gains[...], 0.0)
        rows = [mine[:, i * 128 : (i + 1) * 128] for i in range(lines)]
        rows.append(jnp.zeros((16 - lines, 128), F32))
        target[first : first + 16, width:] = jnp.concatenate(rows, axis=0).astype(BF)


def add_body(numbers, kept, arrived, keep, send):
    half = keep.shape[0]
    keep[...] = (kept[:half, :].astype(F32) + arrived[:half, :].astype(F32)).astype(keep.dtype)
    send[...] = (kept[half:, :].astype(F32) + arrived[half:, :].astype(F32)).astype(send.dtype)


def sum_body(numbers, kept, arrived, summed):
    summed[...] = (kept[...].astype(F32) + arrived[...].astype(F32)).astype(summed.dtype)


def stack_body(count, numbers, *refs):
    firsts, seconds, parts = refs[:count], refs[count : 2 * count], refs[2 * count :]
    column = 0
    for i, part in enumerate(parts):
        first, second = firsts[min(i, count - 1)], seconds[min(i, count - 1)]
        at = slice(column, column + part.shape[1])
        rows = first.shape[0]
        part[:rows, :] = first[:, at]
        part[rows:, :] = second[:, at]
        if count == 1:
            column += part.shape[1]


def tables_body(share_count, first_share, height, count, numbers, *refs):
    sides = (refs[:count], refs[count : 2 * count])
    glob, local, gain = refs[2 * count :]
    width = glob.shape[1]
    gains = None
    for side, parts in enumerate(sides):
        for n in range(share_count):
            start = numbers[first_share + side * share_count + n] * height
            at = pl.ds(pl.multiple_of(start, height), height)
            row = 2 * n * height
            column = 0
            for part in parts:
                inside = min(part.shape[1], width - column)
                to = slice(column, column + inside)
                glob[at, to] = part[row : row + height, :inside].astype(F32)
                local[at, to] = part[row + height : row + 2 * height, :inside].astype(F32)
                column += inside
            term = parts[-1][row : row + 16, parts[-1].shape[1] - 128 :].astype(F32)
            gains = term if gains is None else gains + term
    gain[...] = gains[: gain.shape[0]]


def last_body(numbers, *refs):
    keep, send = refs[-2:]
    row = 0
    for i in range(len(refs) // 2 - 1):
        kept, arrived = refs[2 * i], refs[2 * i + 1]
        half = kept.shape[0] // 2
        at = slice(row, row + half)
        for target, part in ((keep, slice(0, half)), (send, slice(half, 2 * half))):
            value = kept[part, :].astype(F32) + arrived[part, :].astype(F32)
            target[at, :] = value.astype(target.dtype)
        row += half


def finals_body(numbers, kept, arrived, *wholes):
    row = 0
    for whole in wholes:
        at = slice(row, row + whole.shape[0])
        whole[...] = kept[at, :].astype(F32) + arrived[at, :].astype(F32)
        row += whole.shape[0]


def on_device(
    byte_ids,
    global_out,
    global_in_grad,
    out_grad,
    proj_weight,
    emb_local,
    norm_gain,
    up_weight,
    down_weight,
):
    seq_count = lax.axis_size("seq")
    tp_count = lax.axis_size("tp")
    seq_place = lax.axis_index("seq")
    tp_place = lax.axis_index("tp")
    core = seq_place & 1
    chip = seq_place >> 1
    stages = seq_count.bit_length() - 2
    levels = tp_count.bit_length() - 1
    share_count = 1 << stages
    walks = (list(range(1, stages + 1)), list(range(stages, 0, -1)))
    patches, patch = byte_ids.shape
    slot, width = proj_weight.shape
    hidden = up_weight.shape[1]
    vocab = emb_local.shape[0]
    own = patch // tp_count
    part = patches // tp_count
    rows = own * patches
    height = vocab // seq_count
    chunk = hidden // seq_count

    def share_mask(number, walk):
        mask = 0
        for k in range(stages):
            if (number >> (stages - 1 - k)) & 1:
                mask |= 1 << (walk[k] - 1)
        return mask

    def shares_of(which):
        return [
            2 * (chip ^ jnp.where(which == 0, share_mask(n, walks[0]), share_mask(n, walks[1])))
            + which
            for n in range(share_count)
        ]

    shares = shares_of(core)
    others = shares_of(1 - core)
    near = [tp_place ^ m for m in range(tp_count)]
    numbers = jnp.stack(near + shares + others + [core]).astype(jnp.int32)
    core_at = tp_count + 2 * share_count
    call = functools.partial(run, numbers=numbers)

    def core_swap(value):
        return swap(value, "seq", (1,))

    def go(value, step):
        kind, k = step
        if kind == "seq":
            return swap(value, "seq", (1 << walks[0][k], 1 << walks[1][k]))
        return swap(value, "tp", (1 << k,))

    ids_own = byte_ids.T
    ids_other = core_swap(ids_own)
    out_other = core_swap(global_out)
    blocks = call(
        functools.partial(sort_body, patch, part, own),
        [like(own * part, width, BF)] * tp_count,
        [out_grad],
        [],
        flops=STEP,
    )
    blocks = [swap(b, "tp", (m,)) if m else b for m, b in enumerate(blocks)]
    far = pl.BlockSpec(memory_space=pltpu.HBM)
    prev_hot, prev_here = call(
        functools.partial(hots_body, own, tp_count, share_count, height, core_at),
        [like(2 * rows, vocab, BF), like(2 * rows, vocab // 2, BF)],
        [ids_own, ids_other],
        [blocks[0]],
    )

    def by_slot(value):
        return [value[:, j * slot : (j + 1) * slot] for j in range(own)]

    (slot_in,) = call(
        functools.partial(place_body, own, core_at),
        [like(2 * rows, slot, BF)],
        [global_out, out_other],
        [prev_hot],
    )
    before = jnp.dot(prev_hot, emb_local, preferred_element_type=BF)
    u_rows = times(slot_in, proj_weight) + before.astype(F32)
    scale = lax.rsqrt(jnp.mean(u_rows * u_rows, axis=1, keepdims=True) + 1e-05)
    normed = u_rows * scale
    r_rows = (normed * norm_gain).astype(BF)
    (up_here,) = call(
        functools.partial(pick_up_body, tp_count, share_count),
        [like(width, hidden // 2, BF)],
        [up_weight],
        [r_rows],
        in_specs=[far],
        scratch=[VMEM((share_count, width, chunk), BF), pltpu.SemaphoreType.DMA((share_count,))],
    )
    a_rows = times(r_rows, up_here)
    sig = jax.nn.sigmoid(a_rows)
    h_rows = (a_rows * sig).astype(BF)
    slope = (sig * (1.0 + a_rows * (1.0 - sig))).astype(BF)
    h_rows, slope = lax.optimization_barrier((h_rows, slope))
    (down_here,) = call(
        functools.partial(pick_down_body, tp_count, share_count),
        [like(hidden // 2, width, BF)],
        [down_weight],
        [h_rows],
        in_specs=[far],
        scratch=[VMEM((share_count, chunk, width), BF), pltpu.SemaphoreType.DMA((share_count,))],
    )
    strip = chunk // 2
    h_rows = jnp.concatenate(
        [
            h_rows[:, (z * share_count + n) * strip : (z * share_count + n + 1) * strip]
            for n in range(share_count)
            for z in range(2)
        ],
        axis=1,
    )

    grad_own, own_hot = call(
        functools.partial(join_body, part, own, tp_count, share_count, height),
        [like(rows, width, BF), like(rows, vocab, BF)],
        [ids_own, *blocks],
        [h_rows],
        numbers=numbers,
    )
    grad_other = core_swap(grad_own)
    glob = [
        inner(own_hot[j * patches : (j + 1) * patches], value)
        for j, value in enumerate(by_slot(global_in_grad))
    ]
    glob = sum(glob[1:], glob[0])
    glob_sent = glob[vocab // 2 :].astype(BF)
    glob_kept = glob[: vocab // 2].astype(BF)
    glob_more = core_swap(glob_sent)

    (out_rows,) = call(
        functools.partial(place_body, 1, core_at),
        [like(2 * rows, width, BF)],
        [grad_own, grad_other],
        [glob_kept],
    )

    seq_steps = [("seq", k) for k in range(stages)]
    tp_steps = [("tp", k) for k in range(levels)]

    step = functools.partial(call, flops=STEP)

    class Chain:
        def __init__(self, kept, sent, steps):
            self.kept, self.steps, self.at = kept, steps, 0
            self.arrived = go(sent, self.steps[0])
            self.left = self.first = len(self.steps) - 2

        def next(self, after):
            self.at += 1
            self.left -= 1
            rows, columns = self.kept.shape
            ins = [self.kept, self.arrived]
            outs = [like(rows // 2, columns, self.kept.dtype)] * 2
            self.kept, sent = step(add_body, outs, ins, after)
            self.arrived = go(sent, self.steps[self.at])
            return self.kept

    class Table:
        def __init__(self, kept, sent):
            self.kept, self.at = kept, 0
            self.plan = (
                [("half", s) for s in seq_steps]
                + [("sum", s) for s in tp_steps]
                + [("join", s) for s in reversed(seq_steps)]
                + [("join", None)]
            )
            self.left = len(self.plan) - 1
            self.arrived = go(sent, self.plan[0][1])

        def next(self, after):
            last, (kind, hop) = self.plan[self.at][0], self.plan[self.at + 1]
            rows, columns = self.kept.shape
            ins = [self.kept, self.arrived]
            if last == "half" and kind == "half":
                self.kept, sent = step(add_body, [like(rows // 2, columns, BF)] * 2, ins, after)
            elif last == "join":
                many = self.plan[self.at + 1 :]
                cut = columns if len(many) > 2 or len(self.parts) > 1 else columns // PARTS
                outs = [like(2 * rows, cut, BF)] * (PARTS if len(many) <= 2 else 1)
                body = functools.partial(stack_body, len(self.parts))
                build = step if len(many) > 2 else call
                self.parts = build(body, outs, [*self.parts, *self.arrived], after)
                self.kept = self.parts[0]
            else:
                (self.kept,) = step(sum_body, [like(rows, columns, BF)], ins, after)
                sent = self.kept
            self.at += 1
            self.left -= 1
            if kind == "join":
                if last != "join":
                    self.parts = [sent]
                self.arrived = [
                    core_swap(part) if hop is None else go(part, hop) for part in self.parts
                ]
            else:
                self.arrived = go(sent, hop)
            return self.kept

    dh_rows = outer(out_rows, down_here)
    da_rows = (dh_rows * slope.astype(F32)).astype(BF)
    dr_part = outer(da_rows, up_here)
    dr_sent = dr_part.astype(BF)
    kind = BF if chunk // tp_count % 16 == 0 else F32
    half = h_rows.shape[1] // 2
    down_kept = inner(h_rows[:, :half], out_rows).astype(kind)
    down_sent = inner(h_rows[:, half:], out_rows).astype(kind)
    da_rows, _ = lax.optimization_barrier((da_rows, down_sent))
    up_kept = inner(da_rows[:, :half], r_rows).astype(kind)
    up_sent = inner(da_rows[:, half:], r_rows).astype(kind)
    down = Chain(down_kept, down_sent, seq_steps + tp_steps)
    up = Chain(up_kept, up_sent, tp_steps[:1] + seq_steps + tp_steps[1:])
    dr_more = core_swap(dr_sent)
    dr_rows = dr_part + dr_more.astype(F32)

    gain_part = jnp.sum(dr_rows * normed, axis=0, keepdims=True)
    dn_rows = dr_rows * norm_gain
    du_rows = (
        out_rows.astype(F32)
        + scale * (dn_rows - normed * jnp.mean(dn_rows * normed, axis=1, keepdims=True))
    ).astype(BF)
    size = 2 * height
    kept, sent = call(
        functools.partial(tables_in_body, share_count, tp_count, height),
        [like(share_count // 2 * size, width + 128, BF)] * 2,
        [glob_kept, glob_more, inner(prev_here, du_rows), gain_part],
        [up.kept],
    )
    table = Table(kept, sent)
    share = width // seq_count
    kind = BF if share // tp_count % 16 == 0 else F32
    du_later, _ = lax.optimization_barrier((du_rows, table.kept))
    du_here = jnp.concatenate(
        [lax.dynamic_slice_in_dim(du_later, s * share, share, 1) for s in shares], axis=1
    )
    value = inner(du_here, slot_in)
    kept, sent = call(
        functools.partial(split_body, tp_count, share),
        [like(value.shape[0] // 2, slot, kind)] * 2,
        [value],
        [table.kept],
    )
    proj = Chain(kept, sent, seq_steps[:1] + tp_steps[:1] + seq_steps[1:] + tp_steps[1:])
    last = [up.kept, proj.kept, table.kept, down.kept]
    names = {"T": table, "D": down, "U": up, "P": proj}
    ends = [down, up, proj]
    heights = [c.kept.shape[0] >> c.left + 1 for c in ends]
    merged = None

    def last_sums(after):
        kind = down.kept.dtype if down.kept.dtype == proj.kept.dtype else F32
        keep, sent = step(
            last_body,
            [like(sum(heights), width, kind)] * 2,
            [x for c in ends for x in (c.kept, c.arrived)],
            after,
        )
        return keep, go(sent, tp_steps[-1])

    def spread(after):
        du_own, _ = lax.optimization_barrier((du_rows, after))
        du_own = lax.dynamic_slice_in_dim(du_own, core * rows, rows, 0)
        back = outer(du_own, proj_weight).astype(BF)
        return jnp.concatenate(
            [back[j * patches : (j + 1) * patches] for j in range(own)], axis=1
        )

    glob_out_grad = None
    for name in ORDER:
        chain = names.get(name)
        if chain is not None and chain.left:
            last = [chain.next(last)]
            if chain is up and glob_out_grad is None and up.left <= max(0, up.first - 2):
                glob_out_grad = spread(up.kept)
                last.append(glob_out_grad)
        elif name == "F":
            while any(c.left for c in ends):
                for c in ends:
                    if c.left:
                        last = [c.next(last)]
            merged = last_sums(last)
            last = [merged[0]]
    while table.left:
        last = [table.next(last)]

    lines = width // 128
    emb_global_grad, emb_local_grad, gain_grad = call(
        functools.partial(tables_body, share_count, tp_count, height, PARTS),
        [like(vocab, width, F32), like(vocab, width, F32), like(lines, 128, F32)],
        [*table.parts, *table.arrived],
        last,
    )
    down_grad, up_grad, proj_grad = call(
        finals_body,
        [like(h, width, F32) for h in heights],
        [*merged],
        [gain_grad],
    )
    return (
        glob_out_grad,
        emb_global_grad,
        emb_local_grad,
        gain_grad.reshape(width),
        proj_grad.T,
        up_grad.T,
        down_grad,
    )


def solution(mesh):
    placed = (
        P("seq", None),
        P("seq", "tp"),
        P("seq", "tp"),
        P(("seq", "tp"), None),
        P(),
        P(),
        P(),
        P(),
        P(),
    )
    return jax.shard_map(
        on_device,
        mesh=mesh,
        in_specs=placed,
        out_specs=(
            P("seq", "tp"),
            P(),
            P(),
            P(),
            P(None, ("seq", "tp")),
            P(None, ("seq", "tp")),
            P(("seq", "tp"), None),
        ),
        check_vma=False,
    )
```

```python
import functools

import jax
import jax.numpy as jnp
from jax import lax
from jax.experimental import pallas as pl
from jax.experimental.pallas import tpu as pltpu
from jax.sharding import PartitionSpec as P

BF = jnp.bfloat16
F32 = jnp.float32
ROOM = 8 * 1024 * 1024
PARTS = 3
ORDER = "TDTUPTDUPTFTT"
STEP = 6 * 1000 * 1000 * 1000
VMEM = pltpu.VMEM


def inner(left, right):
    return lax.dot_general(
        left, right, (((0,), (0,)), ((), ())), preferred_element_type=F32
    )


def outer(left, right):
    return lax.dot_general(
        left, right, (((1,), (1,)), ((), ())), preferred_element_type=F32
    )


def times(left, right):
    return jnp.dot(left, right, preferred_element_type=F32)


def swap(value, axis, masks):
    count = lax.axis_size(axis)
    pairs = [(i, i ^ masks[i % len(masks)]) for i in range(count)]
    return lax.ppermute(value, axis, pairs)


def like(rows, columns, kind):
    return jax.ShapeDtypeStruct((rows, columns), kind)


def whole(array):
    return pl.BlockSpec(array.shape, lambda n, s: (0,) * len(array.shape))


def run(
    body, outs, ins, after, numbers, in_specs=None, out_specs=None, scratch=(), room=ROOM,
    alias=None, flops=0, grid=1,
):
    count, late = 1 + len(ins), len(after)

    def kernel(*refs):
        body(*refs[:count], *refs[count + late :])

    in_specs = in_specs or [None] * len(ins)
    out_specs = out_specs or [None] * len(outs)
    return pl.pallas_call(
        kernel,
        out_shape=tuple(outs),
        grid_spec=pltpu.PrefetchScalarGridSpec(
            num_scalar_prefetch=1,
            grid=(grid,),
            in_specs=[s or whole(a) for s, a in zip(in_specs, ins)]
            + [pl.BlockSpec(memory_space=pl.ANY)] * late,
            out_specs=tuple(s or whole(a) for s, a in zip(out_specs, outs)),
            scratch_shapes=list(scratch),
        ),
        input_output_aliases=alias or {},
        compiler_params=pltpu.CompilerParams(vmem_limit_bytes=room),
        cost_estimate=pl.CostEstimate(flops=flops, bytes_accessed=0, transcendentals=0),
    )(numbers, *ins, *after)


def sort_body(patch, part, own, numbers, grad, *blocks):
    size = own * part
    row = lax.broadcasted_iota(jnp.int32, (size, grad.shape[0]), 0)
    source = lax.broadcasted_iota(jnp.int32, (size, grad.shape[0]), 1)
    for m, block in enumerate(blocks):
        wanted = (row % part) * patch + numbers[m] * own + row // part
        block[...] = times((source == wanted).astype(BF), grad[...]).astype(BF)


def join_body(part, own, count, share_count, height, numbers, ids_own, *refs):
    blocks, joined, mine = refs[:-2], refs[-2], refs[-1]
    for m, block in enumerate(blocks):
        for j in range(own):
            start = pl.multiple_of((j * count + numbers[m]) * part, part)
            joined[pl.ds(start, part), :] = block[j * part : (j + 1) * part, :]
    line = vocab_line(numbers, count, 2 * share_count, height)
    ids = ids_own[...].T
    patches = ids.shape[0]
    for j in range(own):
        wanted = id_of(ids, numbers[0] * own + j)
        mine[j * patches : (j + 1) * patches, :] = hot(wanted, line)


def sent_order(count):
    return sorted(range(count), key=lambda m: bin(m + count)[:2:-1])


def id_of(ids, place):
    lane = lax.broadcasted_iota(jnp.int32, ids.shape, 1)
    return jnp.sum(jnp.where(lane == place, ids + 1, 0), axis=1, keepdims=True) - 1


def vocab_line(numbers, first, count, height):
    lane = lax.broadcasted_iota(jnp.int32, (1, count * height), 1)
    line = lane % height
    for n in range(count):
        line = line + jnp.where(lane // height == n, numbers[first + n] * height, 0)
    return line


def hot(ids, line):
    return jnp.where(ids == line, 1.0, 0.0).astype(BF)


def place_body(own, core_at, numbers, mine, other, both):
    patches, width = mine.shape[0], mine.shape[1] // own
    rows = own * patches
    for side, value in ((numbers[core_at], mine), (1 - numbers[core_at], other)):
        for j in range(own):
            start = pl.multiple_of(side * rows + j * patches, patches)
            both[pl.ds(start, patches), :] = value[:, j * width : (j + 1) * width]


def hots_body(own, tp_count, share_count, height, core_at, numbers, ids_own, ids_other, prev, here):
    patches = ids_own.shape[1]
    plain = lax.broadcasted_iota(jnp.int32, (1, prev.shape[1]), 1)
    line = vocab_line(numbers, tp_count, share_count, height)
    core = numbers[core_at]
    for side, which in ((core, ids_own), (1 - core, ids_other)):
        ids = which[...].T
        for j in range(own):
            start = pl.multiple_of(side * own * patches + j * patches, patches)
            at = pl.ds(start, patches)
            before = id_of(ids, numbers[0] * own + j - 1)
            prev[at, :] = hot(before, plain)
            here[at, :] = hot(before, line)


def turn_matrix(tp_count, chunk, numbers):
    unit = chunk // tp_count
    row = lax.broadcasted_iota(jnp.int32, (chunk, chunk), 0)
    column = lax.broadcasted_iota(jnp.int32, (chunk, chunk), 1)
    source = column % unit
    for i, m in enumerate(sent_order(tp_count)):
        source = source + jnp.where(column // unit == i, numbers[m] * unit, 0)
    return (row == source).astype(BF)


def pick_up_body(tp_count, share_count, numbers, up, up_here, ups, ready):
    chunk = ups.shape[2]
    half = chunk // 2
    copies = []
    for n in range(share_count):
        at = pl.ds(pl.multiple_of(numbers[tp_count + n] * chunk, chunk), chunk)
        copies.append(pltpu.make_async_copy(up.at[:, at], ups.at[n], ready.at[n]))
        copies[-1].start()
    turn = turn_matrix(tp_count, chunk, numbers)
    for n in range(share_count):
        copies[n].wait()
        value = times(ups[n], turn).astype(BF)
        for z in range(2):
            first = (z * share_count + n) * half
            up_here[:, first : first + half] = value[:, z * half : (z + 1) * half]


def pick_down_body(tp_count, share_count, numbers, down, down_here, downs, ready):
    chunk = downs.shape[1]
    unit = chunk // tp_count
    half = chunk // 2
    copies = []
    for n in range(share_count):
        at = pl.ds(pl.multiple_of(numbers[tp_count + n] * chunk, chunk), chunk)
        copies.append(pltpu.make_async_copy(down.at[at, :], downs.at[n], ready.at[n]))
        copies[-1].start()
    for n in range(share_count):
        copies[n].wait()
        for i, m in enumerate(sent_order(tp_count)):
            z, place = i // (tp_count // 2), i % (tp_count // 2)
            first = (z * share_count + n) * half + place * unit
            start = pl.multiple_of(numbers[m] * unit, unit)
            down_here[first : first + unit, :] = downs[n, pl.ds(start, unit), :]


def split_body(tp_count, share, numbers, value, kept, sent):
    unit = share // tp_count
    half = kept.shape[0]
    inner_shares = value.shape[0] // share // 2
    inner_places = tp_count // 2
    for n in range(2 * inner_shares):
        for i, m in enumerate(sent_order(tp_count)):
            at = pl.ds(n * share + pl.multiple_of(numbers[m] * unit, unit), unit)
            place = 2 * (n // inner_shares) + i // inner_places
            place = place * inner_shares + n % inner_shares
            place = (place * inner_places + i % inner_places) * unit
            target = kept if place < half else sent
            row = place % half
            target[row : row + unit, :] = value[at, :].astype(target.dtype)


def tables_in_body(
    share_count, first_share, height, numbers, glob, glob_more, local, gains, kept, sent
):
    width = glob.shape[1]
    strip = width // (2 * share_count)
    lines = width // 128
    lane = lax.broadcasted_iota(jnp.int32, (1, width), 1)
    both = glob[...].astype(F32) + glob_more[...].astype(F32)
    size = 2 * height
    kept[:, width:] = jnp.zeros((kept.shape[0], 128), BF)
    sent[:, width:] = jnp.zeros((sent.shape[0], 128), BF)
    for n in range(share_count):
        target = kept if n < share_count // 2 else sent
        first = (n % (share_count // 2)) * size
        at = slice(n * height, (n + 1) * height)
        target[first : first + height, :width] = both[at, :].astype(BF)
        target[first + height : first + size, :width] = local[at, :].astype(BF)
        mine = jnp.where(lane // strip == numbers[first_share + n], gains[...], 0.0)
        rows = [mine[:, i * 128 : (i + 1) * 128] for i in range(lines)]
        rows.append(jnp.zeros((16 - lines, 128), F32))
        target[first : first + 16, width:] = jnp.concatenate(rows, axis=0).astype(BF)


def add_body(numbers, kept, arrived, keep, send):
    half = keep.shape[0]
    keep[...] = (kept[:half, :].astype(F32) + arrived[:half, :].astype(F32)).astype(keep.dtype)
    send[...] = (kept[half:, :].astype(F32) + arrived[half:, :].astype(F32)).astype(send.dtype)


def sum_body(numbers, kept, arrived, summed):
    summed[...] = (kept[...].astype(F32) + arrived[...].astype(F32)).astype(summed.dtype)


def stack_body(count, numbers, *refs):
    firsts, seconds, parts = refs[:count], refs[count : 2 * count], refs[2 * count :]
    column = 0
    for i, part in enumerate(parts):
        first, second = firsts[min(i, count - 1)], seconds[min(i, count - 1)]
        at = slice(column, column + part.shape[1])
        rows = first.shape[0]
        part[:rows, :] = first[:, at]
        part[rows:, :] = second[:, at]
        if count == 1:
            column += part.shape[1]


def tables_body(share_count, first_share, height, count, numbers, *refs):
    sides = (refs[:count], refs[count : 2 * count])
    glob, local, gain = refs[2 * count :]
    width = glob.shape[1]
    gains = None
    for side, parts in enumerate(sides):
        for n in range(share_count):
            start = numbers[first_share + side * share_count + n] * height
            at = pl.ds(pl.multiple_of(start, height), height)
            row = 2 * n * height
            column = 0
            for part in parts:
                inside = min(part.shape[1], width - column)
                to = slice(column, column + inside)
                glob[at, to] = part[row : row + height, :inside].astype(F32)
                local[at, to] = part[row + height : row + 2 * height, :inside].astype(F32)
                column += inside
            term = parts[-1][row : row + 16, parts[-1].shape[1] - 128 :].astype(F32)
            gains = term if gains is None else gains + term
    gain[...] = gains[: gain.shape[0]]


def last_body(numbers, *refs):
    keep, send = refs[-2:]
    row = 0
    for i in range(len(refs) // 2 - 1):
        kept, arrived = refs[2 * i], refs[2 * i + 1]
        half = kept.shape[0] // 2
        at = slice(row, row + half)
        for target, part in ((keep, slice(0, half)), (send, slice(half, 2 * half))):
            value = kept[part, :].astype(F32) + arrived[part, :].astype(F32)
            target[at, :] = value.astype(target.dtype)
        row += half


def finals_body(numbers, kept, arrived, *wholes):
    row = 0
    for whole in wholes:
        at = slice(row, row + whole.shape[0])
        whole[...] = kept[at, :].astype(F32) + arrived[at, :].astype(F32)
        row += whole.shape[0]


def on_device(
    byte_ids,
    global_out,
    global_in_grad,
    out_grad,
    proj_weight,
    emb_local,
    norm_gain,
    up_weight,
    down_weight,
):
    seq_count = lax.axis_size("seq")
    tp_count = lax.axis_size("tp")
    seq_place = lax.axis_index("seq")
    tp_place = lax.axis_index("tp")
    core = seq_place & 1
    chip = seq_place >> 1
    stages = seq_count.bit_length() - 2
    levels = tp_count.bit_length() - 1
    share_count = 1 << stages
    walks = (list(range(1, stages + 1)), list(range(stages, 0, -1)))
    patches, patch = byte_ids.shape
    slot, width = proj_weight.shape
    hidden = up_weight.shape[1]
    vocab = emb_local.shape[0]
    own = patch // tp_count
    part = patches // tp_count
    rows = own * patches
    height = vocab // seq_count
    chunk = hidden // seq_count

    def share_mask(number, walk):
        mask = 0
        for k in range(stages):
            if (number >> (stages - 1 - k)) & 1:
                mask |= 1 << (walk[k] - 1)
        return mask

    def shares_of(which):
        return [
            2 * (chip ^ jnp.where(which == 0, share_mask(n, walks[0]), share_mask(n, walks[1])))
            + which
            for n in range(share_count)
        ]

    shares = shares_of(core)
    others = shares_of(1 - core)
    near = [tp_place ^ m for m in range(tp_count)]
    numbers = jnp.stack(near + shares + others + [core]).astype(jnp.int32)
    core_at = tp_count + 2 * share_count
    call = functools.partial(run, numbers=numbers)

    def core_swap(value):
        return swap(value, "seq", (1,))

    def go(value, step):
        kind, k = step
        if kind == "seq":
            return swap(value, "seq", (1 << walks[0][k], 1 << walks[1][k]))
        return swap(value, "tp", (1 << k,))

    ids_own = byte_ids.T
    ids_other = core_swap(ids_own)
    out_other = core_swap(global_out)
    blocks = call(
        functools.partial(sort_body, patch, part, own),
        [like(own * part, width, BF)] * tp_count,
        [out_grad],
        [],
        flops=STEP,
    )
    far = pl.BlockSpec(memory_space=pltpu.HBM)
    prev_hot, prev_here = call(
        functools.partial(hots_body, own, tp_count, share_count, height, core_at),
        [like(2 * rows, vocab, BF), like(2 * rows, vocab // 2, BF)],
        [ids_own, ids_other],
        [blocks[0]],
    )

    near_rows, _ = lax.optimization_barrier((blocks[1], prev_hot))
    blocks = [blocks[0], swap(near_rows, "tp", (1,))] + [
        swap(blocks[m], "tp", (m,)) for m in range(2, tp_count)
    ]

    def by_slot(value):
        return [value[:, j * slot : (j + 1) * slot] for j in range(own)]

    (slot_in,) = call(
        functools.partial(place_body, own, core_at),
        [like(2 * rows, slot, BF)],
        [global_out, out_other],
        [prev_hot],
    )
    before = jnp.dot(prev_hot, emb_local, preferred_element_type=BF)
    u_rows = times(slot_in, proj_weight) + before.astype(F32)
    scale = lax.rsqrt(jnp.mean(u_rows * u_rows, axis=1, keepdims=True) + 1e-05)
    normed = u_rows * scale
    r_rows = (normed * norm_gain).astype(BF)
    (up_here,) = call(
        functools.partial(pick_up_body, tp_count, share_count),
        [like(width, hidden // 2, BF)],
        [up_weight],
        [r_rows],
        in_specs=[far],
        scratch=[VMEM((share_count, width, chunk), BF), pltpu.SemaphoreType.DMA((share_count,))],
    )
    a_rows = times(r_rows, up_here)
    sig = jax.nn.sigmoid(a_rows)
    h_rows = (a_rows * sig).astype(BF)
    slope = (sig * (1.0 + a_rows * (1.0 - sig))).astype(BF)
    h_rows, slope = lax.optimization_barrier((h_rows, slope))
    (down_here,) = call(
        functools.partial(pick_down_body, tp_count, share_count),
        [like(hidden // 2, width, BF)],
        [down_weight],
        [h_rows],
        in_specs=[far],
        scratch=[VMEM((share_count, chunk, width), BF), pltpu.SemaphoreType.DMA((share_count,))],
    )
    strip = chunk // 2
    h_rows = jnp.concatenate(
        [
            h_rows[:, (z * share_count + n) * strip : (z * share_count + n + 1) * strip]
            for n in range(share_count)
            for z in range(2)
        ],
        axis=1,
    )

    grad_own, own_hot = call(
        functools.partial(join_body, part, own, tp_count, share_count, height),
        [like(rows, width, BF), like(rows, vocab, BF)],
        [ids_own, *blocks],
        [h_rows],
        numbers=numbers,
    )
    grad_other = core_swap(grad_own)
    glob = [
        inner(own_hot[j * patches : (j + 1) * patches], value)
        for j, value in enumerate(by_slot(global_in_grad))
    ]
    glob = sum(glob[1:], glob[0])
    glob_sent = glob[vocab // 2 :].astype(BF)
    glob_kept = glob[: vocab // 2].astype(BF)
    glob_more = core_swap(glob_sent)

    (out_rows,) = call(
        functools.partial(place_body, 1, core_at),
        [like(2 * rows, width, BF)],
        [grad_own, grad_other],
        [glob_kept],
    )

    seq_steps = [("seq", k) for k in range(stages)]
    tp_steps = [("tp", k) for k in range(levels)]

    step = functools.partial(call, flops=STEP)

    class Chain:
        def __init__(self, kept, sent, steps):
            self.kept, self.steps, self.at = kept, steps, 0
            self.arrived = go(sent, self.steps[0])
            self.left = self.first = len(self.steps) - 2

        def next(self, after):
            self.at += 1
            self.left -= 1
            rows, columns = self.kept.shape
            ins = [self.kept, self.arrived]
            outs = [like(rows // 2, columns, self.kept.dtype)] * 2
            self.kept, sent = step(add_body, outs, ins, after)
            self.arrived = go(sent, self.steps[self.at])
            return self.kept

    class Table:
        def __init__(self, kept, sent):
            self.kept, self.at = kept, 0
            self.plan = (
                [("half", s) for s in seq_steps]
                + [("sum", s) for s in tp_steps]
                + [("join", s) for s in reversed(seq_steps)]
                + [("join", None)]
            )
            self.left = len(self.plan) - 1
            self.arrived = go(sent, self.plan[0][1])

        def next(self, after):
            last, (kind, hop) = self.plan[self.at][0], self.plan[self.at + 1]
            rows, columns = self.kept.shape
            ins = [self.kept, self.arrived]
            if last == "half" and kind == "half":
                self.kept, sent = step(add_body, [like(rows // 2, columns, BF)] * 2, ins, after)
            elif last == "join":
                many = self.plan[self.at + 1 :]
                cut = columns if len(many) > 2 or len(self.parts) > 1 else columns // PARTS
                outs = [like(2 * rows, cut, BF)] * (PARTS if len(many) <= 2 else 1)
                body = functools.partial(stack_body, len(self.parts))
                build = step if len(many) > 2 else call
                self.parts = build(body, outs, [*self.parts, *self.arrived], after)
                self.kept = self.parts[0]
            else:
                (self.kept,) = step(sum_body, [like(rows, columns, BF)], ins, after)
                sent = self.kept
            self.at += 1
            self.left -= 1
            if kind == "join":
                if last != "join":
                    self.parts = [sent]
                self.arrived = [
                    core_swap(part) if hop is None else go(part, hop) for part in self.parts
                ]
            else:
                self.arrived = go(sent, hop)
            return self.kept

    dh_rows = outer(out_rows, down_here)
    da_rows = (dh_rows * slope.astype(F32)).astype(BF)
    dr_part = outer(da_rows, up_here)
    dr_sent = dr_part.astype(BF)
    kind = BF if chunk // tp_count % 16 == 0 else F32
    half = h_rows.shape[1] // 2
    down_kept = inner(h_rows[:, :half], out_rows).astype(kind)
    down_sent = inner(h_rows[:, half:], out_rows).astype(kind)
    da_rows, _ = lax.optimization_barrier((da_rows, down_sent))
    up_kept = inner(da_rows[:, :half], r_rows).astype(kind)
    up_sent = inner(da_rows[:, half:], r_rows).astype(kind)
    down = Chain(down_kept, down_sent, seq_steps + tp_steps)
    up = Chain(up_kept, up_sent, tp_steps[:1] + seq_steps + tp_steps[1:])
    dr_more = core_swap(dr_sent)
    dr_rows = dr_part + dr_more.astype(F32)

    gain_part = jnp.sum(dr_rows * normed, axis=0, keepdims=True)
    dn_rows = dr_rows * norm_gain
    du_rows = (
        out_rows.astype(F32)
        + scale * (dn_rows - normed * jnp.mean(dn_rows * normed, axis=1, keepdims=True))
    ).astype(BF)
    size = 2 * height
    kept, sent = call(
        functools.partial(tables_in_body, share_count, tp_count, height),
        [like(share_count // 2 * size, width + 128, BF)] * 2,
        [glob_kept, glob_more, inner(prev_here, du_rows), gain_part],
        [up.kept],
    )
    table = Table(kept, sent)
    share = width // seq_count
    kind = BF if share // tp_count % 16 == 0 else F32
    du_later, _ = lax.optimization_barrier((du_rows, table.kept))
    du_here = jnp.concatenate(
        [lax.dynamic_slice_in_dim(du_later, s * share, share, 1) for s in shares], axis=1
    )
    value = inner(du_here, slot_in)
    kept, sent = call(
        functools.partial(split_body, tp_count, share),
        [like(value.shape[0] // 2, slot, kind)] * 2,
        [value],
        [table.kept],
    )
    proj = Chain(kept, sent, seq_steps[:1] + tp_steps[:1] + seq_steps[1:] + tp_steps[1:])
    last = [up.kept, proj.kept, table.kept, down.kept]
    names = {"T": table, "D": down, "U": up, "P": proj}
    ends = [down, up, proj]
    heights = [c.kept.shape[0] >> c.left + 1 for c in ends]
    merged = None

    def last_sums(after):
        kind = down.kept.dtype if down.kept.dtype == proj.kept.dtype else F32
        keep, sent = step(
            last_body,
            [like(sum(heights), width, kind)] * 2,
            [x for c in ends for x in (c.kept, c.arrived)],
            after,
        )
        return keep, go(sent, tp_steps[-1])

    def spread(after):
        du_own, _ = lax.optimization_barrier((du_rows, after))
        du_own = lax.dynamic_slice_in_dim(du_own, core * rows, rows, 0)
        back = outer(du_own, proj_weight).astype(BF)
        return jnp.concatenate(
            [back[j * patches : (j + 1) * patches] for j in range(own)], axis=1
        )

    glob_out_grad = None
    for name in ORDER:
        chain = names.get(name)
        if chain is not None and chain.left:
            last = [chain.next(last)]
            if chain is up and glob_out_grad is None and up.left <= max(0, up.first - 2):
                glob_out_grad = spread(up.kept)
                last.append(glob_out_grad)
        elif name == "F":
            while any(c.left for c in ends):
                for c in ends:
                    if c.left:
                        last = [c.next(last)]
            merged = last_sums(last)
            last = [merged[0]]
    while table.left:
        last = [table.next(last)]

    lines = width // 128
    emb_global_grad, emb_local_grad, gain_grad = call(
        functools.partial(tables_body, share_count, tp_count, height, PARTS),
        [like(vocab, width, F32), like(vocab, width, F32), like(lines, 128, F32)],
        [*table.parts, *table.arrived],
        last,
    )
    down_grad, up_grad, proj_grad = call(
        finals_body,
        [like(h, width, F32) for h in heights],
        [*merged],
        [gain_grad],
    )
    return (
        glob_out_grad,
        emb_global_grad,
        emb_local_grad,
        gain_grad.reshape(width),
        proj_grad.T,
        up_grad.T,
        down_grad,
    )


def solution(mesh):
    placed = (
        P("seq", None),
        P("seq", "tp"),
        P("seq", "tp"),
        P(("seq", "tp"), None),
        P(),
        P(),
        P(),
        P(),
        P(),
    )
    return jax.shard_map(
        on_device,
        mesh=mesh,
        in_specs=placed,
        out_specs=(
            P("seq", "tp"),
            P(),
            P(),
            P(),
            P(None, ("seq", "tp")),
            P(None, ("seq", "tp")),
            P(("seq", "tp"), None),
        ),
        check_vma=False,
    )
```
